128 devices in a mesh: rep: 8 (over y, core), sp: 16 (over x, z).
Axes of the slice: x: 4, y: 4, z: 4, core: 2. Of those that a mesh axis runs over, the one named last changes fastest.
Arguments:
- frames: bfloat16 [8, 64, 256, 1024], P('rep', 'sp'), may hold values from -6 to 6
- out_grad: bfloat16 [8, 64, 256, 1024], P('rep', 'sp'), may hold values from -0.046875 to 0.046875
- error_prev: float32 [8, 9216, 1024], P('rep', 'sp'), may hold values from -6 to 6
- q_prev: float32 [32, 9216], P(None, 'sp'), may hold values from -6 to 6
Outputs:
- error_next: float32 [8, 9216, 1024], P('rep', 'sp')
- q_next: float32 [32, 9216], P(None, 'sp')
The draws below stay inside these ranges and needn't reach their ends.
All inputs are finite; a program needn't handle non-finite values.
Results may differ from the reference program's by a relative error of at most 0.0003.
Values may be sent and summed in bfloat16 or wider, within the bound.
A program may use at most 192 MiB of HBM per device.

```python
import jax
import jax.numpy as jnp
from jax import lax

C = 1024
RANK = 32
WIDTH = 256
ROWS_DEV = 4
KDIM = 9216
HEIGHT = 64
REPS = 8


def steps_of(key, dims, pieces, smallest, top_value):
    loudness = 1.0
    for axis_at, parts in pieces:
        steps = jax.random.uniform(jax.random.fold_in(jax.random.fold_in(key, 6), axis_at), (parts,), jnp.float32, smallest / len(pieces), top_value / len(pieces))
        loudness = loudness * jnp.repeat(jnp.exp(steps), dims[axis_at] // parts).reshape((-1,) + (1,) * (len(dims) - 1 - axis_at))
    return loudness


def noise(key, dims, deviation, bound, split=(), kind=jnp.bfloat16):
    gain = steps_of(key, dims, split, -0.22, 0.18) if split else 1.0
    entries = jax.random.normal(key, dims, jnp.float32) * deviation * gain
    return jnp.minimum(jnp.maximum(entries, -bound), bound).astype(kind)


def setup_inputs(seed: int = 0) -> dict:
    key_of = jax.random.split(jax.random.key(seed), 5)
    return {
        "frames": noise(key_of[0], (REPS, HEIGHT, WIDTH, C), 1.0, 6.0, ((0, 8), (1, 16))),
        "out_grad": noise(key_of[1], (REPS, HEIGHT, WIDTH, C), (1 / (HEIGHT * WIDTH) ** 0.5), 0.046875, ((0, 8), (1, 16))),
        "error_prev": noise(key_of[2], (REPS, KDIM, C), 1.0, 6.0, ((0, 8), (1, 16)), jnp.float32),
        "q_prev": noise(key_of[3], (RANK, KDIM), 1.0, 6.0, ((1, 16),), jnp.float32),
    }


def make_patches(padded, top, count, width):
    taps = []
    for row_off in range(3):
        block = lax.dynamic_slice_in_dim(padded, top + row_off, count, 0)
        for col_off in range(3):
            taps.append(block[:, col_off:col_off + width, :])
    stacked = jnp.stack(taps, axis=-1)
    return stacked.reshape(count * width, stacked.shape[2] * 9)

def replica_grad(pair):
    frame, grad_out = pair
    padded = jnp.pad(frame, ((1, 1), (1, 1), (0, 0)))

    def add_band(total, band):
        top = (band * ROWS_DEV).astype(jnp.int32)
        cols = make_patches(padded, top, ROWS_DEV, WIDTH)
        rows_grad = lax.dynamic_slice_in_dim(grad_out, top, ROWS_DEV, 0).reshape(ROWS_DEV * WIDTH, C)
        term = lax.dot_general(cols.astype(jnp.float32), rows_grad.astype(jnp.float32), (((0,), (0,)), ((), ())), preferred_element_type=jnp.float32)
        return (total + term, None)
    start = jnp.zeros((KDIM, C), jnp.float32)
    total, unused = lax.scan(add_band, start, jnp.arange(HEIGHT // ROWS_DEV, dtype=jnp.int32))
    return total

def reference(frames, out_grad, error_prev, q_prev):
    high = lax.Precision.HIGHEST
    grads = lax.map(replica_grad, (frames, out_grad))
    memory = grads + error_prev
    p_total = jnp.einsum('ak,rkc->ac', q_prev, memory, precision=high)
    gram = jnp.dot(p_total, p_total.T, precision=high)
    lower = jnp.linalg.cholesky(gram)
    p_ortho = jax.scipy.linalg.solve_triangular(lower, p_total, lower=True)
    q_next = jnp.einsum('ac,rkc->ak', p_ortho, memory, precision=high) / REPS
    approx = jnp.einsum('ak,ac->kc', q_next, p_ortho, precision=high)
    error_next = memory - approx[None]
    return (error_next, q_next)
```

```python
import functools

import jax
import jax.numpy as jnp
from jax import lax
from jax.experimental import pallas as pl
from jax.experimental.pallas import tpu as pltpu
from jax.sharding import PartitionSpec as P

MESH = pl.DeviceIdType.MESH
RING = 4
CHUNKS = 8
COLS = 128
TAPS = 9
P_AT = 1


def sp_at(x, z):
    return {"sp": lax.rem(x + RING, RING) * RING + lax.rem(z + RING, RING)}


def remote(src, dst, send, recv, device):
    return pltpu.make_async_remote_copy(
        src_ref=src, dst_ref=dst, send_sem=send, recv_sem=recv, device_id=device, device_id_type=MESH
    )


def split(value):
    high = value.astype(jnp.bfloat16)
    rest = value - high.astype(jnp.float32)
    middle = rest.astype(jnp.bfloat16)
    low = (rest - middle.astype(jnp.float32)).astype(jnp.bfloat16)
    return high, middle, low


def exact_dot(a, b, contract):
    return lax.dot_general(
        a, b, (contract, ((), ())), precision=lax.Precision.HIGHEST, preferred_element_type=jnp.float32
    )


def step_kernel(
    count_rep, frames, g, err, q_own, q_taps, error_next, q_next,
    local, flipped, raw, halo, taps, gbuf, part, relay, piece, total,
    q_near, q_flip, t_term, t_near, p_src, p_near, p_one, p_far, p_all, p_ortho, work, q_src, q_got, q_sum, q_flat,
    l_in, f_send, f_recv, f_own, h_send, h_recv, e_in, g_own,
    d_send, d_recv, r_send, r_recv, a_send, a_recv, b_send, b_recv, out_sem,
    q_send, q_recv, q_copy, t_send, t_recv, s1, r1, s2, r2, s3, r3, s4, r4, s5, r5,
):
    sp, rep = lax.axis_index("sp"), lax.axis_index("rep")
    x, z = sp // RING, lax.rem(sp, RING)
    up, down = sp_at(x, z + 1), sp_at(x, z - 1)
    right, left = sp_at(x + 1, z), sp_at(x - 1, z)
    z_up, z_down = lax.rem(z + 1, RING), lax.rem(z + 3, RING)
    x_right, x_left, x_far = lax.rem(x + 1, RING), lax.rem(x + 3, RING), lax.rem(x + 2, RING)
    band = g.shape[0]
    half = band // 2
    count_sp = RING * RING
    share = part.shape[4] * 2
    width = halo.shape[3]
    rank = q_own.shape[0]

    def at_sp(d):
        return {"sp": lax.rem(sp + d, count_sp)}

    def at_rep(d):
        return {"rep": lax.rem(rep + d, count_rep)}

    def frames_out(step):
        return remote(
            flipped.at[:, lax.rem(z + step, RING)], raw.at[z], f_send.at[step - 1], f_recv.at[step - 1],
            sp_at(x, z + step),
        )

    def frames_in(step):
        return remote(
            flipped.at[:, z], raw.at[lax.rem(z + RING - step, RING)], f_send.at[step - 1], f_recv.at[step - 1], up
        )

    def columns(j):
        return pl.ds(pl.multiple_of(j * COLS, COLS), COLS)

    def slot(which, first, count):
        return pl.ds(pl.multiple_of(which * band + first, half), count)

    def own_grad(j):
        return pltpu.make_async_copy(g.at[:, columns(j)], gbuf.at[j, slot(z, 0, band)], g_own.at[j])

    def direct(j, side):
        return remote(
            g.at[:, columns(j)], gbuf.at[j, slot(z, 0, band)], d_send.at[j, side], d_recv.at[j, side],
            up if side == 0 else down,
        )

    def direct_in(j, side):
        return remote(
            g.at[:, columns(j)], gbuf.at[j, slot(z_down if side == 0 else z_up, 0, band)],
            d_send.at[j, side], d_recv.at[j, side], up,
        )

    def forward(j, side):
        ref = gbuf.at[j, slot(z_down if side == 0 else z_up, side * half, half)]
        return remote(ref, ref, r_send.at[j, side], r_recv.at[j, side], up if side == 0 else down)

    def forward_in(j, side):
        ref = gbuf.at[j, slot(lax.rem(z + 2, RING), side * half, half)]
        return remote(ref, ref, r_send.at[j, side], r_recv.at[j, side], up)

    def err_in(j):
        return pltpu.make_async_copy(err.at[:, columns(j)], total.at[j], e_in.at[j])

    def error_out(j):
        return pltpu.make_async_copy(total.at[j], error_next.at[:, columns(j)], out_sem.at[j])

    def far(j, side):
        return remote(
            part.at[j, x_far, side], relay.at[j, side], a_send.at[j, side], a_recv.at[j, side],
            right if side == 0 else left,
        )

    def near(j, side):
        return remote(
            part.at[j, x_right if side == 0 else x_left], piece.at[j, side], b_send.at[j, side], b_recv.at[j, side],
            right if side == 0 else left,
        )

    def q_out(step):
        return remote(q_taps, q_near.at[:, x], q_send.at[step - 1], q_recv.at[step - 1], sp_at(x + step, z))

    def q_in(step):
        source = lax.rem(x + RING - step, RING)
        return remote(q_taps, q_near.at[:, source], q_send.at[step - 1], q_recv.at[step - 1], right)

    def t_out(step):
        return remote(
            t_term.at[lax.rem(z + step, RING)], t_near.at[step - 1], t_send.at[step - 1], t_recv.at[step - 1],
            sp_at(x, z + step),
        )

    def p_scatter(d):
        return remote(p_src.at[lax.rem(sp + d, count_sp)], p_near.at[d - 1], s1.at[d - 1], r1.at[d - 1], at_sp(d))

    def p_share(d):
        return remote(p_one, p_far.at[rep], s2.at[d - 1], r2.at[d - 1], at_rep(d))

    def p_share_in(d):
        source = lax.rem(rep + count_rep - d, count_rep)
        return remote(p_one, p_far.at[source], s2.at[d - 1], r2.at[d - 1], at_rep(d))

    def p_gather(d):
        return remote(p_all.at[sp], p_all.at[sp], s3.at[d - 1], r3.at[d - 1], at_sp(d))

    def p_gather_in(d):
        ref = p_all.at[lax.rem(sp + count_sp - d, count_sp)]
        return remote(ref, ref, s3.at[d - 1], r3.at[d - 1], at_sp(d))

    def q_scatter(d):
        return remote(q_src.at[lax.rem(rep + d, count_rep)], q_got.at[d - 1], s4.at[d - 1], r4.at[d - 1], at_rep(d))

    def q_gather(d):
        return remote(q_next.at[rep], q_next.at[rep], s5.at[d - 1], r5.at[d - 1], at_rep(d))

    def q_gather_in(d):
        ref = q_next.at[lax.rem(rep + count_rep - d, count_rep)]
        return remote(ref, ref, s5.at[d - 1], r5.at[d - 1], at_rep(d))

    barrier = pltpu.get_barrier_semaphore()
    for d in range(1, count_sp):
        pl.semaphore_signal(barrier, inc=1, device_id=at_sp(d), device_id_type=MESH)
    for d in range(1, count_rep):
        pl.semaphore_signal(barrier, inc=1, device_id=at_rep(d), device_id_type=MESH)

    own_q = pltpu.make_async_copy(q_taps, q_near.at[:, x], q_copy)
    own_q.start()

    def column_in(i):
        return pltpu.make_async_copy(frames.at[:, columns(i)], local.at[i], l_in.at[i])

    pairs = frames.shape[1] // COLS
    owners = COLS // share
    for i in range(pairs):
        column_in(i).start()
    for i in range(pairs):
        column_in(i).wait()
        turned = local[i].T
        for k in range(owners):
            owner = i * owners + k
            flipped[owner // RING, owner % RING] = turned[k * share : (k + 1) * share]

    pl.semaphore_wait(barrier, count_sp + count_rep - 2)

    for step in (1, 3, 2):
        frames_out(step).start()
        q_out(step).start()
    own_frames = pltpu.make_async_copy(flipped.at[:, z], raw.at[z], f_own)
    own_frames.start()
    for j in range(CHUNKS):
        err_in(j).start()
    for j in range(2):
        direct(j, 0).start()
        direct(j, 1).start()
    for j in range(CHUNKS):
        own_grad(j).start()

    for j in range(CHUNKS):
        err_in(j).wait()
        term = exact_dot(q_own[...], total[j], ((1,), (0,)))
        for h in range(2):
            p_src[2 * j + h] = term[h * (rank // 2) : (h + 1) * (rank // 2)]

    own_q.wait()
    for step in (1, 3, 2):
        q_in(step).wait_recv()
    for tap in range(TAPS):
        q_flip[tap] = q_near[tap].reshape(RING * share, q_near.shape[3]).T

    own_frames.wait()
    for step in (1, 3, 2):
        frames_in(step).wait_recv()

    bottom = raw.at[RING - 1, :, :, band - width : band]
    above = remote(bottom, halo.at[0], h_send.at[0], h_recv.at[0], right)
    below = remote(raw.at[0, :, :, 0:width], halo.at[1], h_send.at[1], h_recv.at[1], left)
    above.start()
    below.start()
    lane = lax.broadcasted_iota(jnp.int32, (RING * share, width), 1)

    def place(row, value):
        at = pl.ds(pl.multiple_of(row * width, width), width)
        wide = value.astype(jnp.float32)
        taps[0, :, at] = jnp.where(lane == 0, 0.0, pltpu.roll(wide, 1, 1)).astype(taps.dtype)
        taps[1, :, at] = value
        taps[2, :, at] = jnp.where(lane == width - 1, 0.0, pltpu.roll(wide, width - 1, 1)).astype(taps.dtype)

    def place_band(which, carry):
        for row in range(band // width):
            value = raw[which, :, :, row * width : (row + 1) * width].reshape(RING * share, width)
            place(which * (band // width) + row + 1, value)
        return carry

    lax.fori_loop(0, RING, place_band, 0)
    rows = RING * band // width
    above.wait()
    below.wait()
    zero = jnp.zeros((RING * share, width), halo.dtype)
    place(0, jnp.where(x == 0, zero, halo[0].reshape(RING * share, width)))
    place(rows + 1, jnp.where(x == RING - 1, zero, halo[1].reshape(RING * share, width)))

    def start_forward(j):
        for side in range(2):
            direct_in(j, side).wait_recv()
            forward(j, side).start()

    start_forward(0)
    for j in range(CHUNKS):
        own_grad(j).wait()

    def t_band(which, carry):
        acc = None
        for a in range(3):
            for b in range(3):
                at = pl.ds(pl.multiple_of(which * band + a * width, width), band)
                term = jnp.dot(q_flip[a * 3 + b], taps[b, :, at], preferred_element_type=jnp.float32)
                acc = term if acc is None else acc + term
        t_term[which] = acc[:rank] + (acc[rank : 2 * rank] + acc[2 * rank : 3 * rank])
        return carry

    lax.fori_loop(0, RING, t_band, 0)
    for step in (1, 3, 2):
        t_out(step).start()

    def p_terms():
        for step in (1, 3, 2):
            t_out(step).wait_recv()
        full = t_term[z] + (t_near[0] + t_near[1] + t_near[2])
        parts = jnp.concatenate(split(full), axis=0)

        def add(j, carry):
            acc = jnp.dot(parts, gbuf[j, slot(z, 0, band)], preferred_element_type=jnp.float32)
            term = acc[:rank] + (acc[rank : 2 * rank] + acc[2 * rank :])
            for h in range(2):
                p_src[2 * j + h] = p_src[2 * j + h] + term[h * (rank // 2) : (h + 1) * (rank // 2)]
            return carry

        lax.fori_loop(0, CHUNKS, add, 0)
        for d in range(1, count_sp):
            p_scatter(d).start()

    def p_sum_sp():
        acc = p_src[sp]
        for d in range(1, count_sp):
            p_scatter(d).wait_recv()
            acc = acc + p_near[d - 1]
        p_one[...] = acc
        p_far[rep] = acc
        for d in range(1, count_rep):
            p_share(d).start()

    def p_sum_rep():
        for d in range(1, count_rep):
            p_share_in(d).wait_recv()
        acc = p_far[0]
        for i in range(1, count_rep):
            acc = acc + p_far[i]
        p_all[sp] = acc
        for d in range(1, count_sp):
            p_gather(d).start()

    def p_chunk(j):
        return jnp.concatenate([p_all[2 * j], p_all[2 * j + 1]], axis=0)

    def orthogonal():
        for d in range(1, count_sp):
            p_gather_in(d).wait_recv()
        gram = jnp.zeros((rank, rank), jnp.float32)
        for j in range(CHUNKS):
            block = p_chunk(j)
            gram = gram + exact_dot(block, block, ((1,), (1,)))
        row_at = lax.broadcasted_iota(jnp.int32, (rank, rank), 0)
        col_at = lax.broadcasted_iota(jnp.int32, (rank, rank), 1)
        work[:, :rank] = gram
        work[:, rank : 2 * rank] = jnp.where(row_at == col_at, 1.0, 0.0)
        shape = (rank, 2 * rank)
        line = lax.broadcasted_iota(jnp.int32, shape, 0)
        spot = lax.broadcasted_iota(jnp.int32, shape, 1)

        def eliminate(k, carry):
            state = work[:, : 2 * rank]
            column = jnp.sum(jnp.where(spot == k, state, 0.0), axis=1, keepdims=True)
            pivot = jnp.sum(jnp.where(line == k, state, 0.0), axis=0, keepdims=True)
            diagonal = jnp.sum(jnp.where((spot == k) & (line == k), state, 0.0), axis=(0, 1), keepdims=True)
            inverse = 1.0 / jnp.sqrt(diagonal)
            pivot = pivot * inverse
            work[:, : 2 * rank] = jnp.where(
                line > k, state - (column * inverse) * pivot, jnp.where(line == k, pivot, state)
            )
            return carry

        lax.fori_loop(0, rank, eliminate, 0)
        lower_inverse = jnp.where(col_at <= row_at, work[:, rank : 2 * rank], 0.0)
        for j in range(CHUNKS):
            p_ortho[j] = exact_dot(lower_inverse, p_chunk(j), ((1,), (0,)))
        q_sum[...] = jnp.zeros_like(q_sum)

    def add_q(k):
        q_sum[...] = q_sum[...] + exact_dot(p_ortho[k], total[k], ((1,), (1,)))

    def step(j, carry):
        @pl.when(j + 2 < CHUNKS)
        def _():
            direct(j + 2, 0).start()
            direct(j + 2, 1).start()

        @pl.when(j + 1 < CHUNKS)
        def _():
            start_forward(j + 1)

        @pl.when(j < CHUNKS)
        def _():
            forward_in(j, 0).wait_recv()
            forward_in(j, 1).wait_recv()
            depth = gbuf.shape[1]
            for a in range(3):
                for b in range(3):
                    product = jnp.dot(
                        taps[b, :, a * width : a * width + depth], gbuf[j], preferred_element_type=jnp.float32
                    )
                    count = part.shape[4]
                    for owner in range(RING):
                        for side in range(2):
                            first = (owner * 2 + side) * count
                            part[j, owner, side, a * 3 + b] = product[first : first + count]
            far(j, 0).start()
            far(j, 1).start()

        @pl.when((j >= 1) & (j <= CHUNKS))
        def _():
            k = j - 1
            far(k, 0).wait_recv()
            part[k, x_right, 0] = part[k, x_right, 0] + relay[k, 0]
            near(k, 0).start()
            far(k, 1).wait_recv()
            part[k, x_left, 1] = part[k, x_left, 1] + relay[k, 1]
            near(k, 1).start()

        pl.when(j == P_AT)(p_terms)
        pl.when(j == P_AT + 1)(p_sum_sp)
        pl.when(j == P_AT + 2)(p_sum_rep)
        pl.when(j == P_AT + 3)(orthogonal)

        @pl.when(j >= 2)
        def _():
            k = j - 2
            near(k, 0).wait_recv()
            near(k, 1).wait_recv()
            count = part.shape[4]
            for side in range(2):
                for tap in range(TAPS):
                    at = pl.ds(side * count * TAPS + tap, count, stride=TAPS)
                    total[k, at, :] = (
                        total[k, at, :] + part[k, x, side, tap] + (piece[k, 0, side, tap] + piece[k, 1, side, tap])
                    )

            @pl.when(j >= P_AT + 3)
            def _():
                add_q(k)

        @pl.when(j == P_AT + 3)
        def _():
            for k in range(P_AT + 1):
                add_q(k)

        return carry

    lax.fori_loop(0, CHUNKS + 2, step, 0)

    lines = rank // count_rep
    for i in range(count_rep):
        q_src[i] = q_sum[i * lines : (i + 1) * lines]
    for d in range(1, count_rep):
        q_scatter(d).start()
    acc = q_src[rep]
    for d in range(1, count_rep):
        q_scatter(d).wait_recv()
        acc = acc + q_got[d - 1]
    q_next[rep] = acc * (1.0 / count_rep)
    for d in range(1, count_rep):
        q_gather(d).start()
    for d in range(1, count_rep):
        q_gather_in(d).wait_recv()
    for i in range(count_rep):
        q_flat[i * lines : (i + 1) * lines] = q_next[i]

    q0, q1, q2 = split(q_flat[...])
    q_side = jnp.concatenate([q0, q0, q0, q1, q1, q2], axis=0).T

    def finish(j, carry):
        p0, p1, p2 = split(p_ortho[j])
        p_side = jnp.concatenate([p0, p1, p2, p0, p1, p0], axis=0)
        total[j] = total[j] - jnp.dot(q_side, p_side, preferred_element_type=jnp.float32)
        error_out(j).start()
        for side in range(2):
            direct(j, side).wait_send()
            forward(j, side).wait_send()
            far(j, side).wait_send()
            near(j, side).wait_send()
        return carry

    lax.fori_loop(0, CHUNKS, finish, 0)
    for step_ in (1, 3, 2):
        frames_out(step_).wait_send()
        q_out(step_).wait_send()
        t_out(step_).wait_send()
    for d in range(1, count_sp):
        p_scatter(d).wait_send()
        p_gather(d).wait_send()
    for d in range(1, count_rep):
        p_share(d).wait_send()
        q_scatter(d).wait_send()
        q_gather(d).wait_send()
    for j in range(CHUNKS):
        error_out(j).wait()


def compressed_step(count_rep, frames, g, err, q_own, q_taps):
    band, chans = g.shape
    width = band // 4
    rows = err.shape[0]
    rank = q_own.shape[0]
    count_sp = RING * RING
    share = chans // count_sp
    per_side = share // 2
    dma = pltpu.SemaphoreType.DMA
    two = dma((CHUNKS, 2))
    f32, bf16 = jnp.float32, jnp.bfloat16
    any_spec, vmem_spec = pl.BlockSpec(memory_space=pl.ANY), pl.BlockSpec(memory_space=pltpu.VMEM)
    p_block = (rank // 2, COLS)
    q_block = (rank // count_rep, rows)
    return pl.pallas_call(
        functools.partial(step_kernel, count_rep),
        out_shape=(
            jax.ShapeDtypeStruct((rows, chans), f32),
            jax.ShapeDtypeStruct((count_rep, *q_block), f32),
        ),
        in_specs=[any_spec, any_spec, any_spec, vmem_spec, vmem_spec],
        out_specs=(any_spec, vmem_spec),
        scratch_shapes=[
            pltpu.VMEM((chans // COLS, band, COLS), bf16),
            pltpu.VMEM((RING, RING, share, band), bf16),
            pltpu.VMEM((RING, RING, share, band), bf16),
            pltpu.VMEM((2, RING, share, width), bf16),
            pltpu.VMEM((3, RING * share, RING * band + 2 * width), bf16),
            pltpu.VMEM((CHUNKS, RING * band, COLS), bf16),
            pltpu.VMEM((CHUNKS, RING, 2, TAPS, per_side, COLS), f32),
            pltpu.VMEM((CHUNKS, 2, TAPS, per_side, COLS), f32),
            pltpu.VMEM((CHUNKS, 2, 2, TAPS, per_side, COLS), f32),
            pltpu.VMEM((CHUNKS, rows, COLS), f32),
            pltpu.VMEM((TAPS, RING, share, q_taps.shape[2]), bf16),
            pltpu.VMEM((TAPS, q_taps.shape[2], RING * share), bf16),
            pltpu.VMEM((RING, rank, band), f32),
            pltpu.VMEM((RING - 1, rank, band), f32),
            pltpu.VMEM((count_sp, *p_block), f32),
            pltpu.VMEM((count_sp - 1, *p_block), f32),
            pltpu.VMEM(p_block, f32),
            pltpu.VMEM((count_rep, *p_block), f32),
            pltpu.VMEM((count_sp, *p_block), f32),
            pltpu.VMEM((CHUNKS, rank, COLS), f32),
            pltpu.VMEM((rank, 128), f32),
            pltpu.VMEM((count_rep, *q_block), f32),
            pltpu.VMEM((count_rep - 1, *q_block), f32),
            pltpu.VMEM((rank, rows), f32),
            pltpu.VMEM((rank, rows), f32),
            dma((chans // COLS,)), dma((3,)), dma((3,)), dma, dma((2,)), dma((2,)), dma((CHUNKS,)), dma((CHUNKS,)),
            two, two, two, two, two, two, two, two, dma((CHUNKS,)),
            dma((3,)), dma((3,)), dma, dma((3,)), dma((3,)),
            dma((count_sp - 1,)), dma((count_sp - 1,)), dma((count_rep - 1,)), dma((count_rep - 1,)),
            dma((count_sp - 1,)), dma((count_sp - 1,)), dma((count_rep - 1,)), dma((count_rep - 1,)),
            dma((count_rep - 1,)), dma((count_rep - 1,)),
        ],
        compiler_params=pltpu.CompilerParams(
            collective_id=0, has_side_effects=True, vmem_limit_bytes=58 * 1024 * 1024
        ),
        cost_estimate=pl.CostEstimate(flops=2 * rows * 16 * chans * band, bytes_accessed=10**7, transcendentals=0),
        name="compressed_step",
    )(frames, g, err, q_own, q_taps)


def per_device(count_rep, frames, out_grad, error_prev, q_prev):
    band_rows, width, chans = frames.shape[1:]
    band = band_rows * width
    rank, rows = q_prev.shape
    by_tap = q_prev.reshape(rank, rows // TAPS, TAPS).transpose(2, 1, 0)
    high = lax.reduce_precision(by_tap, 8, 7)
    middle = lax.reduce_precision(by_tap - high, 8, 7)
    low = by_tap - high - middle
    parts = jnp.concatenate([high, middle, low, jnp.zeros_like(low)], axis=2)[:, :, :128]
    error_next, q_next = compressed_step(
        count_rep,
        frames[0].reshape(band, chans),
        out_grad[0].reshape(band, chans),
        error_prev[0],
        q_prev,
        parts.astype(jnp.bfloat16),
    )
    return (error_next[None], q_next.reshape(rank, rows))


def solution(mesh):
    placed = (
        P("rep", "sp", None, None),
        P("rep", "sp", None, None),
        P("rep", "sp", None),
        P(None, "sp"),
    )
    return jax.shard_map(
        functools.partial(per_device, mesh.shape["rep"]),
        mesh=mesh,
        in_specs=placed,
        out_specs=(P("rep", "sp", None), P(None, "sp")),
        check_vma=False,
    )
```

```python
import functools

import jax
import jax.numpy as jnp
from jax import lax
from jax.experimental import pallas as pl
from jax.experimental.pallas import tpu as pltpu
from jax.sharding import PartitionSpec as P

MESH = pl.DeviceIdType.MESH
RING = 4
CHUNKS = 8
COLS = 128
TAPS = 9
P_AT = 2


def sp_at(x, z):
    return {"sp": lax.rem(x + RING, RING) * RING + lax.rem(z + RING, RING)}


def remote(src, dst, send, recv, device):
    return pltpu.make_async_remote_copy(
        src_ref=src, dst_ref=dst, send_sem=send, recv_sem=recv, device_id=device, device_id_type=MESH
    )


def split(value):
    high = value.astype(jnp.bfloat16)
    rest = value - high.astype(jnp.float32)
    middle = rest.astype(jnp.bfloat16)
    low = (rest - middle.astype(jnp.float32)).astype(jnp.bfloat16)
    return high, middle, low


def exact_dot(a, b, contract):
    return lax.dot_general(
        a, b, (contract, ((), ())), precision=lax.Precision.HIGHEST, preferred_element_type=jnp.float32
    )


def step_kernel(
    count_rep, frames, g, err, q_own, memory, q_next, p_ortho,
    local, q_turned, q_taps, flipped, raw, halo, taps, gbuf, part, relay, piece, total,
    q_near, q_flip, t_term, t_near, p_src, p_near, p_one, p_far, p_all, work, q_src, q_got, q_sum,
    l_in, f_send, f_recv, f_own, h_send, h_recv, e_in, g_own,
    d_send, d_recv, r_send, r_recv, a_send, a_recv, b_send, b_recv, out_sem,
    q_send, q_recv, q_copy, t_send, t_recv, s1, r1, s2, r2, s3, r3, s4, r4, s5, r5,
):
    sp, rep = lax.axis_index("sp"), lax.axis_index("rep")
    x, z = sp // RING, lax.rem(sp, RING)
    up, down = sp_at(x, z + 1), sp_at(x, z - 1)
    right, left = sp_at(x + 1, z), sp_at(x - 1, z)
    z_up, z_down = lax.rem(z + 1, RING), lax.rem(z + 3, RING)
    x_right, x_left, x_far = lax.rem(x + 1, RING), lax.rem(x + 3, RING), lax.rem(x + 2, RING)
    band = g.shape[0]
    half = band // 2
    count_sp = RING * RING
    share = part.shape[4] * 2
    width = halo.shape[3]
    rank = q_own.shape[0]

    def at_sp(d):
        return {"sp": lax.rem(sp + d, count_sp)}

    def at_rep(d):
        return {"rep": lax.rem(rep + d, count_rep)}

    def frames_out(step):
        return remote(
            flipped.at[:, lax.rem(z + step, RING)], raw.at[z], f_send.at[step - 1], f_recv.at[step - 1],
            sp_at(x, z + step),
        )

    def frames_in(step):
        return remote(
            flipped.at[:, z], raw.at[lax.rem(z + RING - step, RING)], f_send.at[step - 1], f_recv.at[step - 1], up
        )

    def columns(j):
        return pl.ds(pl.multiple_of(j * COLS, COLS), COLS)

    def slot(which, first, count):
        return pl.ds(pl.multiple_of(which * band + first, half), count)

    def own_grad(j):
        return pltpu.make_async_copy(g.at[:, columns(j)], gbuf.at[j, slot(z, 0, band)], g_own.at[j])

    def direct(j, side):
        return remote(
            g.at[:, columns(j)], gbuf.at[j, slot(z, 0, band)], d_send.at[j, side], d_recv.at[j, side],
            up if side == 0 else down,
        )

    def direct_in(j, side):
        return remote(
            g.at[:, columns(j)], gbuf.at[j, slot(z_down if side == 0 else z_up, 0, band)],
            d_send.at[j, side], d_recv.at[j, side], up,
        )

    def forward(j, side):
        ref = gbuf.at[j, slot(z_down if side == 0 else z_up, side * half, half)]
        return remote(ref, ref, r_send.at[j, side], r_recv.at[j, side], up if side == 0 else down)

    def forward_in(j, side):
        ref = gbuf.at[j, slot(lax.rem(z + 2, RING), side * half, half)]
        return remote(ref, ref, r_send.at[j, side], r_recv.at[j, side], up)

    def err_in(j):
        return pltpu.make_async_copy(err.at[:, columns(j)], total.at[j], e_in.at[j])

    def mem_out(j):
        return pltpu.make_async_copy(total.at[j], memory.at[:, columns(j)], out_sem.at[j])

    def far(j, side, group):
        some = pl.ds(group * 3, 3)
        return remote(
            part.at[j, x_far, side, some], relay.at[j, side, some], a_send.at[j, side, group],
            a_recv.at[j, side, group], right if side == 0 else left,
        )

    def near(j, side, group):
        some = pl.ds(group * 3, 3)
        return remote(
            part.at[j, x_right if side == 0 else x_left, :, some], piece.at[j, side, :, some],
            b_send.at[j, side, group], b_recv.at[j, side, group], right if side == 0 else left,
        )

    def q_out(step):
        return remote(q_taps, q_near.at[:, x], q_send.at[step - 1], q_recv.at[step - 1], sp_at(x + step, z))

    def q_in(step):
        source = lax.rem(x + RING - step, RING)
        return remote(q_taps, q_near.at[:, source], q_send.at[step - 1], q_recv.at[step - 1], right)

    def t_out(step):
        return remote(
            t_term.at[lax.rem(z + step, RING)], t_near.at[step - 1], t_send.at[step - 1], t_recv.at[step - 1],
            sp_at(x, z + step),
        )

    def p_scatter(d):
        return remote(p_src.at[lax.rem(sp + d, count_sp)], p_near.at[d - 1], s1.at[d - 1], r1.at[d - 1], at_sp(d))

    def p_share(d):
        return remote(p_one, p_far.at[rep], s2.at[d - 1], r2.at[d - 1], at_rep(d))

    def p_share_in(d):
        source = lax.rem(rep + count_rep - d, count_rep)
        return remote(p_one, p_far.at[source], s2.at[d - 1], r2.at[d - 1], at_rep(d))

    def p_gather(d):
        return remote(p_all.at[sp], p_all.at[sp], s3.at[d - 1], r3.at[d - 1], at_sp(d))

    def p_gather_in(d):
        ref = p_all.at[lax.rem(sp + count_sp - d, count_sp)]
        return remote(ref, ref, s3.at[d - 1], r3.at[d - 1], at_sp(d))

    def q_scatter(d):
        return remote(q_src.at[lax.rem(rep + d, count_rep)], q_got.at[d - 1], s4.at[d - 1], r4.at[d - 1], at_rep(d))

    def q_gather(d):
        return remote(q_next.at[rep], q_next.at[rep], s5.at[d - 1], r5.at[d - 1], at_rep(d))

    def q_gather_in(d):
        ref = q_next.at[lax.rem(rep + count_rep - d, count_rep)]
        return remote(ref, ref, s5.at[d - 1], r5.at[d - 1], at_rep(d))

    barrier = pltpu.get_barrier_semaphore()
    for d in range(1, count_sp):
        pl.semaphore_signal(barrier, inc=1, device_id=at_sp(d), device_id_type=MESH)
    for d in range(1, count_rep):
        pl.semaphore_signal(barrier, inc=1, device_id=at_rep(d), device_id_type=MESH)

    def column_in(i):
        return pltpu.make_async_copy(frames.at[:, columns(i)], local.at[i], l_in.at[i])

    pairs = frames.shape[1] // COLS
    owners = COLS // share
    for i in range(pairs):
        column_in(i).start()
    pl.semaphore_wait(barrier, count_sp + count_rep - 2)
    direct(0, 0).start()
    direct(0, 1).start()

    for i in range(pairs):
        column_in(i).wait()
        turned = local[i].T
        for k in range(owners):
            owner = i * owners + k
            flipped[owner // RING, owner % RING] = turned[k * share : (k + 1) * share]
    for step in (1, 3, 2):
        frames_out(step).start()
    own_frames = pltpu.make_async_copy(flipped.at[:, z], raw.at[z], f_own)
    own_frames.start()
    for j in range(CHUNKS):
        err_in(j).start()
        own_grad(j).start()

    thirds = [third.astype(jnp.float32) for third in split(q_own[...])]
    lanes = q_taps.shape[2]
    thirds.append(jnp.zeros((lanes - 3 * rank, q_own.shape[1]), jnp.float32))
    q_turned[...] = jnp.concatenate(thirds, axis=0).T
    for tap in range(TAPS):
        q_taps[tap] = q_turned[pl.ds(tap, share, stride=TAPS), :].astype(jnp.bfloat16)
    for step in (1, 3, 2):
        q_out(step).start()
    own_q = pltpu.make_async_copy(q_taps, q_near.at[:, x], q_copy)
    own_q.start()

    lane = lax.broadcasted_iota(jnp.int32, (RING * share, width), 1)

    def place(row, value):
        at = pl.ds(pl.multiple_of(row * width, width), width)
        wide = value.astype(jnp.float32)
        taps[0, :, at] = jnp.where(lane == 0, 0.0, pltpu.roll(wide, 1, 1)).astype(taps.dtype)
        taps[1, :, at] = value
        taps[2, :, at] = jnp.where(lane == width - 1, 0.0, pltpu.roll(wide, width - 1, 1)).astype(taps.dtype)

    def place_band(which):
        def place_row(row, carry):
            at = pl.ds(pl.multiple_of(row * width, width), width)
            place(which * (band // width) + row + 1, raw[which, :, :, at].reshape(RING * share, width))
            return carry

        lax.fori_loop(0, band // width, place_row, 0)

    def start_forward(j):
        for side in range(2):
            direct_in(j, side).wait_recv()
            forward(j, side).start()

    def start_direct(j):
        for side in range(2):
            direct(j, side).start()

    start_forward(0)
    own_frames.wait()
    place_band(z)

    for j in range(CHUNKS):
        err_in(j).wait()
        term = exact_dot(q_own[...], total[j], ((1,), (0,)))
        for h in range(2):
            p_src[2 * j + h] = term[h * (rank // 2) : (h + 1) * (rank // 2)]

    frames_in(1).wait_recv()
    frames_in(3).wait_recv()
    start_direct(1)
    place_band(z_down)
    place_band(z_up)
    frames_in(2).wait_recv()
    start_direct(2)

    bottom = raw.at[RING - 1, :, :, band - width : band]
    above = remote(bottom, halo.at[0], h_send.at[0], h_recv.at[0], right)
    below = remote(raw.at[0, :, :, 0:width], halo.at[1], h_send.at[1], h_recv.at[1], left)
    above.start()
    below.start()
    place_band(lax.rem(z + 2, RING))
    rows = RING * band // width
    above.wait()
    below.wait()
    zero = jnp.zeros((RING * share, width), halo.dtype)
    place(0, jnp.where(x == 0, zero, halo[0].reshape(RING * share, width)))
    place(rows + 1, jnp.where(x == RING - 1, zero, halo[1].reshape(RING * share, width)))

    start_forward(1)
    for j in range(CHUNKS):
        own_grad(j).wait()

    def t_band(which):
        acc = None
        for a in range(3):
            for b in range(3):
                at = pl.ds(pl.multiple_of(which * band + a * width, width), band)
                term = jnp.dot(q_flip[a * 3 + b], taps[b, :, at], preferred_element_type=jnp.float32)
                acc = term if acc is None else acc + term
        t_term[which] = acc[:rank] + (acc[rank : 2 * rank] + acc[2 * rank : 3 * rank])

    def t_start():
        own_q.wait()
        for step in (1, 3, 2):
            q_in(step).wait_recv()
        for tap in range(TAPS):
            q_flip[tap] = q_near[tap].reshape(RING * share, lanes).T

    def t_bands(first):
        def one(i, carry):
            t_band(first + i)
            return carry

        lax.fori_loop(0, RING // 2, one, 0)

    def t_finish():
        for step in (1, 3, 2):
            t_out(step).start()

    def p_terms():
        for step in (1, 3, 2):
            t_out(step).wait_recv()
        full = t_term[z] + (t_near[0] + t_near[1] + t_near[2])
        parts = jnp.concatenate(split(full), axis=0)

        def add(j, carry):
            acc = jnp.dot(parts, gbuf[j, slot(z, 0, band)], preferred_element_type=jnp.float32)
            term = acc[:rank] + (acc[rank : 2 * rank] + acc[2 * rank :])
            for h in range(2):
                p_src[2 * j + h] = p_src[2 * j + h] + term[h * (rank // 2) : (h + 1) * (rank // 2)]
            return carry

        lax.fori_loop(0, CHUNKS, add, 0)
        for d in range(1, count_sp):
            p_scatter(d).start()

    def p_sum_sp():
        acc = p_src[sp]
        for d in range(1, count_sp):
            p_scatter(d).wait_recv()
            acc = acc + p_near[d - 1]
        p_one[...] = acc
        p_far[rep] = acc
        for d in range(1, count_rep):
            p_share(d).start()

    def p_sum_rep():
        for d in range(1, count_rep):
            p_share_in(d).wait_recv()
        acc = p_far[0]
        for i in range(1, count_rep):
            acc = acc + p_far[i]
        p_all[sp] = acc
        for d in range(1, count_sp):
            p_gather(d).start()

    def p_chunk(j):
        return jnp.concatenate([p_all[2 * j], p_all[2 * j + 1]], axis=0)

    def orthogonal():
        for d in range(1, count_sp):
            p_gather_in(d).wait_recv()
        gram = jnp.zeros((rank, rank), jnp.float32)
        for j in range(CHUNKS):
            block = p_chunk(j)
            gram = gram + exact_dot(block, block, ((1,), (1,)))
        row_at = lax.broadcasted_iota(jnp.int32, (rank, rank), 0)
        col_at = lax.broadcasted_iota(jnp.int32, (rank, rank), 1)
        work[:, :rank] = gram
        work[:, rank : 2 * rank] = jnp.where(row_at == col_at, 1.0, 0.0)
        shape = (rank, 2 * rank)
        line = lax.broadcasted_iota(jnp.int32, shape, 0)
        spot = lax.broadcasted_iota(jnp.int32, shape, 1)

        def eliminate(k, carry):
            state = work[:, : 2 * rank]
            pivot = work[pl.ds(k, 1), : 2 * rank]
            column = jnp.sum(jnp.where(spot == k, state, 0.0), axis=1, keepdims=True)
            diagonal = jnp.sum(jnp.where(spot[:1] == k, pivot, 0.0), axis=1, keepdims=True)
            inverse = 1.0 / jnp.sqrt(diagonal)
            pivot = pivot * inverse
            work[:, : 2 * rank] = jnp.where(
                line > k, state - (column * inverse) * pivot, jnp.where(line == k, pivot, state)
            )
            return carry

        lax.fori_loop(0, rank, eliminate, 0)
        lower_inverse = jnp.where(col_at <= row_at, work[:, rank : 2 * rank], 0.0)
        for j in range(CHUNKS):
            p_ortho[j] = exact_dot(lower_inverse, p_chunk(j), ((1,), (0,)))
        q_sum[...] = jnp.zeros_like(q_sum)

    def add_q(k):
        q_sum[...] = q_sum[...] + exact_dot(p_ortho[k], total[k], ((1,), (1,)))

    def step(j, carry):
        @pl.when(j + 3 < CHUNKS)
        def _():
            start_direct(j + 3)

        @pl.when(j + 2 < CHUNKS)
        def _():
            start_forward(j + 2)

        @pl.when(j < CHUNKS)
        def _():
            forward_in(j, 0).wait_recv()
            forward_in(j, 1).wait_recv()
            depth = gbuf.shape[1]
            for a in range(3):
                for b in range(3):
                    product = jnp.dot(
                        taps[b, :, a * width : a * width + depth], gbuf[j], preferred_element_type=jnp.float32
                    )
                    count = part.shape[4]
                    for owner in range(RING):
                        for side in range(2):
                            first = (owner * 2 + side) * count
                            part[j, owner, side, a * 3 + b] = product[first : first + count]
                far(j, 0, a).start()
                far(j, 1, a).start()

        @pl.when((j >= 1) & (j <= CHUNKS))
        def _():
            k = j - 1
            for group in range(3):
                some = pl.ds(group * 3, 3)
                far(k, 0, group).wait_recv()
                part[k, x_right, 0, some] = part[k, x_right, 0, some] + relay[k, 0, some]
                near(k, 0, group).start()
                far(k, 1, group).wait_recv()
                part[k, x_left, 1, some] = part[k, x_left, 1, some] + relay[k, 1, some]
                near(k, 1, group).start()

        @pl.when(j == 0)
        def _():
            t_start()
            t_bands(0)

        @pl.when(j == 1)
        def _():
            t_bands(RING // 2)
            t_finish()

        pl.when(j == P_AT)(p_terms)
        pl.when(j == P_AT + 1)(p_sum_sp)
        pl.when(j == P_AT + 2)(p_sum_rep)
        pl.when(j == P_AT + 3)(orthogonal)

        @pl.when(j >= 2)
        def _():
            k = j - 2
            for group in range(3):
                near(k, 0, group).wait_recv()
                near(k, 1, group).wait_recv()
            count = part.shape[4]
            for side in range(2):
                for tap in range(TAPS):
                    at = pl.ds(side * count * TAPS + tap, count, stride=TAPS)
                    total[k, at, :] = (
                        total[k, at, :] + part[k, x, side, tap] + (piece[k, 0, side, tap] + piece[k, 1, side, tap])
                    )

            mem_out(k).start()

            @pl.when(j >= P_AT + 3)
            def _():
                add_q(k)

        @pl.when(j == P_AT + 3)
        def _():
            for k in range(P_AT + 1):
                add_q(k)

        return carry

    lax.fori_loop(0, CHUNKS + 2, step, 0)

    lines = rank // count_rep
    for i in range(count_rep):
        q_src[i] = q_sum[i * lines : (i + 1) * lines]
    for d in range(1, count_rep):
        q_scatter(d).start()
    acc = q_src[rep]
    for d in range(1, count_rep):
        q_scatter(d).wait_recv()
        acc = acc + q_got[d - 1]
    q_next[rep] = acc * (1.0 / count_rep)
    for d in range(1, count_rep):
        q_gather(d).start()
    for d in range(1, count_rep):
        q_gather_in(d).wait_recv()

    def finish(j, carry):
        for side in range(2):
            direct(j, side).wait_send()
            forward(j, side).wait_send()
            for group in range(3):
                far(j, side, group).wait_send()
                near(j, side, group).wait_send()
        mem_out(j).wait()
        return carry

    lax.fori_loop(0, CHUNKS, finish, 0)
    for step_ in (1, 3, 2):
        frames_out(step_).wait_send()
        q_out(step_).wait_send()
        t_out(step_).wait_send()
    for d in range(1, count_sp):
        p_scatter(d).wait_send()
        p_gather(d).wait_send()
    for d in range(1, count_rep):
        p_share(d).wait_send()
        q_scatter(d).wait_send()
        q_gather(d).wait_send()


def compressed_step(count_rep, frames, g, err, q_own):
    band, chans = g.shape
    width = band // 4
    rows = err.shape[0]
    rank = q_own.shape[0]
    count_sp = RING * RING
    share = chans // count_sp
    per_side = share // 2
    dma = pltpu.SemaphoreType.DMA
    two, three = dma((CHUNKS, 2)), dma((CHUNKS, 2, 3))
    f32, bf16 = jnp.float32, jnp.bfloat16
    any_spec, vmem_spec = pl.BlockSpec(memory_space=pl.ANY), pl.BlockSpec(memory_space=pltpu.VMEM)
    p_block = (rank // 2, COLS)
    q_block = (rank // count_rep, rows)
    return pl.pallas_call(
        functools.partial(step_kernel, count_rep),
        out_shape=(
            jax.ShapeDtypeStruct((rows, chans), f32),
            jax.ShapeDtypeStruct((count_rep, *q_block), f32),
            jax.ShapeDtypeStruct((CHUNKS, rank, COLS), f32),
        ),
        in_specs=[any_spec, any_spec, any_spec, vmem_spec],
        out_specs=(any_spec, vmem_spec, vmem_spec),
        scratch_shapes=[
            pltpu.VMEM((chans // COLS, band, COLS), bf16),
            pltpu.VMEM((rows, 128), f32),
            pltpu.VMEM((TAPS, share, 128), bf16),
            pltpu.VMEM((RING, RING, share, band), bf16),
            pltpu.VMEM((RING, RING, share, band), bf16),
            pltpu.VMEM((2, RING, share, width), bf16),
            pltpu.VMEM((3, RING * share, RING * band + 2 * width), bf16),
            pltpu.VMEM((CHUNKS, RING * band, COLS), bf16),
            pltpu.VMEM((CHUNKS, RING, 2, TAPS, per_side, COLS), f32),
            pltpu.VMEM((CHUNKS, 2, TAPS, per_side, COLS), f32),
            pltpu.VMEM((CHUNKS, 2, 2, TAPS, per_side, COLS), f32),
            pltpu.VMEM((CHUNKS, rows, COLS), f32),
            pltpu.VMEM((TAPS, RING, share, 128), bf16),
            pltpu.VMEM((TAPS, 128, RING * share), bf16),
            pltpu.VMEM((RING, rank, band), f32),
            pltpu.VMEM((RING - 1, rank, band), f32),
            pltpu.VMEM((count_sp, *p_block), f32),
            pltpu.VMEM((count_sp - 1, *p_block), f32),
            pltpu.VMEM(p_block, f32),
            pltpu.VMEM((count_rep, *p_block), f32),
            pltpu.VMEM((count_sp, *p_block), f32),
            pltpu.VMEM((rank, 128), f32),
            pltpu.VMEM((count_rep, *q_block), f32),
            pltpu.VMEM((count_rep - 1, *q_block), f32),
            pltpu.VMEM((rank, rows), f32),
            dma((chans // COLS,)), dma((3,)), dma((3,)), dma, dma((2,)), dma((2,)), dma((CHUNKS,)), dma((CHUNKS,)),
            two, two, two, two, three, three, three, three, dma((CHUNKS,)),
            dma((3,)), dma((3,)), dma, dma((3,)), dma((3,)),
            dma((count_sp - 1,)), dma((count_sp - 1,)), dma((count_rep - 1,)), dma((count_rep - 1,)),
            dma((count_sp - 1,)), dma((count_sp - 1,)), dma((count_rep - 1,)), dma((count_rep - 1,)),
            dma((count_rep - 1,)), dma((count_rep - 1,)),
        ],
        compiler_params=pltpu.CompilerParams(
            collective_id=0, has_side_effects=True, vmem_limit_bytes=58 * 1024 * 1024
        ),
        cost_estimate=pl.CostEstimate(flops=2 * rows * 16 * chans * band, bytes_accessed=10**7, transcendentals=0),
        name="compressed_step",
    )(frames, g, err, q_own)


def feedback_kernel(memory, q_parts, p_ortho, error_next, q_next, q_side):
    count, lines, rows = q_parts.shape

    @pl.when(pl.program_id(0) == 0)
    def _():
        for i in range(count):
            q_next[i * lines : (i + 1) * lines] = q_parts[i]
        q0, q1, q2 = split(q_next[...])
        q_side[...] = jnp.concatenate([q0, q0, q0, q1, q1, q2], axis=0).T

    for i in range(p_ortho.shape[0]):
        p0, p1, p2 = split(p_ortho[i])
        p_side = jnp.concatenate([p0, p1, p2, p0, p1, p0], axis=0)
        at = slice(i * COLS, (i + 1) * COLS)
        error_next[:, at] = memory[:, at] - jnp.dot(q_side[...], p_side, preferred_element_type=jnp.float32)


def feedback(memory, q_parts, p_ortho):
    rows, chans = memory.shape
    count, lines, _ = q_parts.shape
    rank = count * lines
    per_block = 2
    block = (rows, per_block * COLS)
    return pl.pallas_call(
        feedback_kernel,
        grid=(chans // block[1],),
        out_shape=(jax.ShapeDtypeStruct(memory.shape, jnp.float32), jax.ShapeDtypeStruct((rank, rows), jnp.float32)),
        in_specs=[
            pl.BlockSpec(block, lambda i: (0, i)),
            pl.BlockSpec(q_parts.shape, lambda i: (0, 0, 0)),
            pl.BlockSpec((per_block, rank, COLS), lambda i: (i, 0, 0)),
        ],
        out_specs=(pl.BlockSpec(block, lambda i: (0, i)), pl.BlockSpec((rank, rows), lambda i: (0, 0))),
        scratch_shapes=[pltpu.VMEM((rows, 6 * rank), jnp.bfloat16)],
        compiler_params=pltpu.CompilerParams(vmem_limit_bytes=32 * 1024 * 1024),
        name="feedback",
    )(memory, q_parts, p_ortho)


def per_device(count_rep, frames, out_grad, error_prev, q_prev):
    band_rows, width, chans = frames.shape[1:]
    band = band_rows * width
    memory, q_parts, p_ortho = compressed_step(
        count_rep,
        frames[0].reshape(band, chans),
        out_grad[0].reshape(band, chans),
        error_prev[0],
        q_prev,
    )
    error_next, q_next = feedback(memory, q_parts, p_ortho)
    return (error_next[None], q_next)


def solution(mesh):
    placed = (
        P("rep", "sp", None, None),
        P("rep", "sp", None, None),
        P("rep", "sp", None),
        P(None, "sp"),
    )
    return jax.shard_map(
        functools.partial(per_device, mesh.shape["rep"]),
        mesh=mesh,
        in_specs=placed,
        out_specs=(P("rep", "sp", None), P(None, "sp")),
        check_vma=False,
    )
```

```python
import functools

import jax
import jax.numpy as jnp
from jax import lax
from jax.experimental import pallas as pl
from jax.experimental.pallas import tpu as pltpu
from jax.sharding import PartitionSpec as P

MESH = pl.DeviceIdType.MESH
RING = 4
CHUNKS = 8
COLS = 128
TAPS = 9
T_AT = 1
P_AT = 2
EARLY = 3


def sp_at(x, z):
    return {"sp": lax.rem(x + RING, RING) * RING + lax.rem(z + RING, RING)}


def remote(src, dst, send, recv, device):
    return pltpu.make_async_remote_copy(
        src_ref=src, dst_ref=dst, send_sem=send, recv_sem=recv, device_id=device, device_id_type=MESH
    )


def split(value):
    high = value.astype(jnp.bfloat16)
    rest = value - high.astype(jnp.float32)
    middle = rest.astype(jnp.bfloat16)
    low = (rest - middle.astype(jnp.float32)).astype(jnp.bfloat16)
    return high, middle, low


def exact_dot(a, b, contract):
    return lax.dot_general(
        a, b, (contract, ((), ())), precision=lax.Precision.HIGHEST, preferred_element_type=jnp.float32
    )


def step_kernel(
    count_rep, frames, g, err, q_own, memory, q_next, p_ortho,
    local, q_turned, q_taps, flipped, raw, halo, taps, gbuf, part, relay, piece, total,
    q_near, q_flip, t_term, t_near, p_src, p_near, p_one, p_far, p_all, work, q_src, q_got, q_sum,
    l_in, f_send, f_recv, f_own, h_send, h_recv, e_in, g_own,
    d_send, d_recv, r_send, r_recv, a_send, a_recv, b_send, b_recv, out_sem,
    q_send, q_recv, q_copy, t_send, t_recv, s1, r1, s2, r2, s3, r3, s4, r4, s5, r5,
):
    sp, rep = lax.axis_index("sp"), lax.axis_index("rep")
    x, z = sp // RING, lax.rem(sp, RING)
    up, down = sp_at(x, z + 1), sp_at(x, z - 1)
    right, left = sp_at(x + 1, z), sp_at(x - 1, z)
    z_up, z_down = lax.rem(z + 1, RING), lax.rem(z + 3, RING)
    x_right, x_left, x_far = lax.rem(x + 1, RING), lax.rem(x + 3, RING), lax.rem(x + 2, RING)
    band = g.shape[0]
    half = band // 2
    count_sp = RING * RING
    share = part.shape[4] * 2
    width = halo.shape[3]
    rank = q_own.shape[0]

    def at_sp(d):
        return {"sp": lax.rem(sp + d, count_sp)}

    def at_rep(d):
        return {"rep": lax.rem(rep + d, count_rep)}

    def frames_out(step):
        return remote(
            flipped.at[:, lax.rem(z + step, RING)], raw.at[z], f_send.at[step - 1], f_recv.at[step - 1],
            sp_at(x, z + step),
        )

    def frames_in(step):
        return remote(
            flipped.at[:, z], raw.at[lax.rem(z + RING - step, RING)], f_send.at[step - 1], f_recv.at[step - 1], up
        )

    def columns(j):
        return pl.ds(pl.multiple_of(j * COLS, COLS), COLS)

    def slot(which, first, count):
        return pl.ds(pl.multiple_of(which * band + first, half), count)

    def own_grad(j):
        return pltpu.make_async_copy(g.at[:, columns(j)], gbuf.at[j, slot(z, 0, band)], g_own.at[j])

    def direct(j, side):
        return remote(
            g.at[:, columns(j)], gbuf.at[j, slot(z, 0, band)], d_send.at[j, side], d_recv.at[j, side],
            up if side == 0 else down,
        )

    def direct_in(j, side):
        return remote(
            g.at[:, columns(j)], gbuf.at[j, slot(z_down if side == 0 else z_up, 0, band)],
            d_send.at[j, side], d_recv.at[j, side], up,
        )

    def forward(j, side):
        ref = gbuf.at[j, slot(z_down if side == 0 else z_up, side * half, half)]
        return remote(ref, ref, r_send.at[j, side], r_recv.at[j, side], up if side == 0 else down)

    def forward_in(j, side):
        ref = gbuf.at[j, slot(lax.rem(z + 2, RING), side * half, half)]
        return remote(ref, ref, r_send.at[j, side], r_recv.at[j, side], up)

    def err_in(j):
        return pltpu.make_async_copy(err.at[:, columns(j)], total.at[j], e_in.at[j])

    def mem_out(j):
        return pltpu.make_async_copy(total.at[j], memory.at[:, columns(j)], out_sem.at[j])

    def far(j, side, group):
        some = pl.ds(group * 3, 3)
        return remote(
            part.at[j, x_far, side, some], relay.at[j, side, some], a_send.at[j, side, group],
            a_recv.at[j, side, group], right if side == 0 else left,
        )

    def near(j, side, group):
        some = pl.ds(group * 3, 3)
        return remote(
            part.at[j, x_right if side == 0 else x_left, :, some], piece.at[j, side, :, some],
            b_send.at[j, side, group], b_recv.at[j, side, group], right if side == 0 else left,
        )

    def q_out(step):
        return remote(q_taps, q_near.at[:, x], q_send.at[step - 1], q_recv.at[step - 1], sp_at(x + step, z))

    def q_in(step):
        source = lax.rem(x + RING - step, RING)
        return remote(q_taps, q_near.at[:, source], q_send.at[step - 1], q_recv.at[step - 1], right)

    def t_out(step):
        return remote(
            t_term.at[lax.rem(z + step, RING)], t_near.at[step - 1], t_send.at[step - 1], t_recv.at[step - 1],
            sp_at(x, z + step),
        )

    def p_scatter(d):
        return remote(p_src.at[lax.rem(sp + d, count_sp)], p_near.at[d - 1], s1.at[d - 1], r1.at[d - 1], at_sp(d))

    def p_share(d):
        return remote(p_one, p_far.at[rep], s2.at[d - 1], r2.at[d - 1], at_rep(d))

    def p_share_in(d):
        source = lax.rem(rep + count_rep - d, count_rep)
        return remote(p_one, p_far.at[source], s2.at[d - 1], r2.at[d - 1], at_rep(d))

    def p_gather(d):
        return remote(p_all.at[sp], p_all.at[sp], s3.at[d - 1], r3.at[d - 1], at_sp(d))

    def p_gather_in(d):
        ref = p_all.at[lax.rem(sp + count_sp - d, count_sp)]
        return remote(ref, ref, s3.at[d - 1], r3.at[d - 1], at_sp(d))

    def q_scatter(d):
        return remote(q_src.at[lax.rem(rep + d, count_rep)], q_got.at[d - 1], s4.at[d - 1], r4.at[d - 1], at_rep(d))

    def q_gather(d):
        return remote(q_next.at[rep], q_next.at[rep], s5.at[d - 1], r5.at[d - 1], at_rep(d))

    def q_gather_in(d):
        ref = q_next.at[lax.rem(rep + count_rep - d, count_rep)]
        return remote(ref, ref, s5.at[d - 1], r5.at[d - 1], at_rep(d))

    barrier = pltpu.get_barrier_semaphore()
    for d in range(1, count_sp):
        pl.semaphore_signal(barrier, inc=1, device_id=at_sp(d), device_id_type=MESH)
    for d in range(1, count_rep):
        pl.semaphore_signal(barrier, inc=1, device_id=at_rep(d), device_id_type=MESH)

    def column_in(i):
        return pltpu.make_async_copy(frames.at[:, columns(i)], local.at[i], l_in.at[i])

    pairs = frames.shape[1] // COLS
    owners = COLS // share
    for i in range(pairs):
        column_in(i).start()
    pl.semaphore_wait(barrier, count_sp + count_rep - 2)
    direct(0, 0).start()
    direct(0, 1).start()

    for i in range(pairs):
        column_in(i).wait()
        turned = local[i].T
        for k in range(owners):
            owner = i * owners + k
            flipped[owner // RING, owner % RING] = turned[k * share : (k + 1) * share]
    for step in (1, 3, 2):
        frames_out(step).start()
    own_frames = pltpu.make_async_copy(flipped.at[:, z], raw.at[z], f_own)
    own_frames.start()
    for j in range(CHUNKS):
        err_in(j).start()
        own_grad(j).start()

    thirds = [third.astype(jnp.float32) for third in split(q_own[...])]
    lanes = q_taps.shape[2]
    thirds.append(jnp.zeros((lanes - 3 * rank, q_own.shape[1]), jnp.float32))
    q_turned[...] = jnp.concatenate(thirds, axis=0).T
    for tap in range(TAPS):
        q_taps[tap] = q_turned[pl.ds(tap, share, stride=TAPS), :].astype(jnp.bfloat16)
    for step in (1, 3, 2):
        q_out(step).start()
    own_q = pltpu.make_async_copy(q_taps, q_near.at[:, x], q_copy)
    own_q.start()

    lane = lax.broadcasted_iota(jnp.int32, (RING * share, width), 1)

    def place(row, value):
        at = pl.ds(pl.multiple_of(row * width, width), width)
        wide = value.astype(jnp.float32)
        taps[0, :, at] = jnp.where(lane == 0, 0.0, pltpu.roll(wide, 1, 1)).astype(taps.dtype)
        taps[1, :, at] = value
        taps[2, :, at] = jnp.where(lane == width - 1, 0.0, pltpu.roll(wide, width - 1, 1)).astype(taps.dtype)

    def place_band(which):
        def place_row(row, carry):
            at = pl.ds(pl.multiple_of(row * width, width), width)
            place(which * (band // width) + row + 1, raw[which, :, :, at].reshape(RING * share, width))
            return carry

        lax.fori_loop(0, band // width, place_row, 0)

    def start_forward(j):
        for side in range(2):
            direct_in(j, side).wait_recv()
            forward(j, side).start()

    def start_direct(j):
        for side in range(2):
            direct(j, side).start()

    start_forward(0)
    own_frames.wait()
    place_band(z)

    for j in range(CHUNKS):
        err_in(j).wait()
        term = exact_dot(q_own[...], total[j], ((1,), (0,)))
        for h in range(2):
            p_src[2 * j + h] = term[h * (rank // 2) : (h + 1) * (rank // 2)]

    frames_in(1).wait_recv()
    frames_in(3).wait_recv()
    start_direct(1)
    place_band(z_down)
    place_band(z_up)
    frames_in(2).wait_recv()
    start_direct(2)

    bottom = raw.at[RING - 1, :, :, band - width : band]
    above = remote(bottom, halo.at[0], h_send.at[0], h_recv.at[0], right)
    below = remote(raw.at[0, :, :, 0:width], halo.at[1], h_send.at[1], h_recv.at[1], left)
    above.start()
    below.start()
    place_band(lax.rem(z + 2, RING))
    rows = RING * band // width
    above.wait()
    below.wait()
    zero = jnp.zeros((RING * share, width), halo.dtype)
    place(0, jnp.where(x == 0, zero, halo[0].reshape(RING * share, width)))
    place(rows + 1, jnp.where(x == RING - 1, zero, halo[1].reshape(RING * share, width)))

    start_forward(1)
    for j in range(CHUNKS):
        own_grad(j).wait()

    def t_band(which):
        acc = None
        for a in range(3):
            at = pl.ds(pl.multiple_of(which * band + a * width, width), band)
            stacked = taps[:, :, at].reshape(3 * RING * share, band)
            term = jnp.dot(q_flip[a], stacked, preferred_element_type=jnp.float32)
            acc = term if acc is None else acc + term
        t_term[which] = acc[:rank] + (acc[rank : 2 * rank] + acc[2 * rank : 3 * rank])

    def t_start():
        own_q.wait()
        for step in (1, 3, 2):
            q_in(step).wait_recv()
        for a in range(3):
            q_flip[a] = q_near[3 * a : 3 * a + 3].reshape(3 * RING * share, lanes).T

    def t_bands(first):
        def one(i, carry):
            t_band(first + i)
            return carry

        lax.fori_loop(0, RING // 2, one, 0)

    def t_finish():
        for step in (1, 3, 2):
            t_out(step).start()

    def p_terms():
        for step in (1, 3, 2):
            t_out(step).wait_recv()
        full = t_term[z] + (t_near[0] + t_near[1] + t_near[2])
        parts = jnp.concatenate(split(full), axis=0)

        def add(j, carry):
            acc = jnp.dot(parts, gbuf[j, slot(z, 0, band)], preferred_element_type=jnp.float32)
            term = acc[:rank] + (acc[rank : 2 * rank] + acc[2 * rank :])
            for h in range(2):
                p_src[2 * j + h] = p_src[2 * j + h] + term[h * (rank // 2) : (h + 1) * (rank // 2)]
            return carry

        lax.fori_loop(0, CHUNKS, add, 0)
        for d in range(1, count_sp):
            p_scatter(d).start()

    def p_sum_sp():
        acc = p_src[sp]
        for d in range(1, count_sp):
            p_scatter(d).wait_recv()
            acc = acc + p_near[d - 1]
        p_one[...] = acc
        p_far[rep] = acc
        for d in range(1, count_rep):
            p_share(d).start()

    def p_sum_rep():
        for d in range(1, count_rep):
            p_share_in(d).wait_recv()
        acc = p_far[0]
        for i in range(1, count_rep):
            acc = acc + p_far[i]
        p_all[sp] = acc
        for d in range(1, count_sp):
            p_gather(d).start()

    def p_chunk(j):
        return jnp.concatenate([p_all[2 * j], p_all[2 * j + 1]], axis=0)

    def orthogonal():
        for d in range(1, count_sp):
            p_gather_in(d).wait_recv()
        p_total = jnp.concatenate([p_chunk(j) for j in range(CHUNKS)], axis=1)
        gram = exact_dot(p_total, p_total, ((1,), (1,)))
        row_at = lax.broadcasted_iota(jnp.int32, (rank, rank), 0)
        col_at = lax.broadcasted_iota(jnp.int32, (rank, rank), 1)
        work[:, :rank] = gram
        work[:, rank : 2 * rank] = jnp.where(row_at == col_at, 1.0, 0.0)
        shape = (rank, 2 * rank)
        line = lax.broadcasted_iota(jnp.int32, shape, 0)
        spot = lax.broadcasted_iota(jnp.int32, shape, 1)

        def eliminate(k, carry):
            state = work[:, : 2 * rank]
            pivot = work[pl.ds(k, 1), : 2 * rank]
            column = jnp.sum(jnp.where(spot == k, state, 0.0), axis=1, keepdims=True)
            diagonal = jnp.sum(jnp.where(spot[:1] == k, pivot, 0.0), axis=1, keepdims=True)
            inverse = 1.0 / jnp.sqrt(diagonal)
            pivot = pivot * inverse
            work[:, : 2 * rank] = jnp.where(
                line > k, state - (column * inverse) * pivot, jnp.where(line == k, pivot, state)
            )
            return carry

        lax.fori_loop(0, rank, eliminate, 0)
        lower_inverse = jnp.where(col_at <= row_at, work[:, rank : 2 * rank], 0.0)
        whole = exact_dot(lower_inverse, p_total, ((1,), (0,)))
        for j in range(CHUNKS):
            p_ortho[j] = whole[:, j * COLS : (j + 1) * COLS]
        q_sum[...] = jnp.zeros_like(q_sum)

    def add_q(k):
        m0, m1, m2 = split(total[k])
        p0, p1, p2 = split(p_ortho[k])
        m_side = jnp.concatenate([m0, m0, m0, m1, m1, m2], axis=1)
        p_side = jnp.concatenate([p0, p1, p2, p0, p1, p0], axis=1).T
        q_sum[:, :rank] = q_sum[:, :rank] + jnp.dot(m_side, p_side, preferred_element_type=jnp.float32)

    def multiply(first, count):
        depth = gbuf.shape[1]
        per_side = part.shape[4]

        def one(a, carry):
            at = pl.ds(pl.multiple_of(a * width, width), depth)
            stacked = taps[:, :, at].reshape(3 * RING * share, depth)
            chosen = gbuf[first] if count == 1 else jnp.concatenate([gbuf[first], gbuf[first + 1]], axis=1)
            product = jnp.dot(stacked, chosen, preferred_element_type=jnp.float32)
            for c in range(count):
                for b in range(3):
                    for owner in range(RING):
                        for side in range(2):
                            line = b * RING * share + (owner * 2 + side) * per_side
                            part[first + c, owner, side, a * 3 + b] = product[
                                line : line + per_side, c * COLS : (c + 1) * COLS
                            ]
                far(first + c, 0, a).start()
                far(first + c, 1, a).start()
            return carry

        lax.fori_loop(0, 3, one, 0)

    def pass_on(k):
        for group in range(3):
            some = pl.ds(group * 3, 3)
            far(k, 0, group).wait_recv()
            part[k, x_right, 0, some] = part[k, x_right, 0, some] + relay[k, 0, some]
            near(k, 0, group).start()
            far(k, 1, group).wait_recv()
            part[k, x_left, 1, some] = part[k, x_left, 1, some] + relay[k, 1, some]
            near(k, 1, group).start()

    def complete(k, with_q):
        for group in range(3):
            near(k, 0, group).wait_recv()
            near(k, 1, group).wait_recv()
        count = part.shape[4]
        for side in range(2):
            for tap in range(TAPS):
                at = pl.ds(side * count * TAPS + tap, count, stride=TAPS)
                total[k, at, :] = (
                    total[k, at, :] + part[k, x, side, tap] + (piece[k, 0, side, tap] + piece[k, 1, side, tap])
                )
        mem_out(k).start()
        pl.when(with_q)(lambda: add_q(k))

    def over(first, count, body):
        def one(i, carry):
            body(first + i)
            return carry

        lax.fori_loop(0, count, one, 0)

    def step(j, carry):
        @pl.when(j + 3 < CHUNKS)
        def _():
            start_direct(j + 3)

        @pl.when(j + 2 < CHUNKS)
        def _():
            start_forward(j + 2)

        @pl.when(j < CHUNKS)
        def _():
            forward_in(j, 0).wait_recv()
            forward_in(j, 1).wait_recv()

        alone = (j == 0) | (j == CHUNKS - 1)
        paired = (j > 0) & (j < CHUNKS - 1) & (lax.rem(j, 2) == 0)
        pl.when(alone)(lambda: multiply(j, 1))
        pl.when(paired)(lambda: multiply(j - 1, 2))

        pl.when((j == 1) | (j == CHUNKS))(lambda: pass_on(j - 1))
        pl.when((j > 1) & (j < CHUNKS) & (lax.rem(j, 2) == 1))(lambda: over(j - 2, 2, pass_on))

        @pl.when(j == T_AT)
        def _():
            t_start()
            t_bands(0)
            t_bands(RING // 2)
            t_finish()

        pl.when(j == P_AT)(p_terms)
        pl.when(j == P_AT + 1)(p_sum_sp)
        pl.when(j == P_AT + 2)(p_sum_rep)
        pl.when(j == P_AT + 3)(orthogonal)
        ready = j >= P_AT + 3

        pl.when((j == 2) | (j == CHUNKS + 1))(lambda: complete(lax.select(j == 2, 0, CHUNKS - 1), ready))
        pl.when((j > 2) & (j <= CHUNKS) & (lax.rem(j, 2) == 0))(
            lambda: over(j - 3, 2, lambda k: complete(k, ready))
        )
        pl.when(j == P_AT + 3)(lambda: over(0, EARLY, add_q))

        return carry

    lax.fori_loop(0, CHUNKS + 2, step, 0)

    lines = rank // count_rep
    q_lines = q_sum[...].T
    for i in range(count_rep):
        q_src[i] = q_lines[i * lines : (i + 1) * lines]
    for d in range(1, count_rep):
        q_scatter(d).start()
    acc = q_src[rep]
    for d in range(1, count_rep):
        q_scatter(d).wait_recv()
        acc = acc + q_got[d - 1]
    q_next[rep] = acc * (1.0 / count_rep)
    for d in range(1, count_rep):
        q_gather(d).start()
    for d in range(1, count_rep):
        q_gather_in(d).wait_recv()

    def finish(j, carry):
        for side in range(2):
            direct(j, side).wait_send()
            forward(j, side).wait_send()
            for group in range(3):
                far(j, side, group).wait_send()
                near(j, side, group).wait_send()
        mem_out(j).wait()
        return carry

    lax.fori_loop(0, CHUNKS, finish, 0)
    for step_ in (1, 3, 2):
        frames_out(step_).wait_send()
        q_out(step_).wait_send()
        t_out(step_).wait_send()
    for d in range(1, count_sp):
        p_scatter(d).wait_send()
        p_gather(d).wait_send()
    for d in range(1, count_rep):
        p_share(d).wait_send()
        q_scatter(d).wait_send()
        q_gather(d).wait_send()


def compressed_step(count_rep, frames, g, err, q_own):
    band, chans = g.shape
    width = band // 4
    rows = err.shape[0]
    rank = q_own.shape[0]
    count_sp = RING * RING
    share = chans // count_sp
    per_side = share // 2
    dma = pltpu.SemaphoreType.DMA
    two, three = dma((CHUNKS, 2)), dma((CHUNKS, 2, 3))
    f32, bf16 = jnp.float32, jnp.bfloat16
    any_spec, vmem_spec = pl.BlockSpec(memory_space=pl.ANY), pl.BlockSpec(memory_space=pltpu.VMEM)
    p_block = (rank // 2, COLS)
    q_block = (rank // count_rep, rows)
    return pl.pallas_call(
        functools.partial(step_kernel, count_rep),
        out_shape=(
            jax.ShapeDtypeStruct((rows, chans), f32),
            jax.ShapeDtypeStruct((count_rep, *q_block), f32),
            jax.ShapeDtypeStruct((CHUNKS, rank, COLS), f32),
        ),
        in_specs=[any_spec, any_spec, any_spec, vmem_spec],
        out_specs=(any_spec, vmem_spec, vmem_spec),
        scratch_shapes=[
            pltpu.VMEM((chans // COLS, band, COLS), bf16),
            pltpu.VMEM((rows, 128), f32),
            pltpu.VMEM((TAPS, share, 128), bf16),
            pltpu.VMEM((RING, RING, share, band), bf16),
            pltpu.VMEM((RING, RING, share, band), bf16),
            pltpu.VMEM((2, RING, share, width), bf16),
            pltpu.VMEM((3, RING * share, RING * band + 2 * width), bf16),
            pltpu.VMEM((CHUNKS, RING * band, COLS), bf16),
            pltpu.VMEM((CHUNKS, RING, 2, TAPS, per_side, COLS), f32),
            pltpu.VMEM((CHUNKS, 2, TAPS, per_side, COLS), f32),
            pltpu.VMEM((CHUNKS, 2, 2, TAPS, per_side, COLS), f32),
            pltpu.VMEM((CHUNKS, rows, COLS), f32),
            pltpu.VMEM((TAPS, RING, share, 128), bf16),
            pltpu.VMEM((3, 128, 3 * RING * share), bf16),
            pltpu.VMEM((RING, rank, band), f32),
            pltpu.VMEM((RING - 1, rank, band), f32),
            pltpu.VMEM((count_sp, *p_block), f32),
            pltpu.VMEM((count_sp - 1, *p_block), f32),
            pltpu.VMEM(p_block, f32),
            pltpu.VMEM((count_rep, *p_block), f32),
            pltpu.VMEM((count_sp, *p_block), f32),
            pltpu.VMEM((rank, 128), f32),
            pltpu.VMEM((count_rep, *q_block), f32),
            pltpu.VMEM((count_rep - 1, *q_block), f32),
            pltpu.VMEM((rows, 128), f32),
            dma((chans // COLS,)), dma((3,)), dma((3,)), dma, dma((2,)), dma((2,)), dma((CHUNKS,)), dma((CHUNKS,)),
            two, two, two, two, three, three, three, three, dma((CHUNKS,)),
            dma((3,)), dma((3,)), dma, dma((3,)), dma((3,)),
            dma((count_sp - 1,)), dma((count_sp - 1,)), dma((count_rep - 1,)), dma((count_rep - 1,)),
            dma((count_sp - 1,)), dma((count_sp - 1,)), dma((count_rep - 1,)), dma((count_rep - 1,)),
            dma((count_rep - 1,)), dma((count_rep - 1,)),
        ],
        compiler_params=pltpu.CompilerParams(
            collective_id=0, has_side_effects=True, vmem_limit_bytes=58 * 1024 * 1024
        ),
        cost_estimate=pl.CostEstimate(flops=2 * rows * 16 * chans * band, bytes_accessed=10**7, transcendentals=0),
        name="compressed_step",
    )(frames, g, err, q_own)


def feedback_kernel(memory, q_parts, p_ortho, error_next, q_next, q_side):
    count, lines, rows = q_parts.shape

    @pl.when(pl.program_id(0) == 0)
    def _():
        for i in range(count):
            q_next[i * lines : (i + 1) * lines] = q_parts[i]
        q0, q1, q2 = split(q_next[...])
        q_side[...] = jnp.concatenate([q0, q0, q0, q1, q1, q2], axis=0).T

    for i in range(p_ortho.shape[0]):
        p0, p1, p2 = split(p_ortho[i])
        p_side = jnp.concatenate([p0, p1, p2, p0, p1, p0], axis=0)
        at = slice(i * COLS, (i + 1) * COLS)
        error_next[:, at] = memory[:, at] - jnp.dot(q_side[...], p_side, preferred_element_type=jnp.float32)


def feedback(memory, q_parts, p_ortho):
    rows, chans = memory.shape
    count, lines, _ = q_parts.shape
    rank = count * lines
    per_block = 2
    block = (rows, per_block * COLS)
    return pl.pallas_call(
        feedback_kernel,
        grid=(chans // block[1],),
        out_shape=(jax.ShapeDtypeStruct(memory.shape, jnp.float32), jax.ShapeDtypeStruct((rank, rows), jnp.float32)),
        in_specs=[
            pl.BlockSpec(block, lambda i: (0, i)),
            pl.BlockSpec(q_parts.shape, lambda i: (0, 0, 0)),
            pl.BlockSpec((per_block, rank, COLS), lambda i: (i, 0, 0)),
        ],
        out_specs=(pl.BlockSpec(block, lambda i: (0, i)), pl.BlockSpec((rank, rows), lambda i: (0, 0))),
        scratch_shapes=[pltpu.VMEM((rows, 6 * rank), jnp.bfloat16)],
        compiler_params=pltpu.CompilerParams(vmem_limit_bytes=60 * 1024 * 1024),
        name="feedback",
    )(memory, q_parts, p_ortho)


def per_device(count_rep, frames, out_grad, error_prev, q_prev):
    band_rows, width, chans = frames.shape[1:]
    band = band_rows * width
    memory, q_parts, p_ortho = compressed_step(
        count_rep,
        frames[0].reshape(band, chans),
        out_grad[0].reshape(band, chans),
        error_prev[0],
        q_prev,
    )
    error_next, q_next = feedback(memory, q_parts, p_ortho)
    return (error_next[None], q_next)


def solution(mesh):
    placed = (
        P("rep", "sp", None, None),
        P("rep", "sp", None, None),
        P("rep", "sp", None),
        P(None, "sp"),
    )
    return jax.shard_map(
        functools.partial(per_device, mesh.shape["rep"]),
        mesh=mesh,
        in_specs=placed,
        out_specs=(P("rep", "sp", None), P(None, "sp")),
        check_vma=False,
    )
```

```python
import functools

import jax
import jax.numpy as jnp
from jax import lax
from jax.experimental import pallas as pl
from jax.experimental.pallas import tpu as pltpu
from jax.sharding import PartitionSpec as P

MESH = pl.DeviceIdType.MESH
RING = 4
CHUNKS = 8
COLS = 128
TAPS = 9
T_AT = 0
P_AT = (2, 4, 5, 7)
EARLY = 5


def sp_at(x, z):
    return {"sp": lax.rem(x + RING, RING) * RING + lax.rem(z + RING, RING)}


def remote(src, dst, send, recv, device):
    return pltpu.make_async_remote_copy(
        src_ref=src, dst_ref=dst, send_sem=send, recv_sem=recv, device_id=device, device_id_type=MESH
    )


def split(value):
    high = value.astype(jnp.bfloat16)
    rest = value - high.astype(jnp.float32)
    middle = rest.astype(jnp.bfloat16)
    low = (rest - middle.astype(jnp.float32)).astype(jnp.bfloat16)
    return high, middle, low


def exact_dot(a, b, contract):
    return lax.dot_general(
        a, b, (contract, ((), ())), precision=lax.Precision.HIGHEST, preferred_element_type=jnp.float32
    )


def step_kernel(
    count_rep, frames, g, err, q_own, memory, q_next, p_ortho,
    local, q_turned, q_taps, flipped, raw, halo, taps, gbuf, part, relay, piece, total,
    q_near, q_flip, t_term, t_near, p_src, p_near, p_one, p_far, p_all, work, q_src, q_got, q_sum,
    l_in, f_send, f_recv, f_own, h_send, h_recv, e_in, g_own,
    d_send, d_recv, r_send, r_recv, a_send, a_recv, b_send, b_recv, out_sem,
    q_send, q_recv, q_copy, t_send, t_recv, s1, r1, s2, r2, s3, r3, s4, r4, s5, r5,
):
    sp, rep = lax.axis_index("sp"), lax.axis_index("rep")
    x, z = sp // RING, lax.rem(sp, RING)
    up, down = sp_at(x, z + 1), sp_at(x, z - 1)
    right, left = sp_at(x + 1, z), sp_at(x - 1, z)
    z_up, z_down = lax.rem(z + 1, RING), lax.rem(z + 3, RING)
    x_right, x_left, x_far = lax.rem(x + 1, RING), lax.rem(x + 3, RING), lax.rem(x + 2, RING)
    band = g.shape[0]
    half = band // 2
    count_sp = RING * RING
    share = part.shape[4] * 2
    width = halo.shape[3]
    rank = q_own.shape[0]

    def at_sp(d):
        return {"sp": lax.rem(sp + d, count_sp)}

    def at_rep(d):
        return {"rep": lax.rem(rep + d, count_rep)}

    def frames_out(step):
        return remote(
            flipped.at[:, lax.rem(z + step, RING)], raw.at[z], f_send.at[step - 1], f_recv.at[step - 1],
            sp_at(x, z + step),
        )

    def frames_in(step):
        return remote(
            flipped.at[:, z], raw.at[lax.rem(z + RING - step, RING)], f_send.at[step - 1], f_recv.at[step - 1], up
        )

    def columns(j):
        return pl.ds(pl.multiple_of(j * COLS, COLS), COLS)

    def slot(which, first, count):
        return pl.ds(pl.multiple_of(which * band + first, half), count)

    def own_grad(j):
        return pltpu.make_async_copy(g.at[:, columns(j)], gbuf.at[j, slot(z, 0, band)], g_own.at[j])

    def direct(j, side):
        ref = gbuf.at[j, slot(z, 0, band)]
        return remote(ref, ref, d_send.at[j, side], d_recv.at[j, side], up if side == 0 else down)

    def direct_in(j, side):
        ref = gbuf.at[j, slot(z_down if side == 0 else z_up, 0, band)]
        return remote(ref, ref, d_send.at[j, side], d_recv.at[j, side], up)

    def forward(j, side):
        ref = gbuf.at[j, slot(z_down if side == 0 else z_up, side * half, half)]
        return remote(ref, ref, r_send.at[j, side], r_recv.at[j, side], up if side == 0 else down)

    def forward_in(j, side):
        ref = gbuf.at[j, slot(lax.rem(z + 2, RING), side * half, half)]
        return remote(ref, ref, r_send.at[j, side], r_recv.at[j, side], up)

    def err_in(j):
        return pltpu.make_async_copy(err.at[:, columns(j)], total.at[j], e_in.at[j])

    def mem_out(j):
        return pltpu.make_async_copy(total.at[j], memory.at[:, columns(j)], out_sem.at[j])

    def far(j, side, group):
        some = pl.ds(group * 3, 3)
        return remote(
            part.at[j, x_far, side, some], relay.at[j, side, some], a_send.at[j, side, group],
            a_recv.at[j, side, group], right if side == 0 else left,
        )

    def near(j, side, group):
        some = pl.ds(group * 3, 3)
        return remote(
            part.at[j, x_right if side == 0 else x_left, :, some], piece.at[j, side, :, some],
            b_send.at[j, side, group], b_recv.at[j, side, group], right if side == 0 else left,
        )

    def q_out(step):
        return remote(q_taps, q_near.at[:, x], q_send.at[step - 1], q_recv.at[step - 1], sp_at(x + step, z))

    def q_in(step):
        source = lax.rem(x + RING - step, RING)
        return remote(q_taps, q_near.at[:, source], q_send.at[step - 1], q_recv.at[step - 1], right)

    def t_out(step):
        return remote(
            t_term.at[lax.rem(z + step, RING)], t_near.at[step - 1], t_send.at[step - 1], t_recv.at[step - 1],
            sp_at(x, z + step),
        )

    def p_scatter(d):
        return remote(p_src.at[lax.rem(sp + d, count_sp)], p_near.at[d - 1], s1.at[d - 1], r1.at[d - 1], at_sp(d))

    def p_share(d):
        return remote(p_one, p_far.at[rep], s2.at[d - 1], r2.at[d - 1], at_rep(d))

    def p_share_in(d):
        source = lax.rem(rep + count_rep - d, count_rep)
        return remote(p_one, p_far.at[source], s2.at[d - 1], r2.at[d - 1], at_rep(d))

    def p_gather(d):
        return remote(p_all.at[sp], p_all.at[sp], s3.at[d - 1], r3.at[d - 1], at_sp(d))

    def p_gather_in(d):
        ref = p_all.at[lax.rem(sp + count_sp - d, count_sp)]
        return remote(ref, ref, s3.at[d - 1], r3.at[d - 1], at_sp(d))

    def q_scatter(d):
        return remote(q_src.at[lax.rem(rep + d, count_rep)], q_got.at[d - 1], s4.at[d - 1], r4.at[d - 1], at_rep(d))

    def q_gather(d):
        return remote(q_next.at[rep], q_next.at[rep], s5.at[d - 1], r5.at[d - 1], at_rep(d))

    def q_gather_in(d):
        ref = q_next.at[lax.rem(rep + count_rep - d, count_rep)]
        return remote(ref, ref, s5.at[d - 1], r5.at[d - 1], at_rep(d))

    barrier = pltpu.get_barrier_semaphore()
    for d in range(1, count_sp):
        pl.semaphore_signal(barrier, inc=1, device_id=at_sp(d), device_id_type=MESH)
    for d in range(1, count_rep):
        pl.semaphore_signal(barrier, inc=1, device_id=at_rep(d), device_id_type=MESH)

    def column_in(i):
        return pltpu.make_async_copy(frames.at[:, columns(i)], local.at[i], l_in.at[i])

    pairs = frames.shape[1] // COLS
    owners = COLS // share
    own_grad(0).start()
    for i in range(pairs):
        column_in(i).start()
    pl.semaphore_wait(barrier, count_sp + count_rep - 2)
    own_grad(0).wait()
    direct(0, 0).start()
    direct(0, 1).start()

    per_x = RING // owners
    for first in range(per_x):
        for i in range(first, pairs, per_x):
            column_in(i).wait()
            turned = local[i].T
            for k in range(owners):
                owner = i * owners + k
                flipped[owner // RING, owner % RING] = turned[k * share : (k + 1) * share]
        for target in range(first * owners, (first + 1) * owners):
            away = lax.rem(target - z + RING, RING)

            @pl.when(away != 0)
            def _(away=away):
                frames_out(away).start()
    own_frames = pltpu.make_async_copy(flipped.at[:, z], raw.at[z], f_own)
    own_frames.start()
    for j in range(CHUNKS):
        err_in(j).start()
    for j in range(1, CHUNKS):
        own_grad(j).start()

    thirds = [third.astype(jnp.float32) for third in split(q_own[...])]
    lanes = q_taps.shape[2]
    thirds.append(jnp.zeros((lanes - 3 * rank, q_own.shape[1]), jnp.float32))
    q_turned[...] = jnp.concatenate(thirds, axis=0).T
    for tap in range(TAPS):
        q_taps[tap] = q_turned[pl.ds(tap, share, stride=TAPS), :].astype(jnp.bfloat16)
    for step in (1, 3, 2):
        q_out(step).start()
    own_q = pltpu.make_async_copy(q_taps, q_near.at[:, x], q_copy)
    own_q.start()

    lane = lax.broadcasted_iota(jnp.int32, (RING * share, width), 1)

    def place(row, value):
        at = pl.ds(pl.multiple_of(row * width, width), width)
        wide = value.astype(jnp.float32)
        taps[0, :, at] = jnp.where(lane == 0, 0.0, pltpu.roll(wide, 1, 1)).astype(taps.dtype)
        taps[1, :, at] = value
        taps[2, :, at] = jnp.where(lane == width - 1, 0.0, pltpu.roll(wide, width - 1, 1)).astype(taps.dtype)

    def place_band(which):
        def place_row(row, carry):
            at = pl.ds(pl.multiple_of(row * width, width), width)
            place(which * (band // width) + row + 1, raw[which, :, :, at].reshape(RING * share, width))
            return carry

        lax.fori_loop(0, band // width, place_row, 0)

    def start_forward(j):
        for side in range(2):
            direct_in(j, side).wait_recv()
            forward(j, side).start()

    def start_direct(j):
        for side in range(2):
            direct(j, side).start()

    own_frames.wait()
    place_band(z)
    start_forward(0)
    for j in range(1, CHUNKS):
        own_grad(j).wait()

    for j in range(CHUNKS):
        err_in(j).wait()
        term = exact_dot(q_own[...], total[j], ((1,), (0,)))
        for h in range(2):
            p_src[2 * j + h] = term[h * (rank // 2) : (h + 1) * (rank // 2)]

    frames_in(1).wait_recv()
    frames_in(3).wait_recv()
    start_direct(1)
    place_band(z_down)
    place_band(z_up)
    frames_in(2).wait_recv()

    bottom = raw.at[RING - 1, :, :, band - width : band]
    above = remote(bottom, halo.at[0], h_send.at[0], h_recv.at[0], right)
    below = remote(raw.at[0, :, :, 0:width], halo.at[1], h_send.at[1], h_recv.at[1], left)
    above.start()
    below.start()
    place_band(lax.rem(z + 2, RING))
    rows = RING * band // width
    above.wait()
    below.wait()
    zero = jnp.zeros((RING * share, width), halo.dtype)
    place(0, jnp.where(x == 0, zero, halo[0].reshape(RING * share, width)))
    place(rows + 1, jnp.where(x == RING - 1, zero, halo[1].reshape(RING * share, width)))

    def t_band(which):
        acc = None
        for a in range(3):
            at = pl.ds(pl.multiple_of(which * band + a * width, width), band)
            stacked = taps[:, :, at].reshape(3 * RING * share, band)
            term = jnp.dot(q_flip[a], stacked, preferred_element_type=jnp.float32)
            acc = term if acc is None else acc + term
        t_term[which] = acc[:rank] + (acc[rank : 2 * rank] + acc[2 * rank : 3 * rank])

    def t_start():
        own_q.wait()
        for step in (1, 3, 2):
            q_in(step).wait_recv()
        for a in range(3):
            q_flip[a] = q_near[3 * a : 3 * a + 3].reshape(3 * RING * share, lanes).T

    def t_bands(first):
        def one(i, carry):
            t_band(first + i)
            return carry

        lax.fori_loop(0, RING // 2, one, 0)

    def t_finish():
        for step in (1, 3, 2):
            t_out(step).start()

    def p_terms():
        for step in (1, 3, 2):
            t_out(step).wait_recv()
        full = t_term[z] + (t_near[0] + t_near[1] + t_near[2])
        parts = jnp.concatenate(split(full), axis=0)

        def add(j, carry):
            acc = jnp.dot(parts, gbuf[j, slot(z, 0, band)], preferred_element_type=jnp.float32)
            term = acc[:rank] + (acc[rank : 2 * rank] + acc[2 * rank :])
            for h in range(2):
                p_src[2 * j + h] = p_src[2 * j + h] + term[h * (rank // 2) : (h + 1) * (rank // 2)]
            return carry

        lax.fori_loop(0, CHUNKS, add, 0)
        for d in range(1, count_sp):
            p_scatter(d).start()

    def p_sum_sp():
        acc = p_src[sp]
        for d in range(1, count_sp):
            p_scatter(d).wait_recv()
            acc = acc + p_near[d - 1]
        p_one[...] = acc
        p_far[rep] = acc
        for d in range(1, count_rep):
            p_share(d).start()

    def p_sum_rep():
        for d in range(1, count_rep):
            p_share_in(d).wait_recv()
        acc = p_far[0]
        for i in range(1, count_rep):
            acc = acc + p_far[i]
        p_all[sp] = acc
        for d in range(1, count_sp):
            p_gather(d).start()

    def p_chunk(j):
        return jnp.concatenate([p_all[2 * j], p_all[2 * j + 1]], axis=0)

    def orthogonal():
        for d in range(1, count_sp):
            p_gather_in(d).wait_recv()
        p_total = jnp.concatenate([p_chunk(j) for j in range(CHUNKS)], axis=1)
        gram = exact_dot(p_total, p_total, ((1,), (1,)))
        row_at = lax.broadcasted_iota(jnp.int32, (rank, rank), 0)
        col_at = lax.broadcasted_iota(jnp.int32, (rank, rank), 1)
        work[:, :rank] = gram
        work[:, rank : 2 * rank] = jnp.where(row_at == col_at, 1.0, 0.0)
        shape = (rank, 2 * rank)
        line = lax.broadcasted_iota(jnp.int32, shape, 0)
        spot = lax.broadcasted_iota(jnp.int32, shape, 1)

        def eliminate(k, carry):
            state = work[:, : 2 * rank]
            pivot = work[pl.ds(k, 1), : 2 * rank]
            column = jnp.sum(jnp.where(spot == k, state, 0.0), axis=1, keepdims=True)
            diagonal = jnp.sum(jnp.where(spot[:1] == k, pivot, 0.0), axis=1, keepdims=True)
            inverse = 1.0 / jnp.sqrt(diagonal)
            pivot = pivot * inverse
            work[:, : 2 * rank] = jnp.where(
                line > k, state - (column * inverse) * pivot, jnp.where(line == k, pivot, state)
            )
            return carry

        lax.fori_loop(0, rank, eliminate, 0)
        lower_inverse = jnp.where(col_at <= row_at, work[:, rank : 2 * rank], 0.0)
        whole = exact_dot(lower_inverse, p_total, ((1,), (0,)))
        for j in range(CHUNKS):
            p_ortho[j] = whole[:, j * COLS : (j + 1) * COLS]
        q_sum[...] = jnp.zeros_like(q_sum)

    def add_q(k):
        m0, m1, m2 = split(total[k])
        p0, p1, p2 = split(p_ortho[k])
        m_side = jnp.concatenate([m0, m0, m0, m1, m1, m2], axis=1)
        p_side = jnp.concatenate([p0, p1, p2, p0, p1, p0], axis=1).T
        q_sum[:, :rank] = q_sum[:, :rank] + jnp.dot(m_side, p_side, preferred_element_type=jnp.float32)

    def multiply(first, count, after):
        depth = gbuf.shape[1]
        per_side = part.shape[4]

        def one(a, carry):
            at = pl.ds(pl.multiple_of(a * width, width), depth)
            stacked = taps[:, :, at].reshape(3 * RING * share, depth)
            chosen = gbuf[first] if count == 1 else jnp.concatenate([gbuf[first], gbuf[first + 1]], axis=1)
            product = jnp.dot(stacked, chosen, preferred_element_type=jnp.float32)
            for c in range(count):
                for b in range(3):
                    for owner in range(RING):
                        for side in range(2):
                            line = b * RING * share + (owner * 2 + side) * per_side
                            part[first + c, owner, side, a * 3 + b] = product[
                                line : line + per_side, c * COLS : (c + 1) * COLS
                            ]
                far(first + c, 0, a).start()
                far(first + c, 1, a).start()

            @pl.when((a == 0) & (after < CHUNKS))
            def _():
                start_forward(after)

            return carry

        lax.fori_loop(0, 3, one, 0)

    def pass_on(k):
        for group in range(3):
            some = pl.ds(group * 3, 3)
            far(k, 0, group).wait_recv()
            part[k, x_right, 0, some] = part[k, x_right, 0, some] + relay[k, 0, some]
            near(k, 0, group).start()
            far(k, 1, group).wait_recv()
            part[k, x_left, 1, some] = part[k, x_left, 1, some] + relay[k, 1, some]
            near(k, 1, group).start()

    def complete(k, with_q):
        for group in range(3):
            near(k, 0, group).wait_recv()
            near(k, 1, group).wait_recv()
        count = part.shape[4]
        for side in range(2):
            for tap in range(TAPS):
                at = pl.ds(side * count * TAPS + tap, count, stride=TAPS)
                total[k, at, :] = (
                    total[k, at, :] + part[k, x, side, tap] + (piece[k, 0, side, tap] + piece[k, 1, side, tap])
                )
        mem_out(k).start()
        pl.when(with_q)(lambda: add_q(k))

    def over(first, count, body):
        def one(i, carry):
            body(first + i)
            return carry

        lax.fori_loop(0, count, one, 0)

    def step(j, carry):
        @pl.when(j + 2 < CHUNKS)
        def _():
            start_direct(j + 2)

        @pl.when(j < CHUNKS)
        def _():
            forward_in(j, 0).wait_recv()
            forward_in(j, 1).wait_recv()

        alone = (j == 0) | (j == CHUNKS - 1)
        even = lax.rem(j, 2) == 0
        pl.when(alone)(lambda: multiply(j, 1, j + 1))
        pl.when((j > 0) & (j < CHUNKS - 1) & even)(lambda: multiply(j - 1, 2, j + 1))
        pl.when((j < CHUNKS - 1) & jnp.logical_not(even))(lambda: start_forward(j + 1))

        pl.when((j == 1) | (j == CHUNKS))(lambda: pass_on(j - 1))
        pl.when((j > 1) & (j < CHUNKS) & jnp.logical_not(even))(lambda: over(j - 2, 2, pass_on))

        @pl.when(j == T_AT)
        def _():
            t_start()
            t_bands(0)
            t_bands(RING // 2)
            t_finish()

        for at, stage in zip(P_AT, (p_terms, p_sum_sp, p_sum_rep, orthogonal)):
            pl.when(j == at)(stage)
        ready = j >= P_AT[-1]

        pl.when((j == 2) | (j == CHUNKS + 1))(lambda: complete(lax.select(j == 2, 0, CHUNKS - 1), ready))
        pl.when((j > 2) & (j <= CHUNKS) & even)(
            lambda: over(j - 3, 2, lambda k: complete(k, ready))
        )
        pl.when(j == P_AT[-1])(lambda: over(0, EARLY, add_q))

        return carry

    lax.fori_loop(0, CHUNKS + 2, step, 0)

    lines = rank // count_rep
    q_lines = q_sum[...].T
    for i in range(count_rep):
        q_src[i] = q_lines[i * lines : (i + 1) * lines]
    for d in range(1, count_rep):
        q_scatter(d).start()
    acc = q_src[rep]
    for d in range(1, count_rep):
        q_scatter(d).wait_recv()
        acc = acc + q_got[d - 1]
    q_next[rep] = acc * (1.0 / count_rep)
    for d in range(1, count_rep):
        q_gather(d).start()
    for d in range(1, count_rep):
        q_gather_in(d).wait_recv()

    def finish(j, carry):
        for side in range(2):
            direct(j, side).wait_send()
            forward(j, side).wait_send()
            for group in range(3):
                far(j, side, group).wait_send()
                near(j, side, group).wait_send()
        mem_out(j).wait()
        return carry

    lax.fori_loop(0, CHUNKS, finish, 0)
    for step_ in (1, 3, 2):
        frames_out(step_).wait_send()
        q_out(step_).wait_send()
        t_out(step_).wait_send()
    for d in range(1, count_sp):
        p_scatter(d).wait_send()
        p_gather(d).wait_send()
    for d in range(1, count_rep):
        p_share(d).wait_send()
        q_scatter(d).wait_send()
        q_gather(d).wait_send()


def compressed_step(count_rep, frames, g, err, q_own):
    band, chans = g.shape
    width = band // 4
    rows = err.shape[0]
    rank = q_own.shape[0]
    count_sp = RING * RING
    share = chans // count_sp
    per_side = share // 2
    dma = pltpu.SemaphoreType.DMA
    two, three = dma((CHUNKS, 2)), dma((CHUNKS, 2, 3))
    f32, bf16 = jnp.float32, jnp.bfloat16
    any_spec, vmem_spec = pl.BlockSpec(memory_space=pl.ANY), pl.BlockSpec(memory_space=pltpu.VMEM)
    p_block = (rank // 2, COLS)
    q_block = (rank // count_rep, rows)
    return pl.pallas_call(
        functools.partial(step_kernel, count_rep),
        out_shape=(
            jax.ShapeDtypeStruct((rows, chans), f32),
            jax.ShapeDtypeStruct((count_rep, *q_block), f32),
            jax.ShapeDtypeStruct((CHUNKS, rank, COLS), f32),
        ),
        in_specs=[any_spec, any_spec, any_spec, vmem_spec],
        out_specs=(any_spec, vmem_spec, vmem_spec),
        scratch_shapes=[
            pltpu.VMEM((chans // COLS, band, COLS), bf16),
            pltpu.VMEM((rows, 128), f32),
            pltpu.VMEM((TAPS, share, 128), bf16),
            pltpu.VMEM((RING, RING, share, band), bf16),
            pltpu.VMEM((RING, RING, share, band), bf16),
            pltpu.VMEM((2, RING, share, width), bf16),
            pltpu.VMEM((3, RING * share, RING * band + 2 * width), bf16),
            pltpu.VMEM((CHUNKS, RING * band, COLS), bf16),
            pltpu.VMEM((CHUNKS, RING, 2, TAPS, per_side, COLS), f32),
            pltpu.VMEM((CHUNKS, 2, TAPS, per_side, COLS), f32),
            pltpu.VMEM((CHUNKS, 2, 2, TAPS, per_side, COLS), f32),
            pltpu.VMEM((CHUNKS, rows, COLS), f32),
            pltpu.VMEM((TAPS, RING, share, 128), bf16),
            pltpu.VMEM((3, 128, 3 * RING * share), bf16),
            pltpu.VMEM((RING, rank, band), f32),
            pltpu.VMEM((RING - 1, rank, band), f32),
            pltpu.VMEM((count_sp, *p_block), f32),
            pltpu.VMEM((count_sp - 1, *p_block), f32),
            pltpu.VMEM(p_block, f32),
            pltpu.VMEM((count_rep, *p_block), f32),
            pltpu.VMEM((count_sp, *p_block), f32),
            pltpu.VMEM((rank, 128), f32),
            pltpu.VMEM((count_rep, *q_block), f32),
            pltpu.VMEM((count_rep - 1, *q_block), f32),
            pltpu.VMEM((rows, 128), f32),
            dma((chans // COLS,)), dma((3,)), dma((3,)), dma, dma((2,)), dma((2,)), dma((CHUNKS,)), dma((CHUNKS,)),
            two, two, two, two, three, three, three, three, dma((CHUNKS,)),
            dma((3,)), dma((3,)), dma, dma((3,)), dma((3,)),
            dma((count_sp - 1,)), dma((count_sp - 1,)), dma((count_rep - 1,)), dma((count_rep - 1,)),
            dma((count_sp - 1,)), dma((count_sp - 1,)), dma((count_rep - 1,)), dma((count_rep - 1,)),
            dma((count_rep - 1,)), dma((count_rep - 1,)),
        ],
        compiler_params=pltpu.CompilerParams(
            collective_id=0, has_side_effects=True, vmem_limit_bytes=58 * 1024 * 1024
        ),
        cost_estimate=pl.CostEstimate(flops=2 * rows * 16 * chans * band, bytes_accessed=10**7, transcendentals=0),
        name="compressed_step",
    )(frames, g, err, q_own)


def feedback_kernel(memory, q_parts, p_ortho, error_next, q_next, q_side):
    count, lines, rows = q_parts.shape

    @pl.when(pl.program_id(0) == 0)
    def _():
        for i in range(count):
            q_next[i * lines : (i + 1) * lines] = q_parts[i]
        q0, q1, q2 = split(q_next[...])
        q_side[...] = jnp.concatenate([q0, q0, q0, q1, q1, q2], axis=0).T

    for i in range(p_ortho.shape[0]):
        p0, p1, p2 = split(p_ortho[i])
        p_side = jnp.concatenate([p0, p1, p2, p0, p1, p0], axis=0)
        at = slice(i * COLS, (i + 1) * COLS)
        error_next[:, at] = memory[:, at] - jnp.dot(q_side[...], p_side, preferred_element_type=jnp.float32)


def feedback(memory, q_parts, p_ortho):
    rows, chans = memory.shape
    count, lines, _ = q_parts.shape
    rank = count * lines
    per_block = 2
    block = (rows, per_block * COLS)
    return pl.pallas_call(
        feedback_kernel,
        grid=(chans // block[1],),
        out_shape=(jax.ShapeDtypeStruct(memory.shape, jnp.float32), jax.ShapeDtypeStruct((rank, rows), jnp.float32)),
        in_specs=[
            pl.BlockSpec(block, lambda i: (0, i)),
            pl.BlockSpec(q_parts.shape, lambda i: (0, 0, 0)),
            pl.BlockSpec((per_block, rank, COLS), lambda i: (i, 0, 0)),
        ],
        out_specs=(pl.BlockSpec(block, lambda i: (0, i)), pl.BlockSpec((rank, rows), lambda i: (0, 0))),
        scratch_shapes=[pltpu.VMEM((rows, 6 * rank), jnp.bfloat16)],
        compiler_params=pltpu.CompilerParams(vmem_limit_bytes=60 * 1024 * 1024),
        name="feedback",
    )(memory, q_parts, p_ortho)


def per_device(count_rep, frames, out_grad, error_prev, q_prev):
    band_rows, width, chans = frames.shape[1:]
    band = band_rows * width
    memory, q_parts, p_ortho = compressed_step(
        count_rep,
        frames[0].reshape(band, chans),
        out_grad[0].reshape(band, chans),
        error_prev[0],
        q_prev,
    )
    error_next, q_next = feedback(memory, q_parts, p_ortho)
    return (error_next[None], q_next)


def solution(mesh):
    placed = (
        P("rep", "sp", None, None),
        P("rep", "sp", None, None),
        P("rep", "sp", None),
        P(None, "sp"),
    )
    return jax.shard_map(
        functools.partial(per_device, mesh.shape["rep"]),
        mesh=mesh,
        in_specs=placed,
        out_specs=(P("rep", "sp", None), P(None, "sp")),
        check_vma=False,
    )
```

```python
import functools

import jax
import jax.numpy as jnp
from jax import lax
from jax.experimental import pallas as pl
from jax.experimental.pallas import tpu as pltpu
from jax.sharding import PartitionSpec as P

MESH = pl.DeviceIdType.MESH
RING = 4
CHUNKS = 8
COLS = 128
TAPS = 9
T_AT = 0
P_AT = (2, 4, 5, 7)
EARLY = 5


def sp_at(x, z):
    return {"sp": lax.rem(x + RING, RING) * RING + lax.rem(z + RING, RING)}


def remote(src, dst, send, recv, device):
    return pltpu.make_async_remote_copy(
        src_ref=src, dst_ref=dst, send_sem=send, recv_sem=recv, device_id=device, device_id_type=MESH
    )


def split(value):
    high = value.astype(jnp.bfloat16)
    rest = value - high.astype(jnp.float32)
    middle = rest.astype(jnp.bfloat16)
    low = (rest - middle.astype(jnp.float32)).astype(jnp.bfloat16)
    return high, middle, low


def exact_dot(a, b, contract):
    return lax.dot_general(
        a, b, (contract, ((), ())), precision=lax.Precision.HIGHEST, preferred_element_type=jnp.float32
    )


def step_kernel(
    count_rep, frames, g, err, q_own, memory, q_next, p_ortho,
    local, f_relay, t_relay, q_turned, q_taps, flipped, raw, halo, taps, gbuf, part, relay, piece, total,
    q_near, q_flip, t_term, t_near, p_src, p_near, p_one, p_far, p_all, work, q_src, q_got, q_sum,
    l_in, f_send, f_recv, f_own, h_send, h_recv, e_in, g_own,
    d_send, d_recv, r_send, r_recv, a_send, a_recv, b_send, b_recv, out_sem,
    q_send, q_recv, q_copy, t_send, t_recv, s1, r1, s2, r2, s3, r3, s4, r4, s5, r5,
):
    sp, rep = lax.axis_index("sp"), lax.axis_index("rep")
    x, z = sp // RING, lax.rem(sp, RING)
    up, down = sp_at(x, z + 1), sp_at(x, z - 1)
    right, left = sp_at(x + 1, z), sp_at(x - 1, z)
    z_up, z_down = lax.rem(z + 1, RING), lax.rem(z + 3, RING)
    x_right, x_left, x_far = lax.rem(x + 1, RING), lax.rem(x + 3, RING), lax.rem(x + 2, RING)
    band = g.shape[0]
    half = band // 2
    count_sp = RING * RING
    share = part.shape[4] * 2
    width = halo.shape[3]
    rank = q_own.shape[0]

    def at_sp(d):
        return {"sp": lax.rem(sp + d, count_sp)}

    def at_rep(d):
        return {"rep": lax.rem(rep + d, count_rep)}

    near_z, far_z = (z_up, z_down), lax.rem(z + 2, RING)
    towards = (up, down)
    some_x = RING // 2

    def frames_near(side):
        return remote(flipped.at[:, near_z[side]], raw.at[z], f_send.at[side], f_recv.at[side], towards[side])

    def frames_near_in(side):
        return remote(flipped.at[:, z], raw.at[near_z[1 - side]], f_send.at[side], f_recv.at[side], up)

    def frames_far(side):
        part_x = pl.ds(side * some_x, some_x)
        return remote(
            flipped.at[part_x, far_z], f_relay.at[side], f_send.at[2 + side], f_recv.at[2 + side], towards[side]
        )

    def frames_on(side):
        part_x = pl.ds(side * some_x, some_x)
        return remote(
            f_relay.at[side], raw.at[near_z[1 - side], part_x], f_send.at[4 + side], f_recv.at[4 + side], towards[side]
        )

    def frames_far_in(side):
        part_x = pl.ds(side * some_x, some_x)
        return remote(f_relay.at[side], raw.at[far_z, part_x], f_send.at[4 + side], f_recv.at[4 + side], up)

    def columns(j):
        return pl.ds(pl.multiple_of(j * COLS, COLS), COLS)

    def slot(which, first, count):
        return pl.ds(pl.multiple_of(which * band + first, half), count)

    def own_grad(j):
        return pltpu.make_async_copy(g.at[:, columns(j)], gbuf.at[j, slot(z, 0, band)], g_own.at[j])

    def direct(j, side):
        ref = gbuf.at[j, slot(z, 0, band)]
        return remote(ref, ref, d_send.at[j, side], d_recv.at[j, side], up if side == 0 else down)

    def direct_in(j, side):
        ref = gbuf.at[j, slot(z_down if side == 0 else z_up, 0, band)]
        return remote(ref, ref, d_send.at[j, side], d_recv.at[j, side], up)

    def forward(j, side):
        ref = gbuf.at[j, slot(z_down if side == 0 else z_up, side * half, half)]
        return remote(ref, ref, r_send.at[j, side], r_recv.at[j, side], up if side == 0 else down)

    def forward_in(j, side):
        ref = gbuf.at[j, slot(lax.rem(z + 2, RING), side * half, half)]
        return remote(ref, ref, r_send.at[j, side], r_recv.at[j, side], up)

    def err_in(j):
        return pltpu.make_async_copy(err.at[:, columns(j)], total.at[j], e_in.at[j])

    def mem_out(j):
        return pltpu.make_async_copy(total.at[j], memory.at[:, columns(j)], out_sem.at[j])

    def far(j, side, group):
        some = pl.ds(group * 3, 3)
        return remote(
            part.at[j, x_far, side, some], relay.at[j, side, some], a_send.at[j, side, group],
            a_recv.at[j, side, group], right if side == 0 else left,
        )

    def near(j, side, group):
        some = pl.ds(group * 3, 3)
        return remote(
            part.at[j, x_right if side == 0 else x_left, :, some], piece.at[j, side, :, some],
            b_send.at[j, side, group], b_recv.at[j, side, group], right if side == 0 else left,
        )

    def q_out(step):
        return remote(q_taps, q_near.at[:, x], q_send.at[step - 1], q_recv.at[step - 1], sp_at(x + step, z))

    def q_in(step):
        source = lax.rem(x + RING - step, RING)
        return remote(q_taps, q_near.at[:, source], q_send.at[step - 1], q_recv.at[step - 1], right)

    def t_far(side):
        some = pl.ds(side * (rank // 2), rank // 2)
        return remote(t_term.at[far_z, some], t_relay.at[side], t_send.at[side], t_recv.at[side], towards[side])

    def t_out(side):
        return remote(
            t_term.at[near_z[side]], t_near.at[side], t_send.at[2 + side], t_recv.at[2 + side], towards[side]
        )

    def p_scatter(d):
        return remote(p_src.at[lax.rem(sp + d, count_sp)], p_near.at[d - 1], s1.at[d - 1], r1.at[d - 1], at_sp(d))

    def p_share(d):
        return remote(p_one, p_far.at[rep], s2.at[d - 1], r2.at[d - 1], at_rep(d))

    def p_share_in(d):
        source = lax.rem(rep + count_rep - d, count_rep)
        return remote(p_one, p_far.at[source], s2.at[d - 1], r2.at[d - 1], at_rep(d))

    def p_gather(d):
        return remote(p_all.at[sp], p_all.at[sp], s3.at[d - 1], r3.at[d - 1], at_sp(d))

    def p_gather_in(d):
        ref = p_all.at[lax.rem(sp + count_sp - d, count_sp)]
        return remote(ref, ref, s3.at[d - 1], r3.at[d - 1], at_sp(d))

    def q_scatter(d):
        return remote(q_src.at[lax.rem(rep + d, count_rep)], q_got.at[d - 1], s4.at[d - 1], r4.at[d - 1], at_rep(d))

    def q_gather(d):
        return remote(q_next.at[rep], q_next.at[rep], s5.at[d - 1], r5.at[d - 1], at_rep(d))

    def q_gather_in(d):
        ref = q_next.at[lax.rem(rep + count_rep - d, count_rep)]
        return remote(ref, ref, s5.at[d - 1], r5.at[d - 1], at_rep(d))

    barrier = pltpu.get_barrier_semaphore()
    for d in range(1, count_sp):
        pl.semaphore_signal(barrier, inc=1, device_id=at_sp(d), device_id_type=MESH)
    for d in range(1, count_rep):
        pl.semaphore_signal(barrier, inc=1, device_id=at_rep(d), device_id_type=MESH)

    def column_in(i):
        return pltpu.make_async_copy(frames.at[:, columns(i)], local.at[i], l_in.at[i])

    pairs = frames.shape[1] // COLS
    owners = COLS // share
    own_grad(0).start()
    for i in range(pairs):
        column_in(i).start()
    pl.semaphore_wait(barrier, count_sp + count_rep - 2)
    own_grad(0).wait()
    direct(0, 0).start()
    direct(0, 1).start()

    per_x = RING // owners
    for first in range(per_x):
        for i in range(first, pairs, per_x):
            column_in(i).wait()
            turned = local[i].T
            for k in range(owners):
                owner = i * owners + k
                flipped[owner // RING, owner % RING] = turned[k * share : (k + 1) * share]
    for side in range(2):
        frames_far(side).start()
    for side in range(2):
        frames_near(side).start()
    own_frames = pltpu.make_async_copy(flipped.at[:, z], raw.at[z], f_own)
    own_frames.start()
    for j in range(CHUNKS):
        err_in(j).start()
    for j in range(1, CHUNKS):
        own_grad(j).start()

    thirds = [third.astype(jnp.float32) for third in split(q_own[...])]
    lanes = q_taps.shape[2]
    thirds.append(jnp.zeros((lanes - 3 * rank, q_own.shape[1]), jnp.float32))
    q_turned[...] = jnp.concatenate(thirds, axis=0).T
    for tap in range(TAPS):
        q_taps[tap] = q_turned[pl.ds(tap, share, stride=TAPS), :].astype(jnp.bfloat16)
    for step in (1, 3, 2):
        q_out(step).start()
    own_q = pltpu.make_async_copy(q_taps, q_near.at[:, x], q_copy)
    own_q.start()

    lane = lax.broadcasted_iota(jnp.int32, (RING * share, width), 1)

    def place(row, value):
        at = pl.ds(pl.multiple_of(row * width, width), width)
        wide = value.astype(jnp.float32)
        taps[0, :, at] = jnp.where(lane == 0, 0.0, pltpu.roll(wide, 1, 1)).astype(taps.dtype)
        taps[1, :, at] = value
        taps[2, :, at] = jnp.where(lane == width - 1, 0.0, pltpu.roll(wide, width - 1, 1)).astype(taps.dtype)

    def place_band(which):
        def place_row(row, carry):
            at = pl.ds(pl.multiple_of(row * width, width), width)
            place(which * (band // width) + row + 1, raw[which, :, :, at].reshape(RING * share, width))
            return carry

        lax.fori_loop(0, band // width, place_row, 0)

    def start_forward(j):
        for side in range(2):
            direct_in(j, side).wait_recv()
            forward(j, side).start()

    def start_direct(j):
        for side in range(2):
            direct(j, side).start()

    own_frames.wait()
    place_band(z)
    start_forward(0)
    for j in range(1, CHUNKS):
        own_grad(j).wait()

    for j in range(CHUNKS):
        err_in(j).wait()
        term = exact_dot(q_own[...], total[j], ((1,), (0,)))
        for h in range(2):
            p_src[2 * j + h] = term[h * (rank // 2) : (h + 1) * (rank // 2)]

    for side in range(2):
        frames_far(side).wait_recv()
        frames_on(side).start()
    for side in range(2):
        frames_near_in(side).wait_recv()
    start_direct(1)
    place_band(z_down)
    place_band(z_up)
    for side in range(2):
        frames_far_in(side).wait_recv()

    bottom = raw.at[RING - 1, :, :, band - width : band]
    above = remote(bottom, halo.at[0], h_send.at[0], h_recv.at[0], right)
    below = remote(raw.at[0, :, :, 0:width], halo.at[1], h_send.at[1], h_recv.at[1], left)
    above.start()
    below.start()
    place_band(lax.rem(z + 2, RING))
    rows = RING * band // width
    above.wait()
    below.wait()
    zero = jnp.zeros((RING * share, width), halo.dtype)
    place(0, jnp.where(x == 0, zero, halo[0].reshape(RING * share, width)))
    place(rows + 1, jnp.where(x == RING - 1, zero, halo[1].reshape(RING * share, width)))

    def t_band(which):
        acc = None
        for a in range(3):
            at = pl.ds(pl.multiple_of(which * band + a * width, width), band)
            stacked = taps[:, :, at].reshape(3 * RING * share, band)
            term = jnp.dot(q_flip[a], stacked, preferred_element_type=jnp.float32)
            acc = term if acc is None else acc + term
        t_term[which] = acc[:rank] + (acc[rank : 2 * rank] + acc[2 * rank : 3 * rank])

    def t_start():
        own_q.wait()
        for step in (1, 3, 2):
            q_in(step).wait_recv()
        for a in range(3):
            q_flip[a] = q_near[3 * a : 3 * a + 3].reshape(3 * RING * share, lanes).T

    def t_bands(first):
        def one(i, carry):
            t_band(first + i)
            return carry

        lax.fori_loop(0, RING // 2, one, 0)

    def t_finish():
        for side in range(2):
            t_far(side).start()

    def t_pass_on():
        for side in range(2):
            some = pl.ds(side * (rank // 2), rank // 2)
            t_far(side).wait_recv()
            t_term[near_z[side], some] = t_term[near_z[side], some] + t_relay[side]
            t_out(side).start()

    def p_terms():
        for side in range(2):
            t_out(side).wait_recv()
        full = t_term[z] + (t_near[0] + t_near[1])
        parts = jnp.concatenate(split(full), axis=0)

        def add(j, carry):
            acc = jnp.dot(parts, gbuf[j, slot(z, 0, band)], preferred_element_type=jnp.float32)
            term = acc[:rank] + (acc[rank : 2 * rank] + acc[2 * rank :])
            for h in range(2):
                p_src[2 * j + h] = p_src[2 * j + h] + term[h * (rank // 2) : (h + 1) * (rank // 2)]
            return carry

        lax.fori_loop(0, CHUNKS, add, 0)
        for d in range(1, count_sp):
            p_scatter(d).start()

    def p_sum_sp():
        acc = p_src[sp]
        for d in range(1, count_sp):
            p_scatter(d).wait_recv()
            acc = acc + p_near[d - 1]
        p_one[...] = acc
        p_far[rep] = acc
        for d in range(1, count_rep):
            p_share(d).start()

    def p_sum_rep():
        for d in range(1, count_rep):
            p_share_in(d).wait_recv()
        acc = p_far[0]
        for i in range(1, count_rep):
            acc = acc + p_far[i]
        p_all[sp] = acc
        for d in range(1, count_sp):
            p_gather(d).start()

    def p_chunk(j):
        return jnp.concatenate([p_all[2 * j], p_all[2 * j + 1]], axis=0)

    def orthogonal():
        for d in range(1, count_sp):
            p_gather_in(d).wait_recv()
        p_total = jnp.concatenate([p_chunk(j) for j in range(CHUNKS)], axis=1)
        gram = exact_dot(p_total, p_total, ((1,), (1,)))
        row_at = lax.broadcasted_iota(jnp.int32, (rank, rank), 0)
        col_at = lax.broadcasted_iota(jnp.int32, (rank, rank), 1)
        work[:, :rank] = gram
        work[:, rank : 2 * rank] = jnp.where(row_at == col_at, 1.0, 0.0)
        shape = (rank, 2 * rank)
        line = lax.broadcasted_iota(jnp.int32, shape, 0)
        spot = lax.broadcasted_iota(jnp.int32, shape, 1)

        def eliminate(k, carry):
            state = work[:, : 2 * rank]
            pivot = work[pl.ds(k, 1), : 2 * rank]
            column = jnp.sum(jnp.where(spot == k, state, 0.0), axis=1, keepdims=True)
            diagonal = jnp.sum(jnp.where(spot[:1] == k, pivot, 0.0), axis=1, keepdims=True)
            inverse = 1.0 / jnp.sqrt(diagonal)
            pivot = pivot * inverse
            work[:, : 2 * rank] = jnp.where(
                line > k, state - (column * inverse) * pivot, jnp.where(line == k, pivot, state)
            )
            return carry

        lax.fori_loop(0, rank, eliminate, 0)
        lower_inverse = jnp.where(col_at <= row_at, work[:, rank : 2 * rank], 0.0)
        whole = exact_dot(lower_inverse, p_total, ((1,), (0,)))
        for j in range(CHUNKS):
            p_ortho[j] = whole[:, j * COLS : (j + 1) * COLS]
        q_sum[...] = jnp.zeros_like(q_sum)

    def add_q(k):
        m0, m1, m2 = split(total[k])
        p0, p1, p2 = split(p_ortho[k])
        m_side = jnp.concatenate([m0, m0, m0, m1, m1, m2], axis=1)
        p_side = jnp.concatenate([p0, p1, p2, p0, p1, p0], axis=1).T
        q_sum[:, :rank] = q_sum[:, :rank] + jnp.dot(m_side, p_side, preferred_element_type=jnp.float32)

    def multiply(first, count, after):
        depth = gbuf.shape[1]
        per_side = part.shape[4]

        def one(a, carry):
            at = pl.ds(pl.multiple_of(a * width, width), depth)
            stacked = taps[:, :, at].reshape(3 * RING * share, depth)
            chosen = gbuf[first] if count == 1 else jnp.concatenate([gbuf[first], gbuf[first + 1]], axis=1)
            product = jnp.dot(stacked, chosen, preferred_element_type=jnp.float32)
            for c in range(count):
                for b in range(3):
                    for owner in range(RING):
                        for side in range(2):
                            line = b * RING * share + (owner * 2 + side) * per_side
                            part[first + c, owner, side, a * 3 + b] = product[
                                line : line + per_side, c * COLS : (c + 1) * COLS
                            ]
                far(first + c, 0, a).start()
                far(first + c, 1, a).start()

            @pl.when((a == 0) & (after < CHUNKS))
            def _():
                start_forward(after)

            return carry

        lax.fori_loop(0, 3, one, 0)

    def pass_on(k):
        for group in range(3):
            some = pl.ds(group * 3, 3)
            far(k, 0, group).wait_recv()
            part[k, x_right, 0, some] = part[k, x_right, 0, some] + relay[k, 0, some]
            near(k, 0, group).start()
            far(k, 1, group).wait_recv()
            part[k, x_left, 1, some] = part[k, x_left, 1, some] + relay[k, 1, some]
            near(k, 1, group).start()

    def complete(k, with_q):
        for group in range(3):
            near(k, 0, group).wait_recv()
            near(k, 1, group).wait_recv()
        count = part.shape[4]
        for side in range(2):
            for tap in range(TAPS):
                at = pl.ds(side * count * TAPS + tap, count, stride=TAPS)
                total[k, at, :] = (
                    total[k, at, :] + part[k, x, side, tap] + (piece[k, 0, side, tap] + piece[k, 1, side, tap])
                )
        mem_out(k).start()
        pl.when(with_q)(lambda: add_q(k))

    def over(first, count, body):
        def one(i, carry):
            body(first + i)
            return carry

        lax.fori_loop(0, count, one, 0)

    def step(j, carry):
        @pl.when(j + 2 < CHUNKS)
        def _():
            start_direct(j + 2)

        @pl.when(j < CHUNKS)
        def _():
            forward_in(j, 0).wait_recv()
            forward_in(j, 1).wait_recv()

        alone = (j == 0) | (j == CHUNKS - 1)
        even = lax.rem(j, 2) == 0
        pl.when(alone)(lambda: multiply(j, 1, j + 1))
        pl.when((j > 0) & (j < CHUNKS - 1) & even)(lambda: multiply(j - 1, 2, j + 1))
        pl.when((j < CHUNKS - 1) & jnp.logical_not(even))(lambda: start_forward(j + 1))

        pl.when((j == 1) | (j == CHUNKS))(lambda: pass_on(j - 1))
        pl.when((j > 1) & (j < CHUNKS) & jnp.logical_not(even))(lambda: over(j - 2, 2, pass_on))

        @pl.when(j == T_AT)
        def _():
            t_start()
            t_bands(0)
            t_bands(RING // 2)
            t_finish()

        pl.when(j == T_AT + 1)(t_pass_on)
        for at, stage in zip(P_AT, (p_terms, p_sum_sp, p_sum_rep, orthogonal)):
            pl.when(j == at)(stage)
        ready = j >= P_AT[-1]

        pl.when((j == 2) | (j == CHUNKS + 1))(lambda: complete(lax.select(j == 2, 0, CHUNKS - 1), ready))
        pl.when((j > 2) & (j <= CHUNKS) & even)(
            lambda: over(j - 3, 2, lambda k: complete(k, ready))
        )
        pl.when(j == P_AT[-1])(lambda: over(0, EARLY, add_q))

        return carry

    lax.fori_loop(0, CHUNKS + 2, step, 0)

    lines = rank // count_rep
    q_lines = q_sum[...].T
    for i in range(count_rep):
        q_src[i] = q_lines[i * lines : (i + 1) * lines]
    for d in range(1, count_rep):
        q_scatter(d).start()
    acc = q_src[rep]
    for d in range(1, count_rep):
        q_scatter(d).wait_recv()
        acc = acc + q_got[d - 1]
    q_next[rep] = acc * (1.0 / count_rep)
    for d in range(1, count_rep):
        q_gather(d).start()
    for d in range(1, count_rep):
        q_gather_in(d).wait_recv()

    def finish(j, carry):
        for side in range(2):
            direct(j, side).wait_send()
            forward(j, side).wait_send()
            for group in range(3):
                far(j, side, group).wait_send()
                near(j, side, group).wait_send()
        mem_out(j).wait()
        return carry

    lax.fori_loop(0, CHUNKS, finish, 0)
    for side in range(2):
        frames_near(side).wait_send()
        frames_far(side).wait_send()
        frames_on(side).wait_send()
        t_far(side).wait_send()
        t_out(side).wait_send()
    for step_ in (1, 3, 2):
        q_out(step_).wait_send()
    for d in range(1, count_sp):
        p_scatter(d).wait_send()
        p_gather(d).wait_send()
    for d in range(1, count_rep):
        p_share(d).wait_send()
        q_scatter(d).wait_send()
        q_gather(d).wait_send()


def compressed_step(count_rep, frames, g, err, q_own):
    band, chans = g.shape
    width = band // 4
    rows = err.shape[0]
    rank = q_own.shape[0]
    count_sp = RING * RING
    share = chans // count_sp
    per_side = share // 2
    dma = pltpu.SemaphoreType.DMA
    two, three = dma((CHUNKS, 2)), dma((CHUNKS, 2, 3))
    f32, bf16 = jnp.float32, jnp.bfloat16
    any_spec, vmem_spec = pl.BlockSpec(memory_space=pl.ANY), pl.BlockSpec(memory_space=pltpu.VMEM)
    p_block = (rank // 2, COLS)
    q_block = (rank // count_rep, rows)
    return pl.pallas_call(
        functools.partial(step_kernel, count_rep),
        out_shape=(
            jax.ShapeDtypeStruct((rows, chans), f32),
            jax.ShapeDtypeStruct((count_rep, *q_block), f32),
            jax.ShapeDtypeStruct((CHUNKS, rank, COLS), f32),
        ),
        in_specs=[any_spec, any_spec, any_spec, vmem_spec],
        out_specs=(any_spec, vmem_spec, vmem_spec),
        scratch_shapes=[
            pltpu.VMEM((chans // COLS, band, COLS), bf16),
            pltpu.VMEM((2, RING // 2, share, band), bf16),
            pltpu.VMEM((2, rank // 2, band), f32),
            pltpu.VMEM((rows, 128), f32),
            pltpu.VMEM((TAPS, share, 128), bf16),
            pltpu.VMEM((RING, RING, share, band), bf16),
            pltpu.VMEM((RING, RING, share, band), bf16),
            pltpu.VMEM((2, RING, share, width), bf16),
            pltpu.VMEM((3, RING * share, RING * band + 2 * width), bf16),
            pltpu.VMEM((CHUNKS, RING * band, COLS), bf16),
            pltpu.VMEM((CHUNKS, RING, 2, TAPS, per_side, COLS), f32),
            pltpu.VMEM((CHUNKS, 2, TAPS, per_side, COLS), f32),
            pltpu.VMEM((CHUNKS, 2, 2, TAPS, per_side, COLS), f32),
            pltpu.VMEM((CHUNKS, rows, COLS), f32),
            pltpu.VMEM((TAPS, RING, share, 128), bf16),
            pltpu.VMEM((3, 128, 3 * RING * share), bf16),
            pltpu.VMEM((RING, rank, band), f32),
            pltpu.VMEM((2, rank, band), f32),
            pltpu.VMEM((count_sp, *p_block), f32),
            pltpu.VMEM((count_sp - 1, *p_block), f32),
            pltpu.VMEM(p_block, f32),
            pltpu.VMEM((count_rep, *p_block), f32),
            pltpu.VMEM((count_sp, *p_block), f32),
            pltpu.VMEM((rank, 128), f32),
            pltpu.VMEM((count_rep, *q_block), f32),
            pltpu.VMEM((count_rep - 1, *q_block), f32),
            pltpu.VMEM((rows, 128), f32),
            dma((chans // COLS,)), dma((6,)), dma((6,)), dma, dma((2,)), dma((2,)), dma((CHUNKS,)), dma((CHUNKS,)),
            two, two, two, two, three, three, three, three, dma((CHUNKS,)),
            dma((3,)), dma((3,)), dma, dma((4,)), dma((4,)),
            dma((count_sp - 1,)), dma((count_sp - 1,)), dma((count_rep - 1,)), dma((count_rep - 1,)),
            dma((count_sp - 1,)), dma((count_sp - 1,)), dma((count_rep - 1,)), dma((count_rep - 1,)),
            dma((count_rep - 1,)), dma((count_rep - 1,)),
        ],
        compiler_params=pltpu.CompilerParams(
            collective_id=0, has_side_effects=True, vmem_limit_bytes=58 * 1024 * 1024
        ),
        cost_estimate=pl.CostEstimate(flops=2 * rows * 16 * chans * band, bytes_accessed=10**7, transcendentals=0),
        name="compressed_step",
    )(frames, g, err, q_own)


def feedback_kernel(memory, q_parts, p_ortho, error_next, q_next, q_side):
    count, lines, rows = q_parts.shape

    @pl.when(pl.program_id(0) == 0)
    def _():
        for i in range(count):
            q_next[i * lines : (i + 1) * lines] = q_parts[i]
        q0, q1, q2 = split(q_next[...])
        q_side[...] = jnp.concatenate([q0, q0, q0, q1, q1, q2], axis=0).T

    for i in range(p_ortho.shape[0]):
        p0, p1, p2 = split(p_ortho[i])
        p_side = jnp.concatenate([p0, p1, p2, p0, p1, p0], axis=0)
        at = slice(i * COLS, (i + 1) * COLS)
        error_next[:, at] = memory[:, at] - jnp.dot(q_side[...], p_side, preferred_element_type=jnp.float32)


def feedback(memory, q_parts, p_ortho):
    rows, chans = memory.shape
    count, lines, _ = q_parts.shape
    rank = count * lines
    per_block = 2
    block = (rows, per_block * COLS)
    return pl.pallas_call(
        feedback_kernel,
        grid=(chans // block[1],),
        out_shape=(jax.ShapeDtypeStruct(memory.shape, jnp.float32), jax.ShapeDtypeStruct((rank, rows), jnp.float32)),
        in_specs=[
            pl.BlockSpec(block, lambda i: (0, i)),
            pl.BlockSpec(q_parts.shape, lambda i: (0, 0, 0)),
            pl.BlockSpec((per_block, rank, COLS), lambda i: (i, 0, 0)),
        ],
        out_specs=(pl.BlockSpec(block, lambda i: (0, i)), pl.BlockSpec((rank, rows), lambda i: (0, 0))),
        scratch_shapes=[pltpu.VMEM((rows, 6 * rank), jnp.bfloat16)],
        compiler_params=pltpu.CompilerParams(vmem_limit_bytes=60 * 1024 * 1024),
        name="feedback",
    )(memory, q_parts, p_ortho)


def per_device(count_rep, frames, out_grad, error_prev, q_prev):
    band_rows, width, chans = frames.shape[1:]
    band = band_rows * width
    memory, q_parts, p_ortho = compressed_step(
        count_rep,
        frames[0].reshape(band, chans),
        out_grad[0].reshape(band, chans),
        error_prev[0],
        q_prev,
    )
    error_next, q_next = feedback(memory, q_parts, p_ortho)
    return (error_next[None], q_next)


def solution(mesh):
    placed = (
        P("rep", "sp", None, None),
        P("rep", "sp", None, None),
        P("rep", "sp", None),
        P(None, "sp"),
    )
    return jax.shard_map(
        functools.partial(per_device, mesh.shape["rep"]),
        mesh=mesh,
        in_specs=placed,
        out_specs=(P("rep", "sp", None), P(None, "sp")),
        check_vma=False,
    )
```

```python
import functools

import jax
import jax.numpy as jnp
from jax import lax
from jax.experimental import pallas as pl
from jax.experimental.pallas import tpu as pltpu
from jax.sharding import PartitionSpec as P

MESH = pl.DeviceIdType.MESH
RING = 4
CHUNKS = 8
COLS = 128
TAPS = 9
T_AT = 0
P_AT = (2, 3, 4, 5)
EARLY = 3


def sp_at(x, z):
    return {"sp": lax.rem(x + RING, RING) * RING + lax.rem(z + RING, RING)}


def remote(src, dst, send, recv, device):
    return pltpu.make_async_remote_copy(
        src_ref=src, dst_ref=dst, send_sem=send, recv_sem=recv, device_id=device, device_id_type=MESH
    )


def split(value):
    high = value.astype(jnp.bfloat16)
    rest = value - high.astype(jnp.float32)
    middle = rest.astype(jnp.bfloat16)
    low = (rest - middle.astype(jnp.float32)).astype(jnp.bfloat16)
    return high, middle, low


def exact_dot(a, b, contract):
    return lax.dot_general(
        a, b, (contract, ((), ())), precision=lax.Precision.HIGHEST, preferred_element_type=jnp.float32
    )


def step_kernel(
    count_rep, frames, g, err, q_own, memory, q_next, p_side,
    local, f_relay, t_relay, q_turned, q_taps, flipped, raw, halo, taps, gbuf, part, relay, piece, total,
    q_near, q_flip, t_term, t_near, p_src, p_near, p_one, p_far, p_all, work, q_src, q_got, q_sum, x_term, x_got,
    l_in, f_send, f_recv, f_own, h_send, h_recv, e_in, g_own,
    d_send, d_recv, r_send, r_recv, a_send, a_recv, b_send, b_recv, out_sem,
    q_send, q_recv, q_copy, t_send, t_recv, s1, r1, s2, r2, s3, r3, s4, r4, s5, r5, x_send, x_recv,
):
    sp, rep = lax.axis_index("sp"), lax.axis_index("rep")
    x, z = sp // RING, lax.rem(sp, RING)
    up, down = sp_at(x, z + 1), sp_at(x, z - 1)
    right, left = sp_at(x + 1, z), sp_at(x - 1, z)
    z_up, z_down = lax.rem(z + 1, RING), lax.rem(z + 3, RING)
    x_right, x_left, x_far = lax.rem(x + 1, RING), lax.rem(x + 3, RING), lax.rem(x + 2, RING)
    band = g.shape[0]
    half = band // 2
    count_sp = RING * RING
    share = part.shape[4] * 2
    width = halo.shape[3]
    rank = q_own.shape[0]

    def at_sp(d):
        return {"sp": lax.rem(sp + d, count_sp)}

    def at_rep(d):
        return {"rep": lax.rem(rep + d, count_rep)}

    near_z, far_z = (z_up, z_down), lax.rem(z + 2, RING)
    towards = (up, down)
    some_x = RING // 2

    def frames_near(side):
        return remote(flipped.at[:, near_z[side]], raw.at[z], f_send.at[side], f_recv.at[side], towards[side])

    def frames_near_in(side):
        return remote(flipped.at[:, z], raw.at[near_z[1 - side]], f_send.at[side], f_recv.at[side], up)

    def frames_far(side):
        part_x = pl.ds(side * some_x, some_x)
        return remote(
            flipped.at[part_x, far_z], f_relay.at[side], f_send.at[2 + side], f_recv.at[2 + side], towards[side]
        )

    def frames_on(side):
        part_x = pl.ds(side * some_x, some_x)
        return remote(
            f_relay.at[side], raw.at[near_z[1 - side], part_x], f_send.at[4 + side], f_recv.at[4 + side], towards[side]
        )

    def frames_far_in(side):
        part_x = pl.ds(side * some_x, some_x)
        return remote(f_relay.at[side], raw.at[far_z, part_x], f_send.at[4 + side], f_recv.at[4 + side], up)

    def columns(j):
        return pl.ds(pl.multiple_of(j * COLS, COLS), COLS)

    def slot(which, first, count):
        return pl.ds(pl.multiple_of(which * band + first, half), count)

    def own_grad(j):
        return pltpu.make_async_copy(g.at[:, columns(j)], gbuf.at[j, slot(z, 0, band)], g_own.at[j])

    def direct(j, side):
        ref = gbuf.at[j, slot(z, 0, band)]
        return remote(ref, ref, d_send.at[j, side], d_recv.at[j, side], up if side == 0 else down)

    def direct_in(j, side):
        ref = gbuf.at[j, slot(z_down if side == 0 else z_up, 0, band)]
        return remote(ref, ref, d_send.at[j, side], d_recv.at[j, side], up)

    def forward(j, side):
        ref = gbuf.at[j, slot(z_down if side == 0 else z_up, side * half, half)]
        return remote(ref, ref, r_send.at[j, side], r_recv.at[j, side], up if side == 0 else down)

    def forward_in(j, side):
        ref = gbuf.at[j, slot(lax.rem(z + 2, RING), side * half, half)]
        return remote(ref, ref, r_send.at[j, side], r_recv.at[j, side], up)

    def err_in(j):
        return pltpu.make_async_copy(err.at[:, columns(j)], total.at[j], e_in.at[j])

    def mem_out(j):
        return pltpu.make_async_copy(total.at[j], memory.at[:, columns(j)], out_sem.at[j])

    def far(j, side, group):
        some = pl.ds(group * 3, 3)
        return remote(
            part.at[j, x_far, side, some], relay.at[j, side, some], a_send.at[j, side, group],
            a_recv.at[j, side, group], right if side == 0 else left,
        )

    def near(j, side, group):
        some = pl.ds(group * 3, 3)
        return remote(
            part.at[j, x_right if side == 0 else x_left, :, some], piece.at[j, side, :, some],
            b_send.at[j, side, group], b_recv.at[j, side, group], right if side == 0 else left,
        )

    def q_out(step):
        return remote(q_taps, q_near.at[:, x], q_send.at[step - 1], q_recv.at[step - 1], sp_at(x + step, z))

    def q_in(step):
        source = lax.rem(x + RING - step, RING)
        return remote(q_taps, q_near.at[:, source], q_send.at[step - 1], q_recv.at[step - 1], right)

    def t_far(side):
        some = pl.ds(side * (rank // 2), rank // 2)
        return remote(t_term.at[far_z, some], t_relay.at[side], t_send.at[side], t_recv.at[side], towards[side])

    def t_out(side):
        return remote(
            t_term.at[near_z[side]], t_near.at[side], t_send.at[2 + side], t_recv.at[2 + side], towards[side]
        )

    def p_scatter(d):
        return remote(p_src.at[lax.rem(sp + d, count_sp)], p_near.at[d - 1], s1.at[d - 1], r1.at[d - 1], at_sp(d))

    def p_share(d):
        return remote(p_one, p_far.at[rep], s2.at[d - 1], r2.at[d - 1], at_rep(d))

    def p_share_in(d):
        source = lax.rem(rep + count_rep - d, count_rep)
        return remote(p_one, p_far.at[source], s2.at[d - 1], r2.at[d - 1], at_rep(d))

    def p_gather(d):
        return remote(p_all.at[sp], p_all.at[sp], s3.at[d - 1], r3.at[d - 1], at_sp(d))

    def p_gather_in(d):
        ref = p_all.at[lax.rem(sp + count_sp - d, count_sp)]
        return remote(ref, ref, s3.at[d - 1], r3.at[d - 1], at_sp(d))

    def x_out(step):
        return remote(x_term.at[step - 1], x_got.at[step - 1], x_send.at[step - 1], x_recv.at[step - 1], sp_at(x + step, z))

    def q_scatter(d):
        return remote(q_src.at[lax.rem(rep + d, count_rep)], q_got.at[d - 1], s4.at[d - 1], r4.at[d - 1], at_rep(d))

    def q_gather(d):
        return remote(q_next.at[rep], q_next.at[rep], s5.at[d - 1], r5.at[d - 1], at_rep(d))

    def q_gather_in(d):
        ref = q_next.at[lax.rem(rep + count_rep - d, count_rep)]
        return remote(ref, ref, s5.at[d - 1], r5.at[d - 1], at_rep(d))

    barrier = pltpu.get_barrier_semaphore()
    for d in range(1, count_sp):
        pl.semaphore_signal(barrier, inc=1, device_id=at_sp(d), device_id_type=MESH)
    for d in range(1, count_rep):
        pl.semaphore_signal(barrier, inc=1, device_id=at_rep(d), device_id_type=MESH)

    def column_in(i):
        return pltpu.make_async_copy(frames.at[:, columns(i)], local.at[i], l_in.at[i])

    pairs = frames.shape[1] // COLS
    owners = COLS // share
    own_grad(0).start()
    for i in range(pairs):
        column_in(i).start()
    pl.semaphore_wait(barrier, count_sp + count_rep - 2)
    own_grad(0).wait()
    direct(0, 0).start()
    direct(0, 1).start()

    per_x = RING // owners
    for first in range(per_x):
        for i in range(first, pairs, per_x):
            column_in(i).wait()
            turned = local[i].T
            for k in range(owners):
                owner = i * owners + k
                flipped[owner // RING, owner % RING] = turned[k * share : (k + 1) * share]
    for side in range(2):
        frames_far(side).start()
    for side in range(2):
        frames_near(side).start()
    own_frames = pltpu.make_async_copy(flipped.at[:, z], raw.at[z], f_own)
    own_frames.start()
    for j in range(CHUNKS):
        err_in(j).start()
    for j in range(1, CHUNKS):
        own_grad(j).start()

    thirds = [third.astype(jnp.float32) for third in split(q_own[...])]
    lanes = q_taps.shape[2]
    thirds.append(jnp.zeros((lanes - 3 * rank, q_own.shape[1]), jnp.float32))
    q_turned[...] = jnp.concatenate(thirds, axis=0).T
    for tap in range(TAPS):
        q_taps[tap] = q_turned[pl.ds(tap, share, stride=TAPS), :].astype(jnp.bfloat16)
    for step in (1, 3, 2):
        q_out(step).start()
    own_q = pltpu.make_async_copy(q_taps, q_near.at[:, x], q_copy)
    own_q.start()

    lane = lax.broadcasted_iota(jnp.int32, (RING * share, width), 1)

    def place(row, value):
        at = pl.ds(pl.multiple_of(row * width, width), width)
        wide = value.astype(jnp.float32)
        taps[0, :, at] = jnp.where(lane == 0, 0.0, pltpu.roll(wide, 1, 1)).astype(taps.dtype)
        taps[1, :, at] = value
        taps[2, :, at] = jnp.where(lane == width - 1, 0.0, pltpu.roll(wide, width - 1, 1)).astype(taps.dtype)

    def place_band(which):
        def place_row(row, carry):
            at = pl.ds(pl.multiple_of(row * width, width), width)
            place(which * (band // width) + row + 1, raw[which, :, :, at].reshape(RING * share, width))
            return carry

        lax.fori_loop(0, band // width, place_row, 0)

    def start_forward(j):
        for side in range(2):
            direct_in(j, side).wait_recv()
            forward(j, side).start()

    def start_direct(j):
        for side in range(2):
            direct(j, side).start()

    own_frames.wait()
    place_band(z)
    start_forward(0)
    for j in range(1, CHUNKS):
        own_grad(j).wait()

    for j in range(CHUNKS):
        err_in(j).wait()
        term = exact_dot(q_own[...], total[j], ((1,), (0,)))
        for h in range(2):
            p_src[2 * j + h] = term[h * (rank // 2) : (h + 1) * (rank // 2)]

    for side in range(2):
        frames_far(side).wait_recv()
        frames_on(side).start()
    for side in range(2):
        frames_near_in(side).wait_recv()
    start_direct(1)
    place_band(z_down)
    place_band(z_up)
    for side in range(2):
        frames_far_in(side).wait_recv()

    bottom = raw.at[RING - 1, :, :, band - width : band]
    above = remote(bottom, halo.at[0], h_send.at[0], h_recv.at[0], right)
    below = remote(raw.at[0, :, :, 0:width], halo.at[1], h_send.at[1], h_recv.at[1], left)
    above.start()
    below.start()
    place_band(lax.rem(z + 2, RING))
    rows = RING * band // width
    above.wait()
    below.wait()
    zero = jnp.zeros((RING * share, width), halo.dtype)
    place(0, jnp.where(x == 0, zero, halo[0].reshape(RING * share, width)))
    place(rows + 1, jnp.where(x == RING - 1, zero, halo[1].reshape(RING * share, width)))

    def t_band(which):
        acc = None
        for a in range(3):
            at = pl.ds(pl.multiple_of(which * band + a * width, width), band)
            stacked = taps[:, :, at].reshape(3 * RING * share, band)
            term = jnp.dot(q_flip[a], stacked, preferred_element_type=jnp.float32)
            acc = term if acc is None else acc + term
        t_term[which] = acc[:rank] + (acc[rank : 2 * rank] + acc[2 * rank : 3 * rank])

    def t_start():
        own_q.wait()
        for step in (1, 3, 2):
            q_in(step).wait_recv()
        for a in range(3):
            q_flip[a] = q_near[3 * a : 3 * a + 3].reshape(3 * RING * share, lanes).T

    def t_bands(first):
        def one(i, carry):
            t_band(first + i)
            return carry

        lax.fori_loop(0, RING // 2, one, 0)

    def t_finish():
        for side in range(2):
            t_far(side).start()

    def t_pass_on():
        for side in range(2):
            some = pl.ds(side * (rank // 2), rank // 2)
            t_far(side).wait_recv()
            t_term[near_z[side], some] = t_term[near_z[side], some] + t_relay[side]
            t_out(side).start()

    def p_terms():
        for side in range(2):
            t_out(side).wait_recv()
        full = t_term[z] + (t_near[0] + t_near[1])
        parts = jnp.concatenate(split(full), axis=0)

        def add(j, carry):
            acc = jnp.dot(parts, gbuf[j, slot(z, 0, band)], preferred_element_type=jnp.float32)
            term = acc[:rank] + (acc[rank : 2 * rank] + acc[2 * rank :])
            for h in range(2):
                p_src[2 * j + h] = p_src[2 * j + h] + term[h * (rank // 2) : (h + 1) * (rank // 2)]
            return carry

        lax.fori_loop(0, CHUNKS, add, 0)
        for d in range(1, count_sp):
            p_scatter(d).start()

    def p_sum_sp():
        acc = p_src[sp]
        for d in range(1, count_sp):
            p_scatter(d).wait_recv()
            acc = acc + p_near[d - 1]
        p_one[...] = acc
        p_far[rep] = acc
        for d in range(1, count_rep):
            p_share(d).start()

    def p_sum_rep():
        for d in range(1, count_rep):
            p_share_in(d).wait_recv()
        acc = p_far[0]
        for i in range(1, count_rep):
            acc = acc + p_far[i]
        p_all[sp] = acc
        for d in range(1, count_sp):
            p_gather(d).start()

    def p_chunk(j):
        return jnp.concatenate([p_all[2 * j], p_all[2 * j + 1]], axis=0)

    def orthogonal():
        for d in range(1, count_sp):
            p_gather_in(d).wait_recv()
        p_total = jnp.concatenate([p_chunk(j) for j in range(CHUNKS)], axis=1)
        gram = exact_dot(p_total, p_total, ((1,), (1,)))
        row_at = lax.broadcasted_iota(jnp.int32, (rank, rank), 0)
        col_at = lax.broadcasted_iota(jnp.int32, (rank, rank), 1)
        work[:, :rank] = gram
        work[:, rank : 2 * rank] = jnp.where(row_at == col_at, 1.0, 0.0)
        shape = (rank, 2 * rank)
        line = lax.broadcasted_iota(jnp.int32, shape, 0)
        spot = lax.broadcasted_iota(jnp.int32, shape, 1)

        def eliminate(k, carry):
            state = work[:, : 2 * rank]
            pivot = work[pl.ds(k, 1), : 2 * rank]
            column = jnp.sum(jnp.where(spot == k, state, 0.0), axis=1, keepdims=True)
            diagonal = jnp.sum(jnp.where(spot[:1] == k, pivot, 0.0), axis=1, keepdims=True)
            inverse = 1.0 / jnp.sqrt(diagonal)
            pivot = pivot * inverse
            work[:, : 2 * rank] = jnp.where(
                line > k, state - (column * inverse) * pivot, jnp.where(line == k, pivot, state)
            )
            return carry

        lax.fori_loop(0, rank, eliminate, 0)
        lower_inverse = jnp.where(col_at <= row_at, work[:, rank : 2 * rank], 0.0)
        whole = exact_dot(lower_inverse, p_total, ((1,), (0,)))
        p0, p1, p2 = split(whole)
        p_side[...] = jnp.concatenate([p0, p1, p2, p0, p1, p0], axis=0)
        q_sum[...] = jnp.zeros_like(q_sum)

    def by_p(rows_of, k):
        m0, m1, m2 = split(rows_of)
        m_side = jnp.concatenate([m0, m0, m0, m1, m1, m2], axis=1)
        across = jnp.concatenate([p_side[i * rank : (i + 1) * rank, columns(k)] for i in range(6)], axis=1)
        return jnp.dot(m_side, across.T, preferred_element_type=jnp.float32)

    def add_q(k):
        q_sum[:, :rank] = q_sum[:, :rank] + by_p(total[k], k)

    last = CHUNKS - 1

    def last_terms():
        for step in (1, 3, 2):
            owner = lax.rem(x + step, RING)
            terms = by_p(part[last, owner].reshape(q_sum.shape[0], COLS), last)
            x_term[step - 1] = terms.T
            x_out(step).start()

    def last_own():
        count = part.shape[4]
        for side in range(2):
            for tap in range(TAPS):
                at = pl.ds(side * count * TAPS + tap, count, stride=TAPS)
                total[last, at, :] = total[last, at, :] + part[last, x, side, tap]
        add_q(last)

    def last_sum():
        for step in (1, 3, 2):
            x_out(step).wait_recv()
        got = x_got[0] + x_got[1] + x_got[2]
        filled = jnp.concatenate([got, jnp.zeros((128 - rank, got.shape[1]), jnp.float32)], axis=0).T
        count = part.shape[4]
        for side in range(2):
            for tap in range(TAPS):
                at = pl.ds(side * count * TAPS + tap, count, stride=TAPS)
                line = (side * TAPS + tap) * count
                q_sum[at, :] = q_sum[at, :] + filled[line : line + count]

    def multiply(first, count, after):
        depth = gbuf.shape[1]
        per_side = part.shape[4]

        def one(a, carry):
            at = pl.ds(pl.multiple_of(a * width, width), depth)
            stacked = taps[:, :, at].reshape(3 * RING * share, depth)
            chosen = gbuf[first] if count == 1 else jnp.concatenate([gbuf[first], gbuf[first + 1]], axis=1)
            product = jnp.dot(stacked, chosen, preferred_element_type=jnp.float32)
            for c in range(count):
                for b in range(3):
                    for owner in range(RING):
                        for side in range(2):
                            line = b * RING * share + (owner * 2 + side) * per_side
                            part[first + c, owner, side, a * 3 + b] = product[
                                line : line + per_side, c * COLS : (c + 1) * COLS
                            ]
                far(first + c, 0, a).start()
                far(first + c, 1, a).start()

            @pl.when((a == 0) & (after < CHUNKS))
            def _():
                start_forward(after)

            return carry

        lax.fori_loop(0, 3, one, 0)

    def pass_on(k):
        for group in range(3):
            some = pl.ds(group * 3, 3)
            far(k, 0, group).wait_recv()
            part[k, x_right, 0, some] = part[k, x_right, 0, some] + relay[k, 0, some]
            near(k, 0, group).start()
            far(k, 1, group).wait_recv()
            part[k, x_left, 1, some] = part[k, x_left, 1, some] + relay[k, 1, some]
            near(k, 1, group).start()

    def complete(k, with_q):
        for group in range(3):
            near(k, 0, group).wait_recv()
            near(k, 1, group).wait_recv()
        count = part.shape[4]
        for side in range(2):
            for tap in range(TAPS):
                at = pl.ds(side * count * TAPS + tap, count, stride=TAPS)
                total[k, at, :] = (
                    total[k, at, :] + part[k, x, side, tap] + (piece[k, 0, side, tap] + piece[k, 1, side, tap])
                )
        mem_out(k).start()
        pl.when(with_q)(lambda: add_q(k))

    def complete_last():
        for group in range(3):
            near(last, 0, group).wait_recv()
            near(last, 1, group).wait_recv()
        count = part.shape[4]
        for side in range(2):
            for tap in range(TAPS):
                at = pl.ds(side * count * TAPS + tap, count, stride=TAPS)
                total[last, at, :] = total[last, at, :] + (piece[last, 0, side, tap] + piece[last, 1, side, tap])
        mem_out(last).start()

    def over(first, count, body):
        def one(i, carry):
            body(first + i)
            return carry

        lax.fori_loop(0, count, one, 0)

    def step(j, carry):
        @pl.when(j + 2 < CHUNKS)
        def _():
            start_direct(j + 2)

        @pl.when(j < CHUNKS)
        def _():
            forward_in(j, 0).wait_recv()
            forward_in(j, 1).wait_recv()

        alone = (j == 0) | (j == CHUNKS - 1)
        even = lax.rem(j, 2) == 0
        pl.when(alone)(lambda: multiply(j, 1, j + 1))
        pl.when((j > 0) & (j < CHUNKS - 1) & even)(lambda: multiply(j - 1, 2, j + 1))
        pl.when((j < CHUNKS - 1) & jnp.logical_not(even))(lambda: start_forward(j + 1))

        pl.when((j == 1) | (j == CHUNKS))(lambda: pass_on(j - 1))
        pl.when((j > 1) & (j < CHUNKS) & jnp.logical_not(even))(lambda: over(j - 2, 2, pass_on))

        @pl.when(j == T_AT)
        def _():
            t_start()
            t_bands(0)
            t_bands(RING // 2)
            t_finish()

        pl.when(j == T_AT + 1)(t_pass_on)
        pl.when(j == last)(last_terms)

        for at, stage in zip(P_AT, (p_terms, p_sum_sp, p_sum_rep, orthogonal)):
            pl.when(j == at)(stage)
        ready = j >= P_AT[-1]

        pl.when(j == 2)(lambda: complete(0, ready))
        pl.when((j > 2) & (j <= CHUNKS) & even)(lambda: over(j - 3, 2, lambda k: complete(k, ready)))
        pl.when(j == P_AT[-1])(lambda: over(0, EARLY, add_q))

        return carry

    lax.fori_loop(0, CHUNKS + 1, step, 0)
    last_own()
    last_sum()

    lines = rank // count_rep
    q_lines = q_sum[...].T
    for i in range(count_rep):
        q_src[i] = q_lines[i * lines : (i + 1) * lines]
    for d in range(1, count_rep):
        q_scatter(d).start()
    acc = q_src[rep]
    for d in range(1, count_rep):
        q_scatter(d).wait_recv()
        acc = acc + q_got[d - 1]
    q_next[rep] = acc * (1.0 / count_rep)
    for d in range(1, count_rep):
        q_gather(d).start()
    complete_last()
    for d in range(1, count_rep):
        q_gather_in(d).wait_recv()

    def finish(j, carry):
        for side in range(2):
            direct(j, side).wait_send()
            forward(j, side).wait_send()
            for group in range(3):
                far(j, side, group).wait_send()
                near(j, side, group).wait_send()
        mem_out(j).wait()
        return carry

    lax.fori_loop(0, CHUNKS, finish, 0)
    for side in range(2):
        frames_near(side).wait_send()
        frames_far(side).wait_send()
        frames_on(side).wait_send()
        t_far(side).wait_send()
        t_out(side).wait_send()
    for step_ in (1, 3, 2):
        q_out(step_).wait_send()
        x_out(step_).wait_send()
    for d in range(1, count_sp):
        p_scatter(d).wait_send()
        p_gather(d).wait_send()
    for d in range(1, count_rep):
        p_share(d).wait_send()
        q_scatter(d).wait_send()
        q_gather(d).wait_send()


def compressed_step(count_rep, frames, g, err, q_own):
    band, chans = g.shape
    width = band // 4
    rows = err.shape[0]
    rank = q_own.shape[0]
    count_sp = RING * RING
    share = chans // count_sp
    per_side = share // 2
    dma = pltpu.SemaphoreType.DMA
    two, three = dma((CHUNKS, 2)), dma((CHUNKS, 2, 3))
    f32, bf16 = jnp.float32, jnp.bfloat16
    any_spec, vmem_spec = pl.BlockSpec(memory_space=pl.ANY), pl.BlockSpec(memory_space=pltpu.VMEM)
    p_block = (rank // 2, COLS)
    q_block = (rank // count_rep, rows)
    return pl.pallas_call(
        functools.partial(step_kernel, count_rep),
        out_shape=(
            jax.ShapeDtypeStruct((rows, chans), f32),
            jax.ShapeDtypeStruct((count_rep, *q_block), f32),
            jax.ShapeDtypeStruct((6 * rank, chans), bf16),
        ),
        in_specs=[any_spec, any_spec, any_spec, vmem_spec],
        out_specs=(any_spec, vmem_spec, vmem_spec),
        scratch_shapes=[
            pltpu.VMEM((chans // COLS, band, COLS), bf16),
            pltpu.VMEM((2, RING // 2, share, band), bf16),
            pltpu.VMEM((2, rank // 2, band), f32),
            pltpu.VMEM((rows, 128), f32),
            pltpu.VMEM((TAPS, share, 128), bf16),
            pltpu.VMEM((RING, RING, share, band), bf16),
            pltpu.VMEM((RING, RING, share, band), bf16),
            pltpu.VMEM((2, RING, share, width), bf16),
            pltpu.VMEM((3, RING * share, RING * band + 2 * width), bf16),
            pltpu.VMEM((CHUNKS, RING * band, COLS), bf16),
            pltpu.VMEM((CHUNKS, RING, 2, TAPS, per_side, COLS), f32),
            pltpu.VMEM((CHUNKS, 2, TAPS, per_side, COLS), f32),
            pltpu.VMEM((CHUNKS, 2, 2, TAPS, per_side, COLS), f32),
            pltpu.VMEM((CHUNKS, rows, COLS), f32),
            pltpu.VMEM((TAPS, RING, share, 128), bf16),
            pltpu.VMEM((3, 128, 3 * RING * share), bf16),
            pltpu.VMEM((RING, rank, band), f32),
            pltpu.VMEM((2, rank, band), f32),
            pltpu.VMEM((count_sp, *p_block), f32),
            pltpu.VMEM((count_sp - 1, *p_block), f32),
            pltpu.VMEM(p_block, f32),
            pltpu.VMEM((count_rep, *p_block), f32),
            pltpu.VMEM((count_sp, *p_block), f32),
            pltpu.VMEM((rank, 128), f32),
            pltpu.VMEM((count_rep, *q_block), f32),
            pltpu.VMEM((count_rep - 1, *q_block), f32),
            pltpu.VMEM((rows, 128), f32),
            pltpu.VMEM((RING - 1, rank, rows), f32),
            pltpu.VMEM((RING - 1, rank, rows), f32),
            dma((chans // COLS,)), dma((6,)), dma((6,)), dma, dma((2,)), dma((2,)), dma((CHUNKS,)), dma((CHUNKS,)),
            two, two, two, two, three, three, three, three, dma((CHUNKS,)),
            dma((3,)), dma((3,)), dma, dma((4,)), dma((4,)),
            dma((count_sp - 1,)), dma((count_sp - 1,)), dma((count_rep - 1,)), dma((count_rep - 1,)),
            dma((count_sp - 1,)), dma((count_sp - 1,)), dma((count_rep - 1,)), dma((count_rep - 1,)),
            dma((count_rep - 1,)), dma((count_rep - 1,)), dma((3,)), dma((3,)),
        ],
        compiler_params=pltpu.CompilerParams(
            collective_id=0, has_side_effects=True, vmem_limit_bytes=58 * 1024 * 1024
        ),
        cost_estimate=pl.CostEstimate(flops=2 * rows * 16 * chans * band, bytes_accessed=10**7, transcendentals=0),
        name="compressed_step",
    )(frames, g, err, q_own)


def feedback_kernel(memory, q_parts, p_side, error_next, q_next, q_side):
    count, lines, rows = q_parts.shape
    block = memory.shape[0]

    @pl.when(pl.program_id(0) == 0)
    def _():
        for i in range(count):
            q_next[i * lines : (i + 1) * lines] = q_parts[i]
        q0, q1, q2 = split(q_next[...])
        q_side[...] = jnp.concatenate([q0, q0, q0, q1, q1, q2], axis=0).T

    at = pl.ds(pl.multiple_of(pl.program_id(0) * block, block), block)
    error_next[...] = memory[...] - jnp.dot(q_side[at, :], p_side[...], preferred_element_type=jnp.float32)


def feedback(memory, q_parts, p_side):
    rows, chans = memory.shape
    count, lines, _ = q_parts.shape
    rank = count * lines
    block = (rows // 4, chans)
    return pl.pallas_call(
        feedback_kernel,
        grid=(rows // block[0],),
        out_shape=(jax.ShapeDtypeStruct(memory.shape, jnp.float32), jax.ShapeDtypeStruct((rank, rows), jnp.float32)),
        in_specs=[
            pl.BlockSpec(block, lambda i: (i, 0)),
            pl.BlockSpec(q_parts.shape, lambda i: (0, 0, 0)),
            pl.BlockSpec(p_side.shape, lambda i: (0, 0)),
        ],
        out_specs=(pl.BlockSpec(block, lambda i: (i, 0)), pl.BlockSpec((rank, rows), lambda i: (0, 0))),
        scratch_shapes=[pltpu.VMEM((rows, 6 * rank), jnp.bfloat16)],
        compiler_params=pltpu.CompilerParams(vmem_limit_bytes=60 * 1024 * 1024),
        name="feedback",
    )(memory, q_parts, p_side)


def per_device(count_rep, frames, out_grad, error_prev, q_prev):
    band_rows, width, chans = frames.shape[1:]
    band = band_rows * width
    memory, q_parts, p_side = compressed_step(
        count_rep,
        frames[0].reshape(band, chans),
        out_grad[0].reshape(band, chans),
        error_prev[0],
        q_prev,
    )
    error_next, q_next = feedback(memory, q_parts, p_side)
    return (error_next[None], q_next)


def solution(mesh):
    placed = (
        P("rep", "sp", None, None),
        P("rep", "sp", None, None),
        P("rep", "sp", None),
        P(None, "sp"),
    )
    return jax.shard_map(
        functools.partial(per_device, mesh.shape["rep"]),
        mesh=mesh,
        in_specs=placed,
        out_specs=(P("rep", "sp", None), P(None, "sp")),
        check_vma=False,
    )
```

```python
import functools

import jax
import jax.numpy as jnp
from jax import lax
from jax.experimental import pallas as pl
from jax.experimental.pallas import tpu as pltpu
from jax.sharding import PartitionSpec as P

MESH = pl.DeviceIdType.MESH
RING = 4
CHUNKS = 8
COLS = 128
TAPS = 9
T_AT = 0
P_AT = (2, 3, 4, 5)
EARLY = 3


def sp_at(x, z):
    return {"sp": lax.rem(x + RING, RING) * RING + lax.rem(z + RING, RING)}


def remote(src, dst, send, recv, device):
    return pltpu.make_async_remote_copy(
        src_ref=src, dst_ref=dst, send_sem=send, recv_sem=recv, device_id=device, device_id_type=MESH
    )


def split(value):
    high = value.astype(jnp.bfloat16)
    rest = value - high.astype(jnp.float32)
    middle = rest.astype(jnp.bfloat16)
    low = (rest - middle.astype(jnp.float32)).astype(jnp.bfloat16)
    return high, middle, low


def exact_dot(a, b, contract):
    return lax.dot_general(
        a, b, (contract, ((), ())), precision=lax.Precision.HIGHEST, preferred_element_type=jnp.float32
    )


def step_kernel(
    count_rep, frames, g, err, q_own, memory, q_next, p_side,
    local, f_relay, t_relay, q_turned, q_taps, flipped, raw, halo, taps, gbuf, part, relay, piece, total,
    q_near, q_flip, t_work, t_term, t_near, p_src, p_near, p_one, p_far, p_all, work, q_src, q_got, q_sum, x_term, x_got,
    l_in, f_send, f_recv, f_own, h_send, h_recv, e_in, g_own,
    d_send, d_recv, r_send, r_recv, a_send, a_recv, b_send, b_recv, out_sem,
    q_send, q_recv, q_copy, t_send, t_recv, s1, r1, s2, r2, s3, r3, s4, r4, s5, r5, x_send, x_recv,
):
    sp, rep = lax.axis_index("sp"), lax.axis_index("rep")
    x, z = sp // RING, lax.rem(sp, RING)
    up, down = sp_at(x, z + 1), sp_at(x, z - 1)
    right, left = sp_at(x + 1, z), sp_at(x - 1, z)
    z_up, z_down = lax.rem(z + 1, RING), lax.rem(z + 3, RING)
    x_right, x_left, x_far = lax.rem(x + 1, RING), lax.rem(x + 3, RING), lax.rem(x + 2, RING)
    band = g.shape[0]
    half = band // 2
    count_sp = RING * RING
    share = part.shape[4] * 2
    width = halo.shape[3]
    rank = q_own.shape[0]

    def at_sp(d):
        return {"sp": lax.rem(sp + d, count_sp)}

    def at_rep(d):
        return {"rep": lax.rem(rep + d, count_rep)}

    near_z, far_z = (z_up, z_down), lax.rem(z + 2, RING)
    towards = (up, down)
    some_x = RING // 2

    def frames_near(side):
        return remote(flipped.at[:, near_z[side]], raw.at[z], f_send.at[side], f_recv.at[side], towards[side])

    def frames_near_in(side):
        return remote(flipped.at[:, z], raw.at[near_z[1 - side]], f_send.at[side], f_recv.at[side], up)

    def frames_far(side):
        part_x = pl.ds(side * some_x, some_x)
        return remote(
            flipped.at[part_x, far_z], f_relay.at[side], f_send.at[2 + side], f_recv.at[2 + side], towards[side]
        )

    def frames_on(side):
        part_x = pl.ds(side * some_x, some_x)
        return remote(
            f_relay.at[side], raw.at[near_z[1 - side], part_x], f_send.at[4 + side], f_recv.at[4 + side], towards[side]
        )

    def frames_far_in(side):
        part_x = pl.ds(side * some_x, some_x)
        return remote(f_relay.at[side], raw.at[far_z, part_x], f_send.at[4 + side], f_recv.at[4 + side], up)

    def columns(j):
        return pl.ds(pl.multiple_of(j * COLS, COLS), COLS)

    def slot(which, first, count):
        return pl.ds(pl.multiple_of(which * band + first, half), count)

    def own_grad(j):
        return pltpu.make_async_copy(g.at[:, columns(j)], gbuf.at[j, slot(z, 0, band)], g_own.at[j])

    def direct(j, side):
        ref = gbuf.at[j, slot(z, 0, band)]
        return remote(ref, ref, d_send.at[j, side], d_recv.at[j, side], up if side == 0 else down)

    def direct_in(j, side):
        ref = gbuf.at[j, slot(z_down if side == 0 else z_up, 0, band)]
        return remote(ref, ref, d_send.at[j, side], d_recv.at[j, side], up)

    def forward(j, side):
        ref = gbuf.at[j, slot(z_down if side == 0 else z_up, side * half, half)]
        return remote(ref, ref, r_send.at[j, side], r_recv.at[j, side], up if side == 0 else down)

    def forward_in(j, side):
        ref = gbuf.at[j, slot(lax.rem(z + 2, RING), side * half, half)]
        return remote(ref, ref, r_send.at[j, side], r_recv.at[j, side], up)

    def err_in(j):
        return pltpu.make_async_copy(err.at[:, columns(j)], total.at[j], e_in.at[j])

    def mem_out(j):
        return pltpu.make_async_copy(total.at[j], memory.at[:, columns(j)], out_sem.at[j])

    def far(j, side, group):
        some = pl.ds(group * 3, 3)
        return remote(
            part.at[j, x_far, side, some], relay.at[j, side, some], a_send.at[j, side, group],
            a_recv.at[j, side, group], right if side == 0 else left,
        )

    def near(j, side, group):
        some = pl.ds(group * 3, 3)
        return remote(
            part.at[j, x_right if side == 0 else x_left, :, some], piece.at[j, side, :, some],
            b_send.at[j, side, group], b_recv.at[j, side, group], right if side == 0 else left,
        )

    def q_out(step):
        return remote(q_taps, q_near.at[:, x], q_send.at[step - 1], q_recv.at[step - 1], sp_at(x + step, z))

    def q_in(step):
        source = lax.rem(x + RING - step, RING)
        return remote(q_taps, q_near.at[:, source], q_send.at[step - 1], q_recv.at[step - 1], right)

    def t_far(side):
        some = pl.ds(side * (rank // 2), rank // 2)
        return remote(t_term.at[far_z, some], t_relay.at[side], t_send.at[side], t_recv.at[side], towards[side])

    def t_out(side):
        return remote(
            t_term.at[near_z[side]], t_near.at[side], t_send.at[2 + side], t_recv.at[2 + side], towards[side]
        )

    def p_scatter(d):
        return remote(p_src.at[lax.rem(sp + d, count_sp)], p_near.at[d - 1], s1.at[d - 1], r1.at[d - 1], at_sp(d))

    def p_share(d):
        return remote(p_one, p_far.at[rep], s2.at[d - 1], r2.at[d - 1], at_rep(d))

    def p_share_in(d):
        source = lax.rem(rep + count_rep - d, count_rep)
        return remote(p_one, p_far.at[source], s2.at[d - 1], r2.at[d - 1], at_rep(d))

    def p_gather(d):
        return remote(p_all.at[sp], p_all.at[sp], s3.at[d - 1], r3.at[d - 1], at_sp(d))

    def p_gather_in(d):
        ref = p_all.at[lax.rem(sp + count_sp - d, count_sp)]
        return remote(ref, ref, s3.at[d - 1], r3.at[d - 1], at_sp(d))

    def x_out(step):
        return remote(x_term.at[step - 1], x_got.at[step - 1], x_send.at[step - 1], x_recv.at[step - 1], sp_at(x + step, z))

    def q_scatter(d):
        return remote(q_src.at[lax.rem(rep + d, count_rep)], q_got.at[d - 1], s4.at[d - 1], r4.at[d - 1], at_rep(d))

    def q_gather(d):
        return remote(q_next.at[rep], q_next.at[rep], s5.at[d - 1], r5.at[d - 1], at_rep(d))

    def q_gather_in(d):
        ref = q_next.at[lax.rem(rep + count_rep - d, count_rep)]
        return remote(ref, ref, s5.at[d - 1], r5.at[d - 1], at_rep(d))

    barrier = pltpu.get_barrier_semaphore()
    for d in range(1, count_sp):
        pl.semaphore_signal(barrier, inc=1, device_id=at_sp(d), device_id_type=MESH)
    for d in range(1, count_rep):
        pl.semaphore_signal(barrier, inc=1, device_id=at_rep(d), device_id_type=MESH)

    def column_in(i):
        return pltpu.make_async_copy(frames.at[:, columns(i)], local.at[i], l_in.at[i])

    pairs = frames.shape[1] // COLS
    owners = COLS // share
    own_grad(0).start()
    for i in range(pairs):
        column_in(i).start()
    pl.semaphore_wait(barrier, count_sp + count_rep - 2)
    own_grad(0).wait()
    direct(0, 0).start()
    direct(0, 1).start()

    per_x = RING // owners
    for first in range(per_x):
        for i in range(first, pairs, per_x):
            column_in(i).wait()
            turned = local[i].T
            for k in range(owners):
                owner = i * owners + k
                flipped[owner // RING, owner % RING] = turned[k * share : (k + 1) * share]
    for side in range(2):
        frames_far(side).start()
    for side in range(2):
        frames_near(side).start()
    own_frames = pltpu.make_async_copy(flipped.at[:, z], raw.at[z], f_own)
    own_frames.start()
    for j in range(CHUNKS):
        err_in(j).start()
    for j in range(1, CHUNKS):
        own_grad(j).start()

    thirds = [third.astype(jnp.float32) for third in split(q_own[...])]
    lanes = q_taps.shape[2]
    thirds.append(jnp.zeros((lanes - 3 * rank, q_own.shape[1]), jnp.float32))
    q_turned[...] = jnp.concatenate(thirds, axis=0).T
    for tap in range(TAPS):
        q_taps[tap] = q_turned[pl.ds(tap, share, stride=TAPS), :].astype(jnp.bfloat16)
    for step in (1, 3, 2):
        q_out(step).start()
    own_q = pltpu.make_async_copy(q_taps, q_near.at[:, x], q_copy)
    own_q.start()

    lane = lax.broadcasted_iota(jnp.int32, (RING * share, width), 1)

    def place(row, value):
        at = pl.ds(pl.multiple_of(row * width, width), width)
        wide = value.astype(jnp.float32)
        taps[0, :, at] = jnp.where(lane == 0, 0.0, pltpu.roll(wide, 1, 1)).astype(taps.dtype)
        taps[1, :, at] = value
        taps[2, :, at] = jnp.where(lane == width - 1, 0.0, pltpu.roll(wide, width - 1, 1)).astype(taps.dtype)

    def place_band(which):
        def place_row(row, carry):
            at = pl.ds(pl.multiple_of(row * width, width), width)
            place(which * (band // width) + row + 1, raw[which, :, :, at].reshape(RING * share, width))
            return carry

        lax.fori_loop(0, band // width, place_row, 0)

    def start_forward(j):
        for side in range(2):
            direct_in(j, side).wait_recv()
            forward(j, side).start()

    def start_direct(j):
        for side in range(2):
            direct(j, side).start()

    own_frames.wait()
    place_band(z)
    start_forward(0)
    for j in range(1, CHUNKS):
        own_grad(j).wait()
    start_direct(1)

    for side in range(2):
        frames_far(side).wait_recv()
        frames_on(side).start()
    for side in range(2):
        frames_near_in(side).wait_recv()
    place_band(z_down)
    place_band(z_up)
    for side in range(2):
        frames_far_in(side).wait_recv()

    bottom = raw.at[RING - 1, :, :, band - width : band]
    above = remote(bottom, halo.at[0], h_send.at[0], h_recv.at[0], right)
    below = remote(raw.at[0, :, :, 0:width], halo.at[1], h_send.at[1], h_recv.at[1], left)
    above.start()
    below.start()
    place_band(lax.rem(z + 2, RING))
    rows = RING * band // width
    above.wait()
    below.wait()
    zero = jnp.zeros((RING * share, width), halo.dtype)
    place(0, jnp.where(x == 0, zero, halo[0].reshape(RING * share, width)))
    place(rows + 1, jnp.where(x == RING - 1, zero, halo[1].reshape(RING * share, width)))

    def t_start():
        own_q.wait()
        for step in (1, 3, 2):
            q_in(step).wait_recv()
        for tap in range(TAPS):
            turned = q_near[tap].reshape(RING * share, lanes).T
            q_flip[tap * 3 * rank : (tap + 1) * 3 * rank] = turned[: 3 * rank]
        t_work[...] = jnp.zeros_like(t_work)

    def t_rows():
        def one(row, carry):
            at = pl.ds(pl.multiple_of(row * width, width), width)
            product = jnp.dot(q_flip[...], taps[1, :, at], preferred_element_type=jnp.float32)
            for a in range(3):
                for b in range(3):
                    line = (a * 3 + b) * 3 * rank
                    term = product[line : line + rank] + (
                        product[line + rank : line + 2 * rank] + product[line + 2 * rank : line + 3 * rank]
                    )
                    t_work[b, row + 2 - a] = t_work[b, row + 2 - a] + term
            return carry

        lax.fori_loop(0, rows + 2, one, 0)
        lane_of = lax.broadcasted_iota(jnp.int32, (rank, width), 1)
        per_band = band // width
        for row in range(rows):
            before = jnp.where(lane_of == 0, 0.0, pltpu.roll(t_work[0, row + 2], 1, 1))
            after = jnp.where(lane_of == width - 1, 0.0, pltpu.roll(t_work[2, row + 2], width - 1, 1))
            spot = (row % per_band) * width
            t_term[row // per_band, :, spot : spot + width] = t_work[1, row + 2] + (before + after)

    def p_start():
        for j in range(CHUNKS):
            err_in(j).wait()
        q0, q1, _ = split(q_own[...])
        both = jnp.concatenate([q0, q1], axis=0)

        def two(i, carry):
            j = 2 * i
            e0, e1, _ = split(jnp.concatenate([total[j], total[j + 1]], axis=1))
            main = jnp.dot(both, e0, preferred_element_type=jnp.float32)
            term = main[:rank] + (main[rank:] + jnp.dot(q0, e1, preferred_element_type=jnp.float32))
            for c in range(2):
                for h in range(2):
                    p_src[2 * (j + c) + h] = term[
                        h * (rank // 2) : (h + 1) * (rank // 2), c * COLS : (c + 1) * COLS
                    ]
            return carry

        lax.fori_loop(0, CHUNKS // 2, two, 0)

    def t_finish():
        for side in range(2):
            t_far(side).start()

    def t_pass_on():
        for side in range(2):
            some = pl.ds(side * (rank // 2), rank // 2)
            t_far(side).wait_recv()
            t_term[near_z[side], some] = t_term[near_z[side], some] + t_relay[side]
            t_out(side).start()

    def p_terms():
        for side in range(2):
            t_out(side).wait_recv()
        full = t_term[z] + (t_near[0] + t_near[1])
        parts = jnp.concatenate(split(full), axis=0)

        def add(j, carry):
            acc = jnp.dot(parts, gbuf[j, slot(z, 0, band)], preferred_element_type=jnp.float32)
            term = acc[:rank] + (acc[rank : 2 * rank] + acc[2 * rank :])
            for h in range(2):
                p_src[2 * j + h] = p_src[2 * j + h] + term[h * (rank // 2) : (h + 1) * (rank // 2)]
            return carry

        lax.fori_loop(0, CHUNKS, add, 0)
        for d in range(1, count_sp):
            p_scatter(d).start()

    def p_sum_sp():
        acc = p_src[sp]
        for d in range(1, count_sp):
            p_scatter(d).wait_recv()
            acc = acc + p_near[d - 1]
        p_one[...] = acc
        p_far[rep] = acc
        for d in range(1, count_rep):
            p_share(d).start()

    def p_sum_rep():
        for d in range(1, count_rep):
            p_share_in(d).wait_recv()
        acc = p_far[0]
        for i in range(1, count_rep):
            acc = acc + p_far[i]
        p_all[sp] = acc
        for d in range(1, count_sp):
            p_gather(d).start()

    def p_chunk(j):
        return jnp.concatenate([p_all[2 * j], p_all[2 * j + 1]], axis=0)

    def orthogonal():
        for d in range(1, count_sp):
            p_gather_in(d).wait_recv()
        p_total = jnp.concatenate([p_chunk(j) for j in range(CHUNKS)], axis=1)
        gram = exact_dot(p_total, p_total, ((1,), (1,)))
        row_at = lax.broadcasted_iota(jnp.int32, (rank, rank), 0)
        col_at = lax.broadcasted_iota(jnp.int32, (rank, rank), 1)
        work[:, :rank] = gram
        work[:, rank : 2 * rank] = jnp.where(row_at == col_at, 1.0, 0.0)
        shape = (rank, 2 * rank)
        line = lax.broadcasted_iota(jnp.int32, shape, 0)
        spot = lax.broadcasted_iota(jnp.int32, shape, 1)

        def eliminate(k, carry):
            state = work[:, : 2 * rank]
            pivot = work[pl.ds(k, 1), : 2 * rank]
            column = jnp.sum(jnp.where(spot == k, state, 0.0), axis=1, keepdims=True)
            diagonal = jnp.sum(jnp.where(spot[:1] == k, pivot, 0.0), axis=1, keepdims=True)
            inverse = 1.0 / jnp.sqrt(diagonal)
            pivot = pivot * inverse
            work[:, : 2 * rank] = jnp.where(
                line > k, state - (column * inverse) * pivot, jnp.where(line == k, pivot, state)
            )
            return carry

        lax.fori_loop(0, rank, eliminate, 0)
        lower_inverse = jnp.where(col_at <= row_at, work[:, rank : 2 * rank], 0.0)
        whole = exact_dot(lower_inverse, p_total, ((1,), (0,)))
        p0, p1, p2 = split(whole)
        p_side[...] = jnp.concatenate([p0, p1, p2, p0, p1, p0], axis=0)
        q_sum[...] = jnp.zeros_like(q_sum)

    def by_p(rows_of, k):
        m0, m1, m2 = split(rows_of)
        m_side = jnp.concatenate([m0, m0, m0, m1, m1, m2], axis=1)
        across = jnp.concatenate([p_side[i * rank : (i + 1) * rank, columns(k)] for i in range(6)], axis=1)
        return jnp.dot(m_side, across.T, preferred_element_type=jnp.float32)

    def add_q(k):
        q_sum[:, :rank] = q_sum[:, :rank] + by_p(total[k], k)

    last = CHUNKS - 1

    def last_terms():
        for step in (1, 3, 2):
            owner = lax.rem(x + step, RING)
            terms = by_p(part[last, owner].reshape(q_sum.shape[0], COLS), last)
            x_term[step - 1] = terms.T
            x_out(step).start()

    def last_own():
        count = part.shape[4]
        for side in range(2):
            for tap in range(TAPS):
                at = pl.ds(side * count * TAPS + tap, count, stride=TAPS)
                total[last, at, :] = total[last, at, :] + part[last, x, side, tap]
        add_q(last)

    def last_sum():
        for step in (1, 3, 2):
            x_out(step).wait_recv()
        got = x_got[0] + x_got[1] + x_got[2]
        filled = jnp.concatenate([got, jnp.zeros((128 - rank, got.shape[1]), jnp.float32)], axis=0).T
        count = part.shape[4]
        for side in range(2):
            for tap in range(TAPS):
                at = pl.ds(side * count * TAPS + tap, count, stride=TAPS)
                line = (side * TAPS + tap) * count
                q_sum[at, :] = q_sum[at, :] + filled[line : line + count]

    def multiply(first, count, after):
        depth = gbuf.shape[1]
        per_side = part.shape[4]

        def one(a, carry):
            at = pl.ds(pl.multiple_of(a * width, width), depth)
            stacked = taps[:, :, at].reshape(3 * RING * share, depth)
            chosen = gbuf[first] if count == 1 else jnp.concatenate([gbuf[first], gbuf[first + 1]], axis=1)
            product = jnp.dot(stacked, chosen, preferred_element_type=jnp.float32)
            for c in range(count):
                for b in range(3):
                    for owner in range(RING):
                        for side in range(2):
                            line = b * RING * share + (owner * 2 + side) * per_side
                            part[first + c, owner, side, a * 3 + b] = product[
                                line : line + per_side, c * COLS : (c + 1) * COLS
                            ]
                far(first + c, 0, a).start()
                far(first + c, 1, a).start()

            @pl.when((a == 0) & (after < CHUNKS))
            def _():
                start_forward(after)

            return carry

        lax.fori_loop(0, 3, one, 0)

    def pass_on(k):
        for group in range(3):
            some = pl.ds(group * 3, 3)
            far(k, 0, group).wait_recv()
            part[k, x_right, 0, some] = part[k, x_right, 0, some] + relay[k, 0, some]
            near(k, 0, group).start()
            far(k, 1, group).wait_recv()
            part[k, x_left, 1, some] = part[k, x_left, 1, some] + relay[k, 1, some]
            near(k, 1, group).start()

    def complete(k, with_q):
        for group in range(3):
            near(k, 0, group).wait_recv()
            near(k, 1, group).wait_recv()
        count = part.shape[4]
        for side in range(2):
            for tap in range(TAPS):
                at = pl.ds(side * count * TAPS + tap, count, stride=TAPS)
                total[k, at, :] = (
                    total[k, at, :] + part[k, x, side, tap] + (piece[k, 0, side, tap] + piece[k, 1, side, tap])
                )
        mem_out(k).start()
        pl.when(with_q)(lambda: add_q(k))

    def complete_last():
        for group in range(3):
            near(last, 0, group).wait_recv()
            near(last, 1, group).wait_recv()
        count = part.shape[4]
        for side in range(2):
            for tap in range(TAPS):
                at = pl.ds(side * count * TAPS + tap, count, stride=TAPS)
                total[last, at, :] = total[last, at, :] + (piece[last, 0, side, tap] + piece[last, 1, side, tap])
        mem_out(last).start()

    def over(first, count, body):
        def one(i, carry):
            body(first + i)
            return carry

        lax.fori_loop(0, count, one, 0)

    def step(j, carry):
        @pl.when(j + 2 < CHUNKS)
        def _():
            start_direct(j + 2)

        @pl.when(j < CHUNKS)
        def _():
            forward_in(j, 0).wait_recv()
            forward_in(j, 1).wait_recv()

        alone = (j == 0) | (j == CHUNKS - 1)
        even = lax.rem(j, 2) == 0
        pl.when(alone)(lambda: multiply(j, 1, j + 1))
        pl.when((j > 0) & (j < CHUNKS - 1) & even)(lambda: multiply(j - 1, 2, j + 1))
        pl.when((j < CHUNKS - 1) & jnp.logical_not(even))(lambda: start_forward(j + 1))

        pl.when((j == 1) | (j == CHUNKS))(lambda: pass_on(j - 1))
        pl.when((j > 1) & (j < CHUNKS) & jnp.logical_not(even))(lambda: over(j - 2, 2, pass_on))

        @pl.when(j == T_AT)
        def _():
            t_start()
            t_rows()
            t_finish()

        @pl.when(j == T_AT + 1)
        def _():
            t_pass_on()
            p_start()
        pl.when(j == last)(last_terms)

        for at, stage in zip(P_AT, (p_terms, p_sum_sp, p_sum_rep, orthogonal)):
            pl.when(j == at)(stage)
        ready = j >= P_AT[-1]

        pl.when(j == 2)(lambda: complete(0, ready))
        pl.when((j > 2) & (j <= CHUNKS) & even)(lambda: over(j - 3, 2, lambda k: complete(k, ready)))
        pl.when(j == P_AT[-1])(lambda: over(0, EARLY, add_q))

        return carry

    lax.fori_loop(0, CHUNKS + 1, step, 0)
    last_own()
    last_sum()

    lines = rank // count_rep
    q_lines = q_sum[...].T
    for i in range(count_rep):
        q_src[i] = q_lines[i * lines : (i + 1) * lines]
    for d in range(1, count_rep):
        q_scatter(d).start()
    acc = q_src[rep]
    for d in range(1, count_rep):
        q_scatter(d).wait_recv()
        acc = acc + q_got[d - 1]
    q_next[rep] = acc * (1.0 / count_rep)
    for d in range(1, count_rep):
        q_gather(d).start()
    complete_last()
    for d in range(1, count_rep):
        q_gather_in(d).wait_recv()

    def finish(j, carry):
        for side in range(2):
            direct(j, side).wait_send()
            forward(j, side).wait_send()
            for group in range(3):
                far(j, side, group).wait_send()
                near(j, side, group).wait_send()
        mem_out(j).wait()
        return carry

    lax.fori_loop(0, CHUNKS, finish, 0)
    for side in range(2):
        frames_near(side).wait_send()
        frames_far(side).wait_send()
        frames_on(side).wait_send()
        t_far(side).wait_send()
        t_out(side).wait_send()
    for step_ in (1, 3, 2):
        q_out(step_).wait_send()
        x_out(step_).wait_send()
    for d in range(1, count_sp):
        p_scatter(d).wait_send()
        p_gather(d).wait_send()
    for d in range(1, count_rep):
        p_share(d).wait_send()
        q_scatter(d).wait_send()
        q_gather(d).wait_send()


def compressed_step(count_rep, frames, g, err, q_own):
    band, chans = g.shape
    width = band // 4
    rows = err.shape[0]
    rank = q_own.shape[0]
    count_sp = RING * RING
    share = chans // count_sp
    per_side = share // 2
    dma = pltpu.SemaphoreType.DMA
    two, three = dma((CHUNKS, 2)), dma((CHUNKS, 2, 3))
    f32, bf16 = jnp.float32, jnp.bfloat16
    any_spec, vmem_spec = pl.BlockSpec(memory_space=pl.ANY), pl.BlockSpec(memory_space=pltpu.VMEM)
    p_block = (rank // 2, COLS)
    q_block = (rank // count_rep, rows)
    return pl.pallas_call(
        functools.partial(step_kernel, count_rep),
        out_shape=(
            jax.ShapeDtypeStruct((rows, chans), f32),
            jax.ShapeDtypeStruct((count_rep, *q_block), f32),
            jax.ShapeDtypeStruct((6 * rank, chans), bf16),
        ),
        in_specs=[any_spec, any_spec, any_spec, vmem_spec],
        out_specs=(any_spec, vmem_spec, vmem_spec),
        scratch_shapes=[
            pltpu.VMEM((chans // COLS, band, COLS), bf16),
            pltpu.VMEM((2, RING // 2, share, band), bf16),
            pltpu.VMEM((2, rank // 2, band), f32),
            pltpu.VMEM((rows, 128), f32),
            pltpu.VMEM((TAPS, share, 128), bf16),
            pltpu.VMEM((RING, RING, share, band), bf16),
            pltpu.VMEM((RING, RING, share, band), bf16),
            pltpu.VMEM((2, RING, share, width), bf16),
            pltpu.VMEM((3, RING * share, RING * band + 2 * width), bf16),
            pltpu.VMEM((CHUNKS, RING * band, COLS), bf16),
            pltpu.VMEM((CHUNKS, RING, 2, TAPS, per_side, COLS), f32),
            pltpu.VMEM((CHUNKS, 2, TAPS, per_side, COLS), f32),
            pltpu.VMEM((CHUNKS, 2, 2, TAPS, per_side, COLS), f32),
            pltpu.VMEM((CHUNKS, rows, COLS), f32),
            pltpu.VMEM((TAPS, RING, share, 128), bf16),
            pltpu.VMEM((TAPS * 3 * rank, RING * share), bf16),
            pltpu.VMEM((3, RING * band // width + 4, rank, width), f32),
            pltpu.VMEM((RING, rank, band), f32),
            pltpu.VMEM((2, rank, band), f32),
            pltpu.VMEM((count_sp, *p_block), f32),
            pltpu.VMEM((count_sp - 1, *p_block), f32),
            pltpu.VMEM(p_block, f32),
            pltpu.VMEM((count_rep, *p_block), f32),
            pltpu.VMEM((count_sp, *p_block), f32),
            pltpu.VMEM((rank, 128), f32),
            pltpu.VMEM((count_rep, *q_block), f32),
            pltpu.VMEM((count_rep - 1, *q_block), f32),
            pltpu.VMEM((rows, 128), f32),
            pltpu.VMEM((RING - 1, rank, rows), f32),
            pltpu.VMEM((RING - 1, rank, rows), f32),
            dma((chans // COLS,)), dma((6,)), dma((6,)), dma, dma((2,)), dma((2,)), dma((CHUNKS,)), dma((CHUNKS,)),
            two, two, two, two, three, three, three, three, dma((CHUNKS,)),
            dma((3,)), dma((3,)), dma, dma((4,)), dma((4,)),
            dma((count_sp - 1,)), dma((count_sp - 1,)), dma((count_rep - 1,)), dma((count_rep - 1,)),
            dma((count_sp - 1,)), dma((count_sp - 1,)), dma((count_rep - 1,)), dma((count_rep - 1,)),
            dma((count_rep - 1,)), dma((count_rep - 1,)), dma((3,)), dma((3,)),
        ],
        compiler_params=pltpu.CompilerParams(
            collective_id=0, has_side_effects=True, vmem_limit_bytes=58 * 1024 * 1024
        ),
        cost_estimate=pl.CostEstimate(flops=2 * rows * 16 * chans * band, bytes_accessed=10**7, transcendentals=0),
        name="compressed_step",
    )(frames, g, err, q_own)


def feedback_kernel(memory, q_parts, p_side, error_next, q_next, q_side):
    count, lines, rows = q_parts.shape
    block = memory.shape[0]

    @pl.when(pl.program_id(0) == 0)
    def _():
        for i in range(count):
            q_next[i * lines : (i + 1) * lines] = q_parts[i]
        q0, q1, q2 = split(q_next[...])
        q_side[...] = jnp.concatenate([q0, q0, q0, q1, q1, q2], axis=0).T

    at = pl.ds(pl.multiple_of(pl.program_id(0) * block, block), block)
    error_next[...] = memory[...] - jnp.dot(q_side[at, :], p_side[...], preferred_element_type=jnp.float32)


def feedback(memory, q_parts, p_side):
    rows, chans = memory.shape
    count, lines, _ = q_parts.shape
    rank = count * lines
    block = (rows // 4, chans)
    return pl.pallas_call(
        feedback_kernel,
        grid=(rows // block[0],),
        out_shape=(jax.ShapeDtypeStruct(memory.shape, jnp.float32), jax.ShapeDtypeStruct((rank, rows), jnp.float32)),
        in_specs=[
            pl.BlockSpec(block, lambda i: (i, 0)),
            pl.BlockSpec(q_parts.shape, lambda i: (0, 0, 0)),
            pl.BlockSpec(p_side.shape, lambda i: (0, 0)),
        ],
        out_specs=(pl.BlockSpec(block, lambda i: (i, 0)), pl.BlockSpec((rank, rows), lambda i: (0, 0))),
        scratch_shapes=[pltpu.VMEM((rows, 6 * rank), jnp.bfloat16)],
        compiler_params=pltpu.CompilerParams(vmem_limit_bytes=60 * 1024 * 1024),
        name="feedback",
    )(memory, q_parts, p_side)


def per_device(count_rep, frames, out_grad, error_prev, q_prev):
    band_rows, width, chans = frames.shape[1:]
    band = band_rows * width
    memory, q_parts, p_side = compressed_step(
        count_rep,
        frames[0].reshape(band, chans),
        out_grad[0].reshape(band, chans),
        error_prev[0],
        q_prev,
    )
    error_next, q_next = feedback(memory, q_parts, p_side)
    return (error_next[None], q_next)


def solution(mesh):
    placed = (
        P("rep", "sp", None, None),
        P("rep", "sp", None, None),
        P("rep", "sp", None),
        P(None, "sp"),
    )
    return jax.shard_map(
        functools.partial(per_device, mesh.shape["rep"]),
        mesh=mesh,
        in_specs=placed,
        out_specs=(P("rep", "sp", None), P(None, "sp")),
        check_vma=False,
    )
```

```python
import functools

import jax
import jax.numpy as jnp
from jax import lax
from jax.experimental import pallas as pl
from jax.experimental.pallas import tpu as pltpu
from jax.sharding import PartitionSpec as P

MESH = pl.DeviceIdType.MESH
RING = 4
CHUNKS = 8
COLS = 128
TAPS = 9
T_AT = 0
P_AT = (2, 3, 4, 5)
EARLY = 3


def sp_at(x, z):
    return {"sp": lax.rem(x + RING, RING) * RING + lax.rem(z + RING, RING)}


def remote(src, dst, send, recv, device):
    return pltpu.make_async_remote_copy(
        src_ref=src, dst_ref=dst, send_sem=send, recv_sem=recv, device_id=device, device_id_type=MESH
    )


def split(value):
    high = value.astype(jnp.bfloat16)
    rest = value - high.astype(jnp.float32)
    middle = rest.astype(jnp.bfloat16)
    low = (rest - middle.astype(jnp.float32)).astype(jnp.bfloat16)
    return high, middle, low


def exact_dot(a, b, contract):
    return lax.dot_general(
        a, b, (contract, ((), ())), precision=lax.Precision.HIGHEST, preferred_element_type=jnp.float32
    )


def step_kernel(
    count_rep, frames, g, err, q_own, memory, q_next, p_side,
    local, f_relay, t_relay, q_turned, q_taps, flipped, raw, halo, taps, gbuf, part, relay, piece, total,
    q_near, q_flip, t_term, t_near, p_src, p_near, p_one, p_far, p_all, work, q_src, q_got, q_sum, x_term, x_got,
    l_in, f_send, f_recv, f_own, h_send, h_recv, e_in, g_own,
    d_send, d_recv, r_send, r_recv, a_send, a_recv, b_send, b_recv, out_sem,
    q_send, q_recv, q_copy, t_send, t_recv, s1, r1, s2, r2, s3, r3, s4, r4, s5, r5, x_send, x_recv,
):
    sp, rep = lax.axis_index("sp"), lax.axis_index("rep")
    x, z = sp // RING, lax.rem(sp, RING)
    up, down = sp_at(x, z + 1), sp_at(x, z - 1)
    right, left = sp_at(x + 1, z), sp_at(x - 1, z)
    z_up, z_down = lax.rem(z + 1, RING), lax.rem(z + 3, RING)
    x_right, x_left, x_far = lax.rem(x + 1, RING), lax.rem(x + 3, RING), lax.rem(x + 2, RING)
    band = g.shape[0]
    half = band // 2
    count_sp = RING * RING
    share = part.shape[4] * 2
    width = halo.shape[3]
    rank = q_own.shape[0]

    def at_sp(d):
        return {"sp": lax.rem(sp + d, count_sp)}

    def at_rep(d):
        return {"rep": lax.rem(rep + d, count_rep)}

    near_z, far_z = (z_up, z_down), lax.rem(z + 2, RING)
    towards = (up, down)
    some_x = RING // 2

    def frames_near(side):
        return remote(flipped.at[:, near_z[side]], raw.at[z], f_send.at[side], f_recv.at[side], towards[side])

    def frames_near_in(side):
        return remote(flipped.at[:, z], raw.at[near_z[1 - side]], f_send.at[side], f_recv.at[side], up)

    def frames_far(side):
        part_x = pl.ds(side * some_x, some_x)
        return remote(
            flipped.at[part_x, far_z], f_relay.at[side], f_send.at[2 + side], f_recv.at[2 + side], towards[side]
        )

    def frames_on(side):
        part_x = pl.ds(side * some_x, some_x)
        return remote(
            f_relay.at[side], raw.at[near_z[1 - side], part_x], f_send.at[4 + side], f_recv.at[4 + side], towards[side]
        )

    def frames_far_in(side):
        part_x = pl.ds(side * some_x, some_x)
        return remote(f_relay.at[side], raw.at[far_z, part_x], f_send.at[4 + side], f_recv.at[4 + side], up)

    def columns(j):
        return pl.ds(pl.multiple_of(j * COLS, COLS), COLS)

    def slot(which, first, count):
        return pl.ds(pl.multiple_of(which * band + first, half), count)

    def own_grad(j):
        return pltpu.make_async_copy(g.at[:, columns(j)], gbuf.at[j, slot(z, 0, band)], g_own.at[j])

    def direct(j, side):
        ref = gbuf.at[j, slot(z, 0, band)]
        return remote(ref, ref, d_send.at[j, side], d_recv.at[j, side], up if side == 0 else down)

    def direct_in(j, side):
        ref = gbuf.at[j, slot(z_down if side == 0 else z_up, 0, band)]
        return remote(ref, ref, d_send.at[j, side], d_recv.at[j, side], up)

    def forward(j, side):
        ref = gbuf.at[j, slot(z_down if side == 0 else z_up, side * half, half)]
        return remote(ref, ref, r_send.at[j, side], r_recv.at[j, side], up if side == 0 else down)

    def forward_in(j, side):
        ref = gbuf.at[j, slot(lax.rem(z + 2, RING), side * half, half)]
        return remote(ref, ref, r_send.at[j, side], r_recv.at[j, side], up)

    def err_in(j):
        return pltpu.make_async_copy(err.at[:, columns(j)], total.at[j], e_in.at[j])

    def mem_out(j):
        return pltpu.make_async_copy(total.at[j], memory.at[:, columns(j)], out_sem.at[j])

    def far(j, side):
        return remote(
            part.at[j, x_far, side], relay.at[j, side], a_send.at[j, side], a_recv.at[j, side],
            right if side == 0 else left,
        )

    def near(j, side):
        return remote(
            part.at[j, x_right if side == 0 else x_left], piece.at[j, side], b_send.at[j, side], b_recv.at[j, side],
            right if side == 0 else left,
        )

    def q_out(step):
        return remote(q_taps, q_near.at[:, x], q_send.at[step - 1], q_recv.at[step - 1], sp_at(x + step, z))

    def q_in(step):
        source = lax.rem(x + RING - step, RING)
        return remote(q_taps, q_near.at[:, source], q_send.at[step - 1], q_recv.at[step - 1], right)

    def t_far(side):
        some = pl.ds(side * (rank // 2), rank // 2)
        return remote(t_term.at[far_z, some], t_relay.at[side], t_send.at[side], t_recv.at[side], towards[side])

    def t_out(side):
        return remote(
            t_term.at[near_z[side]], t_near.at[side], t_send.at[2 + side], t_recv.at[2 + side], towards[side]
        )

    def p_scatter(d):
        return remote(p_src.at[lax.rem(sp + d, count_sp)], p_near.at[d - 1], s1.at[d - 1], r1.at[d - 1], at_sp(d))

    def p_share(d):
        return remote(p_one, p_far.at[rep], s2.at[d - 1], r2.at[d - 1], at_rep(d))

    def p_share_in(d):
        source = lax.rem(rep + count_rep - d, count_rep)
        return remote(p_one, p_far.at[source], s2.at[d - 1], r2.at[d - 1], at_rep(d))

    def p_gather(d):
        return remote(p_all.at[sp], p_all.at[sp], s3.at[d - 1], r3.at[d - 1], at_sp(d))

    def p_gather_in(d):
        ref = p_all.at[lax.rem(sp + count_sp - d, count_sp)]
        return remote(ref, ref, s3.at[d - 1], r3.at[d - 1], at_sp(d))

    def x_out(step):
        return remote(x_term.at[step - 1], x_got.at[step - 1], x_send.at[step - 1], x_recv.at[step - 1], sp_at(x + step, z))

    def q_scatter(d):
        return remote(q_src.at[lax.rem(rep + d, count_rep)], q_got.at[d - 1], s4.at[d - 1], r4.at[d - 1], at_rep(d))

    def q_gather(d):
        return remote(q_next.at[rep], q_next.at[rep], s5.at[d - 1], r5.at[d - 1], at_rep(d))

    def q_gather_in(d):
        ref = q_next.at[lax.rem(rep + count_rep - d, count_rep)]
        return remote(ref, ref, s5.at[d - 1], r5.at[d - 1], at_rep(d))

    barrier = pltpu.get_barrier_semaphore()
    for d in range(1, count_sp):
        pl.semaphore_signal(barrier, inc=1, device_id=at_sp(d), device_id_type=MESH)
    for d in range(1, count_rep):
        pl.semaphore_signal(barrier, inc=1, device_id=at_rep(d), device_id_type=MESH)

    def column_in(i):
        return pltpu.make_async_copy(frames.at[:, columns(i)], local.at[i], l_in.at[i])

    pairs = frames.shape[1] // COLS
    owners = COLS // share
    own_grad(0).start()
    for i in range(pairs):
        column_in(i).start()
    pl.semaphore_wait(barrier, count_sp + count_rep - 2)
    own_grad(0).wait()
    direct(0, 0).start()
    direct(0, 1).start()

    per_x = RING // owners
    for first in range(per_x):
        for i in range(first, pairs, per_x):
            column_in(i).wait()
            turned = local[i].T
            for k in range(owners):
                owner = i * owners + k
                flipped[owner // RING, owner % RING] = turned[k * share : (k + 1) * share]
    for side in range(2):
        frames_far(side).start()
    for side in range(2):
        frames_near(side).start()
    own_frames = pltpu.make_async_copy(flipped.at[:, z], raw.at[z], f_own)
    own_frames.start()
    for j in range(CHUNKS):
        err_in(j).start()
    for j in range(1, CHUNKS):
        own_grad(j).start()

    thirds = [third.astype(jnp.float32) for third in split(q_own[...])]
    lanes = q_taps.shape[2]
    thirds.append(jnp.zeros((lanes - 3 * rank, q_own.shape[1]), jnp.float32))
    q_turned[...] = jnp.concatenate(thirds, axis=0).T
    for tap in range(TAPS):
        q_taps[tap] = q_turned[pl.ds(tap, share, stride=TAPS), :].astype(jnp.bfloat16)
    for step in (1, 3, 2):
        q_out(step).start()
    own_q = pltpu.make_async_copy(q_taps, q_near.at[:, x], q_copy)
    own_q.start()

    lane = lax.broadcasted_iota(jnp.int32, (RING * share, width), 1)

    def place(row, value):
        at = pl.ds(pl.multiple_of(row * width, width), width)
        wide = value.astype(jnp.float32)
        taps[0, :, at] = jnp.where(lane == 0, 0.0, pltpu.roll(wide, 1, 1)).astype(taps.dtype)
        taps[1, :, at] = value
        taps[2, :, at] = jnp.where(lane == width - 1, 0.0, pltpu.roll(wide, width - 1, 1)).astype(taps.dtype)

    def place_band(which):
        def place_row(row, carry):
            at = pl.ds(pl.multiple_of(row * width, width), width)
            place(which * (band // width) + row + 1, raw[which, :, :, at].reshape(RING * share, width))
            return carry

        lax.fori_loop(0, band // width, place_row, 0)

    def start_forward(j):
        for side in range(2):
            direct_in(j, side).wait_recv()
            forward(j, side).start()

    def start_direct(j):
        for side in range(2):
            direct(j, side).start()

    own_frames.wait()
    place_band(z)
    start_forward(0)
    for j in range(1, CHUNKS):
        own_grad(j).wait()

    for j in range(CHUNKS):
        err_in(j).wait()
        term = exact_dot(q_own[...], total[j], ((1,), (0,)))
        for h in range(2):
            p_src[2 * j + h] = term[h * (rank // 2) : (h + 1) * (rank // 2)]

    for side in range(2):
        frames_far(side).wait_recv()
        frames_on(side).start()
    for side in range(2):
        frames_near_in(side).wait_recv()
    start_direct(1)
    place_band(z_down)
    place_band(z_up)
    for side in range(2):
        frames_far_in(side).wait_recv()

    bottom = raw.at[RING - 1, :, :, band - width : band]
    above = remote(bottom, halo.at[0], h_send.at[0], h_recv.at[0], right)
    below = remote(raw.at[0, :, :, 0:width], halo.at[1], h_send.at[1], h_recv.at[1], left)
    above.start()
    below.start()
    place_band(lax.rem(z + 2, RING))
    rows = RING * band // width
    above.wait()
    below.wait()
    zero = jnp.zeros((RING * share, width), halo.dtype)
    place(0, jnp.where(x == 0, zero, halo[0].reshape(RING * share, width)))
    place(rows + 1, jnp.where(x == RING - 1, zero, halo[1].reshape(RING * share, width)))

    def t_band(which):
        acc = None
        for a in range(3):
            at = pl.ds(pl.multiple_of(which * band + a * width, width), band)
            stacked = taps[:, :, at].reshape(3 * RING * share, band)
            term = jnp.dot(q_flip[a], stacked, preferred_element_type=jnp.float32)
            acc = term if acc is None else acc + term
        t_term[which] = acc[:rank] + (acc[rank : 2 * rank] + acc[2 * rank : 3 * rank])

    def t_start():
        own_q.wait()
        for step in (1, 3, 2):
            q_in(step).wait_recv()
        for a in range(3):
            q_flip[a] = q_near[3 * a : 3 * a + 3].reshape(3 * RING * share, lanes).T

    def t_bands(first):
        def one(i, carry):
            t_band(first + i)
            return carry

        lax.fori_loop(0, RING // 2, one, 0)

    def t_finish():
        for side in range(2):
            t_far(side).start()

    def t_pass_on():
        for side in range(2):
            some = pl.ds(side * (rank // 2), rank // 2)
            t_far(side).wait_recv()
            t_term[near_z[side], some] = t_term[near_z[side], some] + t_relay[side]
            t_out(side).start()

    def p_terms():
        for side in range(2):
            t_out(side).wait_recv()
        full = t_term[z] + (t_near[0] + t_near[1])
        parts = jnp.concatenate(split(full), axis=0)

        def add(j, carry):
            acc = jnp.dot(parts, gbuf[j, slot(z, 0, band)], preferred_element_type=jnp.float32)
            term = acc[:rank] + (acc[rank : 2 * rank] + acc[2 * rank :])
            for h in range(2):
                p_src[2 * j + h] = p_src[2 * j + h] + term[h * (rank // 2) : (h + 1) * (rank // 2)]
            return carry

        lax.fori_loop(0, CHUNKS, add, 0)
        for d in range(1, count_sp):
            p_scatter(d).start()

    def p_sum_sp():
        acc = p_src[sp]
        for d in range(1, count_sp):
            p_scatter(d).wait_recv()
            acc = acc + p_near[d - 1]
        p_one[...] = acc
        p_far[rep] = acc
        for d in range(1, count_rep):
            p_share(d).start()

    def p_sum_rep():
        for d in range(1, count_rep):
            p_share_in(d).wait_recv()
        acc = p_far[0]
        for i in range(1, count_rep):
            acc = acc + p_far[i]
        p_all[sp] = acc
        for d in range(1, count_sp):
            p_gather(d).start()

    def p_chunk(j):
        return jnp.concatenate([p_all[2 * j], p_all[2 * j + 1]], axis=0)

    def orthogonal():
        for d in range(1, count_sp):
            p_gather_in(d).wait_recv()
        p_total = jnp.concatenate([p_chunk(j) for j in range(CHUNKS)], axis=1)
        gram = exact_dot(p_total, p_total, ((1,), (1,)))
        row_at = lax.broadcasted_iota(jnp.int32, (rank, rank), 0)
        col_at = lax.broadcasted_iota(jnp.int32, (rank, rank), 1)
        work[:, :rank] = gram
        work[:, rank : 2 * rank] = jnp.where(row_at == col_at, 1.0, 0.0)
        shape = (rank, 2 * rank)
        line = lax.broadcasted_iota(jnp.int32, shape, 0)
        spot = lax.broadcasted_iota(jnp.int32, shape, 1)

        def eliminate(k, carry):
            state = work[:, : 2 * rank]
            pivot = work[pl.ds(k, 1), : 2 * rank]
            column = jnp.sum(jnp.where(spot == k, state, 0.0), axis=1, keepdims=True)
            diagonal = jnp.sum(jnp.where(spot[:1] == k, pivot, 0.0), axis=1, keepdims=True)
            inverse = 1.0 / jnp.sqrt(diagonal)
            pivot = pivot * inverse
            work[:, : 2 * rank] = jnp.where(
                line > k, state - (column * inverse) * pivot, jnp.where(line == k, pivot, state)
            )
            return carry

        lax.fori_loop(0, rank, eliminate, 0)
        lower_inverse = jnp.where(col_at <= row_at, work[:, rank : 2 * rank], 0.0)
        whole = exact_dot(lower_inverse, p_total, ((1,), (0,)))
        p0, p1, p2 = split(whole)
        p_side[...] = jnp.concatenate([p0, p1, p2, p0, p1, p0], axis=0)
        q_sum[...] = jnp.zeros_like(q_sum)

    def by_p(rows_of, k):
        m0, m1, m2 = split(rows_of)
        m_side = jnp.concatenate([m0, m0, m0, m1, m1, m2], axis=1)
        across = jnp.concatenate([p_side[i * rank : (i + 1) * rank, columns(k)] for i in range(6)], axis=1)
        return jnp.dot(m_side, across.T, preferred_element_type=jnp.float32)

    def add_q(k):
        q_sum[:, :rank] = q_sum[:, :rank] + by_p(total[k], k)

    last = CHUNKS - 1

    def last_terms():
        for step in (1, 3, 2):
            owner = lax.rem(x + step, RING)
            terms = by_p(part[last, owner].reshape(q_sum.shape[0], COLS), last)
            x_term[step - 1] = terms.T
            x_out(step).start()

    def last_own():
        count = part.shape[4]
        for side in range(2):
            for tap in range(TAPS):
                at = pl.ds(side * count * TAPS + tap, count, stride=TAPS)
                total[last, at, :] = total[last, at, :] + part[last, x, side, tap]
        add_q(last)

    def last_sum():
        for step in (1, 3, 2):
            x_out(step).wait_recv()
        got = x_got[0] + x_got[1] + x_got[2]
        filled = jnp.concatenate([got, jnp.zeros((128 - rank, got.shape[1]), jnp.float32)], axis=0).T
        count = part.shape[4]
        for side in range(2):
            for tap in range(TAPS):
                at = pl.ds(side * count * TAPS + tap, count, stride=TAPS)
                line = (side * TAPS + tap) * count
                q_sum[at, :] = q_sum[at, :] + filled[line : line + count]

    def multiply(first, count, after):
        depth = gbuf.shape[1]
        per_side = part.shape[4]

        def one(a, carry):
            at = pl.ds(pl.multiple_of(a * width, width), depth)
            stacked = taps[:, :, at].reshape(3 * RING * share, depth)
            chosen = gbuf[first] if count == 1 else jnp.concatenate([gbuf[first], gbuf[first + 1]], axis=1)
            product = jnp.dot(stacked, chosen, preferred_element_type=jnp.float32)
            for c in range(count):
                for b in range(3):
                    for owner in range(RING):
                        for side in range(2):
                            line = b * RING * share + (owner * 2 + side) * per_side
                            part[first + c, owner, side, a * 3 + b] = product[
                                line : line + per_side, c * COLS : (c + 1) * COLS
                            ]
            @pl.when((a == 0) & (after < CHUNKS))
            def _():
                start_forward(after)

            return carry

        lax.fori_loop(0, 3, one, 0)
        for c in range(count):
            far(first + c, 0).start()
            far(first + c, 1).start()

    def pass_on(k):
        far(k, 0).wait_recv()
        part[k, x_right, 0] = part[k, x_right, 0] + relay[k, 0]
        near(k, 0).start()
        far(k, 1).wait_recv()
        part[k, x_left, 1] = part[k, x_left, 1] + relay[k, 1]
        near(k, 1).start()

    def complete(k, with_q):
        near(k, 0).wait_recv()
        near(k, 1).wait_recv()
        count = part.shape[4]
        for side in range(2):
            for tap in range(TAPS):
                at = pl.ds(side * count * TAPS + tap, count, stride=TAPS)
                total[k, at, :] = (
                    total[k, at, :] + part[k, x, side, tap] + (piece[k, 0, side, tap] + piece[k, 1, side, tap])
                )
        mem_out(k).start()
        pl.when(with_q)(lambda: add_q(k))

    def complete_last():
        near(last, 0).wait_recv()
        near(last, 1).wait_recv()
        count = part.shape[4]
        for side in range(2):
            for tap in range(TAPS):
                at = pl.ds(side * count * TAPS + tap, count, stride=TAPS)
                total[last, at, :] = total[last, at, :] + (piece[last, 0, side, tap] + piece[last, 1, side, tap])
        mem_out(last).start()

    def over(first, count, body):
        def one(i, carry):
            body(first + i)
            return carry

        lax.fori_loop(0, count, one, 0)

    def step(j, carry):
        @pl.when(j + 2 < CHUNKS)
        def _():
            start_direct(j + 2)

        @pl.when(j < CHUNKS)
        def _():
            forward_in(j, 0).wait_recv()
            forward_in(j, 1).wait_recv()

        alone = (j == 0) | (j == CHUNKS - 1)
        even = lax.rem(j, 2) == 0
        pl.when(alone)(lambda: multiply(j, 1, j + 1))
        pl.when((j > 0) & (j < CHUNKS - 1) & even)(lambda: multiply(j - 1, 2, j + 1))
        pl.when((j < CHUNKS - 1) & jnp.logical_not(even))(lambda: start_forward(j + 1))

        pl.when((j == 1) | (j == CHUNKS))(lambda: pass_on(j - 1))
        pl.when((j > 1) & (j < CHUNKS) & jnp.logical_not(even))(lambda: over(j - 2, 2, pass_on))

        @pl.when(j == T_AT)
        def _():
            t_start()
            t_bands(0)
            t_bands(RING // 2)
            t_finish()

        pl.when(j == T_AT + 1)(t_pass_on)
        pl.when(j == last)(last_terms)

        for at, stage in zip(P_AT, (p_terms, p_sum_sp, p_sum_rep, orthogonal)):
            pl.when(j == at)(stage)
        ready = j >= P_AT[-1]

        pl.when(j == 2)(lambda: complete(0, ready))
        pl.when((j > 2) & (j <= CHUNKS) & even)(lambda: over(j - 3, 2, lambda k: complete(k, ready)))
        pl.when(j == P_AT[-1])(lambda: over(0, EARLY, add_q))

        return carry

    lax.fori_loop(0, CHUNKS + 1, step, 0)
    last_own()
    last_sum()

    lines = rank // count_rep
    q_lines = q_sum[...].T
    for i in range(count_rep):
        q_src[i] = q_lines[i * lines : (i + 1) * lines]
    for d in range(1, count_rep):
        q_scatter(d).start()
    acc = q_src[rep]
    for d in range(1, count_rep):
        q_scatter(d).wait_recv()
        acc = acc + q_got[d - 1]
    q_next[rep] = acc * (1.0 / count_rep)
    for d in range(1, count_rep):
        q_gather(d).start()
    complete_last()
    for d in range(1, count_rep):
        q_gather_in(d).wait_recv()

    def finish(j, carry):
        for side in range(2):
            direct(j, side).wait_send()
            forward(j, side).wait_send()
            far(j, side).wait_send()
            near(j, side).wait_send()
        mem_out(j).wait()
        return carry

    lax.fori_loop(0, CHUNKS, finish, 0)
    for side in range(2):
        frames_near(side).wait_send()
        frames_far(side).wait_send()
        frames_on(side).wait_send()
        t_far(side).wait_send()
        t_out(side).wait_send()
    for step_ in (1, 3, 2):
        q_out(step_).wait_send()
        x_out(step_).wait_send()
    for d in range(1, count_sp):
        p_scatter(d).wait_send()
        p_gather(d).wait_send()
    for d in range(1, count_rep):
        p_share(d).wait_send()
        q_scatter(d).wait_send()
        q_gather(d).wait_send()


def compressed_step(count_rep, frames, g, err, q_own):
    band, chans = g.shape
    width = band // 4
    rows = err.shape[0]
    rank = q_own.shape[0]
    count_sp = RING * RING
    share = chans // count_sp
    per_side = share // 2
    dma = pltpu.SemaphoreType.DMA
    two = dma((CHUNKS, 2))
    f32, bf16 = jnp.float32, jnp.bfloat16
    any_spec, vmem_spec = pl.BlockSpec(memory_space=pl.ANY), pl.BlockSpec(memory_space=pltpu.VMEM)
    p_block = (rank // 2, COLS)
    q_block = (rank // count_rep, rows)
    return pl.pallas_call(
        functools.partial(step_kernel, count_rep),
        out_shape=(
            jax.ShapeDtypeStruct((rows, chans), f32),
            jax.ShapeDtypeStruct((count_rep, *q_block), f32),
            jax.ShapeDtypeStruct((6 * rank, chans), bf16),
        ),
        in_specs=[any_spec, any_spec, any_spec, vmem_spec],
        out_specs=(any_spec, vmem_spec, vmem_spec),
        scratch_shapes=[
            pltpu.VMEM((chans // COLS, band, COLS), bf16),
            pltpu.VMEM((2, RING // 2, share, band), bf16),
            pltpu.VMEM((2, rank // 2, band), f32),
            pltpu.VMEM((rows, 128), f32),
            pltpu.VMEM((TAPS, share, 128), bf16),
            pltpu.VMEM((RING, RING, share, band), bf16),
            pltpu.VMEM((RING, RING, share, band), bf16),
            pltpu.VMEM((2, RING, share, width), bf16),
            pltpu.VMEM((3, RING * share, RING * band + 2 * width), bf16),
            pltpu.VMEM((CHUNKS, RING * band, COLS), bf16),
            pltpu.VMEM((CHUNKS, RING, 2, TAPS, per_side, COLS), f32),
            pltpu.VMEM((CHUNKS, 2, TAPS, per_side, COLS), f32),
            pltpu.VMEM((CHUNKS, 2, 2, TAPS, per_side, COLS), f32),
            pltpu.VMEM((CHUNKS, rows, COLS), f32),
            pltpu.VMEM((TAPS, RING, share, 128), bf16),
            pltpu.VMEM((3, 128, 3 * RING * share), bf16),
            pltpu.VMEM((RING, rank, band), f32),
            pltpu.VMEM((2, rank, band), f32),
            pltpu.VMEM((count_sp, *p_block), f32),
            pltpu.VMEM((count_sp - 1, *p_block), f32),
            pltpu.VMEM(p_block, f32),
            pltpu.VMEM((count_rep, *p_block), f32),
            pltpu.VMEM((count_sp, *p_block), f32),
            pltpu.VMEM((rank, 128), f32),
            pltpu.VMEM((count_rep, *q_block), f32),
            pltpu.VMEM((count_rep - 1, *q_block), f32),
            pltpu.VMEM((rows, 128), f32),
            pltpu.VMEM((RING - 1, rank, rows), f32),
            pltpu.VMEM((RING - 1, rank, rows), f32),
            dma((chans // COLS,)), dma((6,)), dma((6,)), dma, dma((2,)), dma((2,)), dma((CHUNKS,)), dma((CHUNKS,)),
            two, two, two, two, two, two, two, two, dma((CHUNKS,)),
            dma((3,)), dma((3,)), dma, dma((4,)), dma((4,)),
            dma((count_sp - 1,)), dma((count_sp - 1,)), dma((count_rep - 1,)), dma((count_rep - 1,)),
            dma((count_sp - 1,)), dma((count_sp - 1,)), dma((count_rep - 1,)), dma((count_rep - 1,)),
            dma((count_rep - 1,)), dma((count_rep - 1,)), dma((3,)), dma((3,)),
        ],
        compiler_params=pltpu.CompilerParams(
            collective_id=0, has_side_effects=True, vmem_limit_bytes=58 * 1024 * 1024
        ),
        cost_estimate=pl.CostEstimate(flops=2 * rows * 16 * chans * band, bytes_accessed=10**7, transcendentals=0),
        name="compressed_step",
    )(frames, g, err, q_own)


def feedback_kernel(memory, q_parts, p_side, error_next, q_next, q_side):
    count, lines, rows = q_parts.shape
    block = memory.shape[0]

    @pl.when(pl.program_id(0) == 0)
    def _():
        for i in range(count):
            q_next[i * lines : (i + 1) * lines] = q_parts[i]
        q0, q1, q2 = split(q_next[...])
        q_side[...] = jnp.concatenate([q0, q0, q0, q1, q1, q2], axis=0).T

    at = pl.ds(pl.multiple_of(pl.program_id(0) * block, block), block)
    error_next[...] = memory[...] - jnp.dot(q_side[at, :], p_side[...], preferred_element_type=jnp.float32)


def feedback(memory, q_parts, p_side):
    rows, chans = memory.shape
    count, lines, _ = q_parts.shape
    rank = count * lines
    block = (rows // 4, chans)
    return pl.pallas_call(
        feedback_kernel,
        grid=(rows // block[0],),
        out_shape=(jax.ShapeDtypeStruct(memory.shape, jnp.float32), jax.ShapeDtypeStruct((rank, rows), jnp.float32)),
        in_specs=[
            pl.BlockSpec(block, lambda i: (i, 0)),
            pl.BlockSpec(q_parts.shape, lambda i: (0, 0, 0)),
            pl.BlockSpec(p_side.shape, lambda i: (0, 0)),
        ],
        out_specs=(pl.BlockSpec(block, lambda i: (i, 0)), pl.BlockSpec((rank, rows), lambda i: (0, 0))),
        scratch_shapes=[pltpu.VMEM((rows, 6 * rank), jnp.bfloat16)],
        compiler_params=pltpu.CompilerParams(vmem_limit_bytes=60 * 1024 * 1024),
        name="feedback",
    )(memory, q_parts, p_side)


def per_device(count_rep, frames, out_grad, error_prev, q_prev):
    band_rows, width, chans = frames.shape[1:]
    band = band_rows * width
    memory, q_parts, p_side = compressed_step(
        count_rep,
        frames[0].reshape(band, chans),
        out_grad[0].reshape(band, chans),
        error_prev[0],
        q_prev,
    )
    error_next, q_next = feedback(memory, q_parts, p_side)
    return (error_next[None], q_next)


def solution(mesh):
    placed = (
        P("rep", "sp", None, None),
        P("rep", "sp", None, None),
        P("rep", "sp", None),
        P(None, "sp"),
    )
    return jax.shard_map(
        functools.partial(per_device, mesh.shape["rep"]),
        mesh=mesh,
        in_specs=placed,
        out_specs=(P("rep", "sp", None), P(None, "sp")),
        check_vma=False,
    )
```

```python
import functools

import jax
import jax.numpy as jnp
from jax import lax
from jax.experimental import pallas as pl
from jax.experimental.pallas import tpu as pltpu
from jax.sharding import PartitionSpec as P

MESH = pl.DeviceIdType.MESH
RING = 4
CHUNKS = 8
COLS = 128
TAPS = 9
T_AT = 0
P_AT = (2, 3, 4, 5)
EARLY = 3


def sp_at(x, z):
    return {"sp": lax.rem(x + RING, RING) * RING + lax.rem(z + RING, RING)}


def remote(src, dst, send, recv, device):
    return pltpu.make_async_remote_copy(
        src_ref=src, dst_ref=dst, send_sem=send, recv_sem=recv, device_id=device, device_id_type=MESH
    )


def split(value):
    high = value.astype(jnp.bfloat16)
    rest = value - high.astype(jnp.float32)
    middle = rest.astype(jnp.bfloat16)
    low = (rest - middle.astype(jnp.float32)).astype(jnp.bfloat16)
    return high, middle, low


def exact_dot(a, b, contract):
    return lax.dot_general(
        a, b, (contract, ((), ())), precision=lax.Precision.HIGHEST, preferred_element_type=jnp.float32
    )


SCALE_ROWS = 16
RANGE = 1024.0


def encode(block):
    largest = jnp.max(jnp.abs(block), axis=(0, 1), keepdims=True)
    scale = jnp.maximum(largest * 1.01, 1e-30).astype(jnp.bfloat16)
    size = jnp.abs(block) * (RANGE / scale.astype(jnp.float32))
    second = size * size
    fourth = second * second
    twelfth = fourth * fourth * fourth
    signed = jnp.where(block < 0, -twelfth, twelfth).astype(jnp.bfloat16)
    return signed, jnp.broadcast_to(scale, (SCALE_ROWS, block.shape[1]))


def decode(coded):
    count = coded.shape[0] - SCALE_ROWS
    signed = coded[:count].astype(jnp.float32)
    scale = coded[count : count + 1].astype(jnp.float32) * (1.0 / RANGE)
    size = jnp.abs(signed)
    value = jnp.exp(jnp.log(jnp.maximum(size, 1e-37)) * (1.0 / 12.0)) * scale
    value = jnp.where(size < 1e-37, 0.0, value)
    return jnp.where(signed < 0, -value, value)


def step_kernel(
    count_rep, frames, g, err, q_own, memory, q_next, p_side,
    local, f_relay, t_relay, q_turned, q_taps, flipped, raw, halo, taps, gbuf, part, far_code, near_code, relay, piece, total,
    q_near, q_flip, t_term, t_near, p_src, p_near, p_one, p_far, p_all, work, q_src, q_got, q_sum, x_term, x_got,
    l_in, f_send, f_recv, f_own, h_send, h_recv, e_in, g_own,
    d_send, d_recv, r_send, r_recv, a_send, a_recv, b_send, b_recv, out_sem,
    q_send, q_recv, q_copy, t_send, t_recv, s1, r1, s2, r2, s3, r3, s4, r4, s5, r5, x_send, x_recv,
):
    sp, rep = lax.axis_index("sp"), lax.axis_index("rep")
    x, z = sp // RING, lax.rem(sp, RING)
    up, down = sp_at(x, z + 1), sp_at(x, z - 1)
    right, left = sp_at(x + 1, z), sp_at(x - 1, z)
    z_up, z_down = lax.rem(z + 1, RING), lax.rem(z + 3, RING)
    x_right, x_left, x_far = lax.rem(x + 1, RING), lax.rem(x + 3, RING), lax.rem(x + 2, RING)
    band = g.shape[0]
    half = band // 2
    count_sp = RING * RING
    share = part.shape[4] * 2
    width = halo.shape[3]
    rank = q_own.shape[0]

    def at_sp(d):
        return {"sp": lax.rem(sp + d, count_sp)}

    def at_rep(d):
        return {"rep": lax.rem(rep + d, count_rep)}

    near_z, far_z = (z_up, z_down), lax.rem(z + 2, RING)
    towards = (up, down)
    some_x = RING // 2

    def frames_near(side):
        return remote(flipped.at[:, near_z[side]], raw.at[z], f_send.at[side], f_recv.at[side], towards[side])

    def frames_near_in(side):
        return remote(flipped.at[:, z], raw.at[near_z[1 - side]], f_send.at[side], f_recv.at[side], up)

    def frames_far(side):
        part_x = pl.ds(side * some_x, some_x)
        return remote(
            flipped.at[part_x, far_z], f_relay.at[side], f_send.at[2 + side], f_recv.at[2 + side], towards[side]
        )

    def frames_on(side):
        part_x = pl.ds(side * some_x, some_x)
        return remote(
            f_relay.at[side], raw.at[near_z[1 - side], part_x], f_send.at[4 + side], f_recv.at[4 + side], towards[side]
        )

    def frames_far_in(side):
        part_x = pl.ds(side * some_x, some_x)
        return remote(f_relay.at[side], raw.at[far_z, part_x], f_send.at[4 + side], f_recv.at[4 + side], up)

    def columns(j):
        return pl.ds(pl.multiple_of(j * COLS, COLS), COLS)

    def slot(which, first, count):
        return pl.ds(pl.multiple_of(which * band + first, half), count)

    def own_grad(j):
        return pltpu.make_async_copy(g.at[:, columns(j)], gbuf.at[j, slot(z, 0, band)], g_own.at[j])

    def direct(j, side):
        ref = gbuf.at[j, slot(z, 0, band)]
        return remote(ref, ref, d_send.at[j, side], d_recv.at[j, side], up if side == 0 else down)

    def direct_in(j, side):
        ref = gbuf.at[j, slot(z_down if side == 0 else z_up, 0, band)]
        return remote(ref, ref, d_send.at[j, side], d_recv.at[j, side], up)

    def forward(j, side):
        ref = gbuf.at[j, slot(z_down if side == 0 else z_up, side * half, half)]
        return remote(ref, ref, r_send.at[j, side], r_recv.at[j, side], up if side == 0 else down)

    def forward_in(j, side):
        ref = gbuf.at[j, slot(lax.rem(z + 2, RING), side * half, half)]
        return remote(ref, ref, r_send.at[j, side], r_recv.at[j, side], up)

    def err_in(j):
        return pltpu.make_async_copy(err.at[:, columns(j)], total.at[j], e_in.at[j])

    def mem_out(j):
        return pltpu.make_async_copy(total.at[j], memory.at[:, columns(j)], out_sem.at[j])

    def far(j, side):
        return remote(
            far_code.at[j, side], relay.at[j, side], a_send.at[j, side], a_recv.at[j, side],
            right if side == 0 else left,
        )

    def near(j, side):
        return remote(
            near_code.at[j, side], piece.at[j, side], b_send.at[j, side], b_recv.at[j, side],
            right if side == 0 else left,
        )

    def q_out(step):
        return remote(q_taps, q_near.at[:, x], q_send.at[step - 1], q_recv.at[step - 1], sp_at(x + step, z))

    def q_in(step):
        source = lax.rem(x + RING - step, RING)
        return remote(q_taps, q_near.at[:, source], q_send.at[step - 1], q_recv.at[step - 1], right)

    def t_far(side):
        some = pl.ds(side * (rank // 2), rank // 2)
        return remote(t_term.at[far_z, some], t_relay.at[side], t_send.at[side], t_recv.at[side], towards[side])

    def t_out(side):
        return remote(
            t_term.at[near_z[side]], t_near.at[side], t_send.at[2 + side], t_recv.at[2 + side], towards[side]
        )

    def p_scatter(d):
        return remote(p_src.at[lax.rem(sp + d, count_sp)], p_near.at[d - 1], s1.at[d - 1], r1.at[d - 1], at_sp(d))

    def p_share(d):
        return remote(p_one, p_far.at[rep], s2.at[d - 1], r2.at[d - 1], at_rep(d))

    def p_share_in(d):
        source = lax.rem(rep + count_rep - d, count_rep)
        return remote(p_one, p_far.at[source], s2.at[d - 1], r2.at[d - 1], at_rep(d))

    def p_gather(d):
        return remote(p_all.at[sp], p_all.at[sp], s3.at[d - 1], r3.at[d - 1], at_sp(d))

    def p_gather_in(d):
        ref = p_all.at[lax.rem(sp + count_sp - d, count_sp)]
        return remote(ref, ref, s3.at[d - 1], r3.at[d - 1], at_sp(d))

    def x_out(step):
        return remote(x_term.at[step - 1], x_got.at[step - 1], x_send.at[step - 1], x_recv.at[step - 1], sp_at(x + step, z))

    def q_scatter(d):
        return remote(q_src.at[lax.rem(rep + d, count_rep)], q_got.at[d - 1], s4.at[d - 1], r4.at[d - 1], at_rep(d))

    def q_gather(d):
        return remote(q_next.at[rep], q_next.at[rep], s5.at[d - 1], r5.at[d - 1], at_rep(d))

    def q_gather_in(d):
        ref = q_next.at[lax.rem(rep + count_rep - d, count_rep)]
        return remote(ref, ref, s5.at[d - 1], r5.at[d - 1], at_rep(d))

    barrier = pltpu.get_barrier_semaphore()
    for d in range(1, count_sp):
        pl.semaphore_signal(barrier, inc=1, device_id=at_sp(d), device_id_type=MESH)
    for d in range(1, count_rep):
        pl.semaphore_signal(barrier, inc=1, device_id=at_rep(d), device_id_type=MESH)

    def column_in(i):
        return pltpu.make_async_copy(frames.at[:, columns(i)], local.at[i], l_in.at[i])

    pairs = frames.shape[1] // COLS
    owners = COLS // share
    own_grad(0).start()
    for i in range(pairs):
        column_in(i).start()
    pl.semaphore_wait(barrier, count_sp + count_rep - 2)
    own_grad(0).wait()
    direct(0, 0).start()
    direct(0, 1).start()

    per_x = RING // owners
    for first in range(per_x):
        for i in range(first, pairs, per_x):
            column_in(i).wait()
            turned = local[i].T
            for k in range(owners):
                owner = i * owners + k
                flipped[owner // RING, owner % RING] = turned[k * share : (k + 1) * share]
    for side in range(2):
        frames_far(side).start()
    for side in range(2):
        frames_near(side).start()
    own_frames = pltpu.make_async_copy(flipped.at[:, z], raw.at[z], f_own)
    own_frames.start()
    for j in range(CHUNKS):
        err_in(j).start()
    for j in range(1, CHUNKS):
        own_grad(j).start()

    thirds = [third.astype(jnp.float32) for third in split(q_own[...])]
    lanes = q_taps.shape[2]
    thirds.append(jnp.zeros((lanes - 3 * rank, q_own.shape[1]), jnp.float32))
    q_turned[...] = jnp.concatenate(thirds, axis=0).T
    for tap in range(TAPS):
        q_taps[tap] = q_turned[pl.ds(tap, share, stride=TAPS), :].astype(jnp.bfloat16)
    for step in (1, 3, 2):
        q_out(step).start()
    own_q = pltpu.make_async_copy(q_taps, q_near.at[:, x], q_copy)
    own_q.start()

    lane = lax.broadcasted_iota(jnp.int32, (RING * share, width), 1)

    def place(row, value):
        at = pl.ds(pl.multiple_of(row * width, width), width)
        wide = value.astype(jnp.float32)
        taps[0, :, at] = jnp.where(lane == 0, 0.0, pltpu.roll(wide, 1, 1)).astype(taps.dtype)
        taps[1, :, at] = value
        taps[2, :, at] = jnp.where(lane == width - 1, 0.0, pltpu.roll(wide, width - 1, 1)).astype(taps.dtype)

    def place_band(which):
        def place_row(row, carry):
            at = pl.ds(pl.multiple_of(row * width, width), width)
            place(which * (band // width) + row + 1, raw[which, :, :, at].reshape(RING * share, width))
            return carry

        lax.fori_loop(0, band // width, place_row, 0)

    def start_forward(j):
        for side in range(2):
            direct_in(j, side).wait_recv()
            forward(j, side).start()

    def start_direct(j):
        for side in range(2):
            direct(j, side).start()

    own_frames.wait()
    place_band(z)
    start_forward(0)
    for j in range(1, CHUNKS):
        own_grad(j).wait()

    for j in range(CHUNKS):
        err_in(j).wait()
        term = exact_dot(q_own[...], total[j], ((1,), (0,)))
        for h in range(2):
            p_src[2 * j + h] = term[h * (rank // 2) : (h + 1) * (rank // 2)]

    for side in range(2):
        frames_far(side).wait_recv()
        frames_on(side).start()
    for side in range(2):
        frames_near_in(side).wait_recv()
    start_direct(1)
    place_band(z_down)
    place_band(z_up)
    for side in range(2):
        frames_far_in(side).wait_recv()

    bottom = raw.at[RING - 1, :, :, band - width : band]
    above = remote(bottom, halo.at[0], h_send.at[0], h_recv.at[0], right)
    below = remote(raw.at[0, :, :, 0:width], halo.at[1], h_send.at[1], h_recv.at[1], left)
    above.start()
    below.start()
    place_band(lax.rem(z + 2, RING))
    rows = RING * band // width
    above.wait()
    below.wait()
    zero = jnp.zeros((RING * share, width), halo.dtype)
    place(0, jnp.where(x == 0, zero, halo[0].reshape(RING * share, width)))
    place(rows + 1, jnp.where(x == RING - 1, zero, halo[1].reshape(RING * share, width)))

    def t_band(which):
        acc = None
        for a in range(3):
            at = pl.ds(pl.multiple_of(which * band + a * width, width), band)
            stacked = taps[:, :, at].reshape(3 * RING * share, band)
            term = jnp.dot(q_flip[a], stacked, preferred_element_type=jnp.float32)
            acc = term if acc is None else acc + term
        t_term[which] = acc[:rank] + (acc[rank : 2 * rank] + acc[2 * rank : 3 * rank])

    def t_start():
        own_q.wait()
        for step in (1, 3, 2):
            q_in(step).wait_recv()
        for a in range(3):
            q_flip[a] = q_near[3 * a : 3 * a + 3].reshape(3 * RING * share, lanes).T

    def t_bands(first):
        def one(i, carry):
            t_band(first + i)
            return carry

        lax.fori_loop(0, RING // 2, one, 0)

    def t_finish():
        for side in range(2):
            t_far(side).start()

    def t_pass_on():
        for side in range(2):
            some = pl.ds(side * (rank // 2), rank // 2)
            t_far(side).wait_recv()
            t_term[near_z[side], some] = t_term[near_z[side], some] + t_relay[side]
            t_out(side).start()

    def p_terms():
        for side in range(2):
            t_out(side).wait_recv()
        full = t_term[z] + (t_near[0] + t_near[1])
        parts = jnp.concatenate(split(full), axis=0)

        def add(j, carry):
            acc = jnp.dot(parts, gbuf[j, slot(z, 0, band)], preferred_element_type=jnp.float32)
            term = acc[:rank] + (acc[rank : 2 * rank] + acc[2 * rank :])
            for h in range(2):
                p_src[2 * j + h] = p_src[2 * j + h] + term[h * (rank // 2) : (h + 1) * (rank // 2)]
            return carry

        lax.fori_loop(0, CHUNKS, add, 0)
        for d in range(1, count_sp):
            p_scatter(d).start()

    def p_sum_sp():
        acc = p_src[sp]
        for d in range(1, count_sp):
            p_scatter(d).wait_recv()
            acc = acc + p_near[d - 1]
        p_one[...] = acc
        p_far[rep] = acc
        for d in range(1, count_rep):
            p_share(d).start()

    def p_sum_rep():
        for d in range(1, count_rep):
            p_share_in(d).wait_recv()
        acc = p_far[0]
        for i in range(1, count_rep):
            acc = acc + p_far[i]
        p_all[sp] = acc
        for d in range(1, count_sp):
            p_gather(d).start()

    def p_chunk(j):
        return jnp.concatenate([p_all[2 * j], p_all[2 * j + 1]], axis=0)

    def orthogonal():
        for d in range(1, count_sp):
            p_gather_in(d).wait_recv()
        p_total = jnp.concatenate([p_chunk(j) for j in range(CHUNKS)], axis=1)
        gram = exact_dot(p_total, p_total, ((1,), (1,)))
        row_at = lax.broadcasted_iota(jnp.int32, (rank, rank), 0)
        col_at = lax.broadcasted_iota(jnp.int32, (rank, rank), 1)
        work[:, :rank] = gram
        work[:, rank : 2 * rank] = jnp.where(row_at == col_at, 1.0, 0.0)
        shape = (rank, 2 * rank)
        line = lax.broadcasted_iota(jnp.int32, shape, 0)
        spot = lax.broadcasted_iota(jnp.int32, shape, 1)

        def eliminate(k, carry):
            state = work[:, : 2 * rank]
            pivot = work[pl.ds(k, 1), : 2 * rank]
            column = jnp.sum(jnp.where(spot == k, state, 0.0), axis=1, keepdims=True)
            diagonal = jnp.sum(jnp.where(spot[:1] == k, pivot, 0.0), axis=1, keepdims=True)
            inverse = 1.0 / jnp.sqrt(diagonal)
            pivot = pivot * inverse
            work[:, : 2 * rank] = jnp.where(
                line > k, state - (column * inverse) * pivot, jnp.where(line == k, pivot, state)
            )
            return carry

        lax.fori_loop(0, rank, eliminate, 0)
        lower_inverse = jnp.where(col_at <= row_at, work[:, rank : 2 * rank], 0.0)
        whole = exact_dot(lower_inverse, p_total, ((1,), (0,)))
        p0, p1, p2 = split(whole)
        p_side[...] = jnp.concatenate([p0, p1, p2, p0, p1, p0], axis=0)
        q_sum[...] = jnp.zeros_like(q_sum)

    def by_p(rows_of, k):
        m0, m1, m2 = split(rows_of)
        m_side = jnp.concatenate([m0, m0, m0, m1, m1, m2], axis=1)
        across = jnp.concatenate([p_side[i * rank : (i + 1) * rank, columns(k)] for i in range(6)], axis=1)
        return jnp.dot(m_side, across.T, preferred_element_type=jnp.float32)

    def add_q(k):
        q_sum[:, :rank] = q_sum[:, :rank] + by_p(total[k], k)

    last = CHUNKS - 1

    def last_terms():
        for step in (1, 3, 2):
            owner = lax.rem(x + step, RING)
            terms = by_p(part[last, owner].reshape(q_sum.shape[0], COLS), last)
            x_term[step - 1] = terms.T
            x_out(step).start()

    def last_own():
        count = part.shape[4]
        for side in range(2):
            for tap in range(TAPS):
                at = pl.ds(side * count * TAPS + tap, count, stride=TAPS)
                total[last, at, :] = total[last, at, :] + part[last, x, side, tap]
        add_q(last)

    def last_sum():
        for step in (1, 3, 2):
            x_out(step).wait_recv()
        got = x_got[0] + x_got[1] + x_got[2]
        filled = jnp.concatenate([got, jnp.zeros((128 - rank, got.shape[1]), jnp.float32)], axis=0).T
        count = part.shape[4]
        for side in range(2):
            for tap in range(TAPS):
                at = pl.ds(side * count * TAPS + tap, count, stride=TAPS)
                line = (side * TAPS + tap) * count
                q_sum[at, :] = q_sum[at, :] + filled[line : line + count]

    def multiply(first, count, after):
        depth = gbuf.shape[1]
        per_side = part.shape[4]

        def one(a, carry):
            at = pl.ds(pl.multiple_of(a * width, width), depth)
            stacked = taps[:, :, at].reshape(3 * RING * share, depth)
            chosen = gbuf[first] if count == 1 else jnp.concatenate([gbuf[first], gbuf[first + 1]], axis=1)
            product = jnp.dot(stacked, chosen, preferred_element_type=jnp.float32)
            for c in range(count):
                for b in range(3):
                    for owner in range(RING):
                        for side in range(2):
                            line = b * RING * share + (owner * 2 + side) * per_side
                            part[first + c, owner, side, a * 3 + b] = product[
                                line : line + per_side, c * COLS : (c + 1) * COLS
                            ]
            @pl.when((a == 0) & (after < CHUNKS))
            def _():
                start_forward(after)

            return carry

        lax.fori_loop(0, 3, one, 0)
        for c in range(count):
            for side in range(2):
                put(far_code.at[first + c, side], part[first + c, x_far, side].reshape(half_rows, COLS))
                far(first + c, side).start()

    half_rows = TAPS * part.shape[4]

    def put(ref, block):
        signed, scale = encode(block)
        ref[:half_rows] = signed
        ref[half_rows:] = scale

    def pass_on(k):
        for side, owner in ((0, x_right), (1, x_left)):
            put(near_code.at[k, side, 1 - side], part[k, owner, 1 - side].reshape(half_rows, COLS))
            far(k, side).wait_recv()
            both = part[k, owner, side].reshape(half_rows, COLS) + decode(relay[k, side])
            put(near_code.at[k, side, side], both)
            near(k, side).start()

    def add_near(k, own):
        count = part.shape[4]
        for side in range(2):
            got = decode(piece[k, 0, side]) + decode(piece[k, 1, side])
            for tap in range(TAPS):
                at = pl.ds(side * count * TAPS + tap, count, stride=TAPS)
                term = got[tap * count : (tap + 1) * count]
                if own:
                    term = term + part[k, x, side, tap]
                total[k, at, :] = total[k, at, :] + term

    def complete(k, with_q):
        near(k, 0).wait_recv()
        near(k, 1).wait_recv()
        add_near(k, True)
        mem_out(k).start()
        pl.when(with_q)(lambda: add_q(k))

    def complete_last():
        near(last, 0).wait_recv()
        near(last, 1).wait_recv()
        add_near(last, False)
        mem_out(last).start()

    def over(first, count, body):
        def one(i, carry):
            body(first + i)
            return carry

        lax.fori_loop(0, count, one, 0)

    def step(j, carry):
        @pl.when(j + 2 < CHUNKS)
        def _():
            start_direct(j + 2)

        @pl.when(j < CHUNKS)
        def _():
            forward_in(j, 0).wait_recv()
            forward_in(j, 1).wait_recv()

        alone = (j == 0) | (j == CHUNKS - 1)
        even = lax.rem(j, 2) == 0
        pl.when(alone)(lambda: multiply(j, 1, j + 1))
        pl.when((j > 0) & (j < CHUNKS - 1) & even)(lambda: multiply(j - 1, 2, j + 1))
        pl.when((j < CHUNKS - 1) & jnp.logical_not(even))(lambda: start_forward(j + 1))

        pl.when((j == 1) | (j == CHUNKS))(lambda: pass_on(j - 1))
        pl.when((j > 1) & (j < CHUNKS) & jnp.logical_not(even))(lambda: over(j - 2, 2, pass_on))

        @pl.when(j == T_AT)
        def _():
            t_start()
            t_bands(0)
            t_bands(RING // 2)
            t_finish()

        pl.when(j == T_AT + 1)(t_pass_on)
        pl.when(j == last)(last_terms)

        for at, stage in zip(P_AT, (p_terms, p_sum_sp, p_sum_rep, orthogonal)):
            pl.when(j == at)(stage)
        ready = j >= P_AT[-1]

        pl.when(j == 2)(lambda: complete(0, ready))
        pl.when((j > 2) & (j <= CHUNKS) & even)(lambda: over(j - 3, 2, lambda k: complete(k, ready)))
        pl.when(j == P_AT[-1])(lambda: over(0, EARLY, add_q))

        return carry

    lax.fori_loop(0, CHUNKS + 1, step, 0)
    last_own()
    last_sum()

    lines = rank // count_rep
    q_lines = q_sum[...].T
    for i in range(count_rep):
        q_src[i] = q_lines[i * lines : (i + 1) * lines]
    for d in range(1, count_rep):
        q_scatter(d).start()
    acc = q_src[rep]
    for d in range(1, count_rep):
        q_scatter(d).wait_recv()
        acc = acc + q_got[d - 1]
    q_next[rep] = acc * (1.0 / count_rep)
    for d in range(1, count_rep):
        q_gather(d).start()
    complete_last()
    for d in range(1, count_rep):
        q_gather_in(d).wait_recv()

    def finish(j, carry):
        for side in range(2):
            direct(j, side).wait_send()
            forward(j, side).wait_send()
            far(j, side).wait_send()
            near(j, side).wait_send()
        mem_out(j).wait()
        return carry

    lax.fori_loop(0, CHUNKS, finish, 0)
    for side in range(2):
        frames_near(side).wait_send()
        frames_far(side).wait_send()
        frames_on(side).wait_send()
        t_far(side).wait_send()
        t_out(side).wait_send()
    for step_ in (1, 3, 2):
        q_out(step_).wait_send()
        x_out(step_).wait_send()
    for d in range(1, count_sp):
        p_scatter(d).wait_send()
        p_gather(d).wait_send()
    for d in range(1, count_rep):
        p_share(d).wait_send()
        q_scatter(d).wait_send()
        q_gather(d).wait_send()


def compressed_step(count_rep, frames, g, err, q_own):
    band, chans = g.shape
    width = band // 4
    rows = err.shape[0]
    rank = q_own.shape[0]
    count_sp = RING * RING
    share = chans // count_sp
    per_side = share // 2
    code_rows = TAPS * per_side + SCALE_ROWS
    dma = pltpu.SemaphoreType.DMA
    two = dma((CHUNKS, 2))
    f32, bf16 = jnp.float32, jnp.bfloat16
    any_spec, vmem_spec = pl.BlockSpec(memory_space=pl.ANY), pl.BlockSpec(memory_space=pltpu.VMEM)
    p_block = (rank // 2, COLS)
    q_block = (rank // count_rep, rows)
    return pl.pallas_call(
        functools.partial(step_kernel, count_rep),
        out_shape=(
            jax.ShapeDtypeStruct((rows, chans), f32),
            jax.ShapeDtypeStruct((count_rep, *q_block), f32),
            jax.ShapeDtypeStruct((6 * rank, chans), bf16),
        ),
        in_specs=[any_spec, any_spec, any_spec, vmem_spec],
        out_specs=(any_spec, vmem_spec, vmem_spec),
        scratch_shapes=[
            pltpu.VMEM((chans // COLS, band, COLS), bf16),
            pltpu.VMEM((2, RING // 2, share, band), bf16),
            pltpu.VMEM((2, rank // 2, band), f32),
            pltpu.VMEM((rows, 128), f32),
            pltpu.VMEM((TAPS, share, 128), bf16),
            pltpu.VMEM((RING, RING, share, band), bf16),
            pltpu.VMEM((RING, RING, share, band), bf16),
            pltpu.VMEM((2, RING, share, width), bf16),
            pltpu.VMEM((3, RING * share, RING * band + 2 * width), bf16),
            pltpu.VMEM((CHUNKS, RING * band, COLS), bf16),
            pltpu.VMEM((CHUNKS, RING, 2, TAPS, per_side, COLS), f32),
            pltpu.VMEM((CHUNKS, 2, code_rows, COLS), bf16),
            pltpu.VMEM((CHUNKS, 2, 2, code_rows, COLS), bf16),
            pltpu.VMEM((CHUNKS, 2, code_rows, COLS), bf16),
            pltpu.VMEM((CHUNKS, 2, 2, code_rows, COLS), bf16),
            pltpu.VMEM((CHUNKS, rows, COLS), f32),
            pltpu.VMEM((TAPS, RING, share, 128), bf16),
            pltpu.VMEM((3, 128, 3 * RING * share), bf16),
            pltpu.VMEM((RING, rank, band), f32),
            pltpu.VMEM((2, rank, band), f32),
            pltpu.VMEM((count_sp, *p_block), f32),
            pltpu.VMEM((count_sp - 1, *p_block), f32),
            pltpu.VMEM(p_block, f32),
            pltpu.VMEM((count_rep, *p_block), f32),
            pltpu.VMEM((count_sp, *p_block), f32),
            pltpu.VMEM((rank, 128), f32),
            pltpu.VMEM((count_rep, *q_block), f32),
            pltpu.VMEM((count_rep - 1, *q_block), f32),
            pltpu.VMEM((rows, 128), f32),
            pltpu.VMEM((RING - 1, rank, rows), f32),
            pltpu.VMEM((RING - 1, rank, rows), f32),
            dma((chans // COLS,)), dma((6,)), dma((6,)), dma, dma((2,)), dma((2,)), dma((CHUNKS,)), dma((CHUNKS,)),
            two, two, two, two, two, two, two, two, dma((CHUNKS,)),
            dma((3,)), dma((3,)), dma, dma((4,)), dma((4,)),
            dma((count_sp - 1,)), dma((count_sp - 1,)), dma((count_rep - 1,)), dma((count_rep - 1,)),
            dma((count_sp - 1,)), dma((count_sp - 1,)), dma((count_rep - 1,)), dma((count_rep - 1,)),
            dma((count_rep - 1,)), dma((count_rep - 1,)), dma((3,)), dma((3,)),
        ],
        compiler_params=pltpu.CompilerParams(
            collective_id=0, has_side_effects=True, vmem_limit_bytes=58 * 1024 * 1024
        ),
        cost_estimate=pl.CostEstimate(flops=2 * rows * 16 * chans * band, bytes_accessed=10**7, transcendentals=0),
        name="compressed_step",
    )(frames, g, err, q_own)


def feedback_kernel(memory, q_parts, p_side, error_next, q_next, q_side):
    count, lines, rows = q_parts.shape
    block = memory.shape[0]

    @pl.when(pl.program_id(0) == 0)
    def _():
        for i in range(count):
            q_next[i * lines : (i + 1) * lines] = q_parts[i]
        q0, q1, q2 = split(q_next[...])
        q_side[...] = jnp.concatenate([q0, q0, q0, q1, q1, q2], axis=0).T

    at = pl.ds(pl.multiple_of(pl.program_id(0) * block, block), block)
    error_next[...] = memory[...] - jnp.dot(q_side[at, :], p_side[...], preferred_element_type=jnp.float32)


def feedback(memory, q_parts, p_side):
    rows, chans = memory.shape
    count, lines, _ = q_parts.shape
    rank = count * lines
    block = (rows // 4, chans)
    return pl.pallas_call(
        feedback_kernel,
        grid=(rows // block[0],),
        out_shape=(jax.ShapeDtypeStruct(memory.shape, jnp.float32), jax.ShapeDtypeStruct((rank, rows), jnp.float32)),
        in_specs=[
            pl.BlockSpec(block, lambda i: (i, 0)),
            pl.BlockSpec(q_parts.shape, lambda i: (0, 0, 0)),
            pl.BlockSpec(p_side.shape, lambda i: (0, 0)),
        ],
        out_specs=(pl.BlockSpec(block, lambda i: (i, 0)), pl.BlockSpec((rank, rows), lambda i: (0, 0))),
        scratch_shapes=[pltpu.VMEM((rows, 6 * rank), jnp.bfloat16)],
        compiler_params=pltpu.CompilerParams(vmem_limit_bytes=60 * 1024 * 1024),
        name="feedback",
    )(memory, q_parts, p_side)


def per_device(count_rep, frames, out_grad, error_prev, q_prev):
    band_rows, width, chans = frames.shape[1:]
    band = band_rows * width
    memory, q_parts, p_side = compressed_step(
        count_rep,
        frames[0].reshape(band, chans),
        out_grad[0].reshape(band, chans),
        error_prev[0],
        q_prev,
    )
    error_next, q_next = feedback(memory, q_parts, p_side)
    return (error_next[None], q_next)


def solution(mesh):
    placed = (
        P("rep", "sp", None, None),
        P("rep", "sp", None, None),
        P("rep", "sp", None),
        P(None, "sp"),
    )
    return jax.shard_map(
        functools.partial(per_device, mesh.shape["rep"]),
        mesh=mesh,
        in_specs=placed,
        out_specs=(P("rep", "sp", None), P(None, "sp")),
        check_vma=False,
    )
```

```python
import functools

import jax
import jax.numpy as jnp
from jax import lax
from jax.experimental import pallas as pl
from jax.experimental.pallas import tpu as pltpu
from jax.sharding import PartitionSpec as P

MESH = pl.DeviceIdType.MESH
RING = 4
CHUNKS = 8
COLS = 128
TAPS = 9
T_AT = 0
P_AT = (2, 3, 4, 5)
EARLY = 3


def sp_at(x, z):
    return {"sp": lax.rem(x + RING, RING) * RING + lax.rem(z + RING, RING)}


def remote(src, dst, send, recv, device):
    return pltpu.make_async_remote_copy(
        src_ref=src, dst_ref=dst, send_sem=send, recv_sem=recv, device_id=device, device_id_type=MESH
    )


def split(value):
    high = value.astype(jnp.bfloat16)
    rest = value - high.astype(jnp.float32)
    middle = rest.astype(jnp.bfloat16)
    low = (rest - middle.astype(jnp.float32)).astype(jnp.bfloat16)
    return high, middle, low


def exact_dot(a, b, contract):
    return lax.dot_general(
        a, b, (contract, ((), ())), precision=lax.Precision.HIGHEST, preferred_element_type=jnp.float32
    )


SCALE_ROWS = 16
RANGE = 1024.0


def encode(block):
    largest = jnp.max(jnp.abs(block), axis=(0, 1), keepdims=True)
    scale = jnp.maximum(largest * 1.01, 1e-30).astype(jnp.bfloat16)
    size = jnp.abs(block) * (RANGE / scale.astype(jnp.float32))
    second = size * size
    fourth = second * second
    twelfth = fourth * fourth * fourth
    signed = jnp.where(block < 0, -twelfth, twelfth).astype(jnp.bfloat16)
    return signed, jnp.broadcast_to(scale, (SCALE_ROWS, block.shape[1]))


def decode(coded):
    count = coded.shape[0] - SCALE_ROWS
    signed = coded[:count].astype(jnp.float32)
    scale = coded[count : count + 1].astype(jnp.float32) * (1.0 / RANGE)
    size = jnp.abs(signed)
    value = jnp.exp(jnp.log(jnp.maximum(size, 1e-37)) * (1.0 / 12.0)) * scale
    value = jnp.where(size < 1e-37, 0.0, value)
    return jnp.where(signed < 0, -value, value)


def step_kernel(
    count_rep, frames, g, err, q_own, memory, q_next, p_side,
    local, f_relay, t_relay, q_turned, q_taps, flipped, raw, halo, taps, gbuf, part, far_code, near_code, relay, piece, total,
    q_near, q_flip, t_term, t_near, p_src, p_near, p_one, p_far, p_all, work, q_src, q_got, q_sum, x_term, x_got,
    l_in, f_send, f_recv, f_own, h_send, h_recv, e_in, g_own,
    d_send, d_recv, r_send, r_recv, a_send, a_recv, b_send, b_recv, out_sem,
    q_send, q_recv, q_copy, t_send, t_recv, s1, r1, s2, r2, s3, r3, s4, r4, s5, r5, x_send, x_recv,
):
    sp, rep = lax.axis_index("sp"), lax.axis_index("rep")
    x, z = sp // RING, lax.rem(sp, RING)
    up, down = sp_at(x, z + 1), sp_at(x, z - 1)
    right, left = sp_at(x + 1, z), sp_at(x - 1, z)
    z_up, z_down = lax.rem(z + 1, RING), lax.rem(z + 3, RING)
    x_right, x_left, x_far = lax.rem(x + 1, RING), lax.rem(x + 3, RING), lax.rem(x + 2, RING)
    band = g.shape[0]
    half = band // 2
    count_sp = RING * RING
    share = part.shape[4] * 2
    width = halo.shape[3]
    rank = q_own.shape[0]

    def at_sp(d):
        return {"sp": lax.rem(sp + d, count_sp)}

    def at_rep(d):
        return {"rep": lax.rem(rep + d, count_rep)}

    near_z, far_z = (z_up, z_down), lax.rem(z + 2, RING)
    towards = (up, down)
    some_x = RING // 2

    def frames_near(side):
        return remote(flipped.at[:, near_z[side]], raw.at[z], f_send.at[side], f_recv.at[side], towards[side])

    def frames_near_in(side):
        return remote(flipped.at[:, z], raw.at[near_z[1 - side]], f_send.at[side], f_recv.at[side], up)

    def frames_far(side):
        part_x = pl.ds(side * some_x, some_x)
        return remote(
            flipped.at[part_x, far_z], f_relay.at[side], f_send.at[2 + side], f_recv.at[2 + side], towards[side]
        )

    def frames_on(side):
        part_x = pl.ds(side * some_x, some_x)
        return remote(
            f_relay.at[side], raw.at[near_z[1 - side], part_x], f_send.at[4 + side], f_recv.at[4 + side], towards[side]
        )

    def frames_far_in(side):
        part_x = pl.ds(side * some_x, some_x)
        return remote(f_relay.at[side], raw.at[far_z, part_x], f_send.at[4 + side], f_recv.at[4 + side], up)

    def columns(j):
        return pl.ds(pl.multiple_of(j * COLS, COLS), COLS)

    def slot(which, first, count):
        return pl.ds(pl.multiple_of(which * band + first, half), count)

    def own_grad(j):
        return pltpu.make_async_copy(g.at[:, columns(j)], gbuf.at[j, slot(z, 0, band)], g_own.at[j])

    def direct(j, side):
        ref = gbuf.at[j, slot(z, 0, band)]
        return remote(ref, ref, d_send.at[j, side], d_recv.at[j, side], up if side == 0 else down)

    def direct_in(j, side):
        ref = gbuf.at[j, slot(z_down if side == 0 else z_up, 0, band)]
        return remote(ref, ref, d_send.at[j, side], d_recv.at[j, side], up)

    def forward(j, side):
        ref = gbuf.at[j, slot(z_down if side == 0 else z_up, side * half, half)]
        return remote(ref, ref, r_send.at[j, side], r_recv.at[j, side], up if side == 0 else down)

    def forward_in(j, side):
        ref = gbuf.at[j, slot(lax.rem(z + 2, RING), side * half, half)]
        return remote(ref, ref, r_send.at[j, side], r_recv.at[j, side], up)

    def err_in(j):
        return pltpu.make_async_copy(err.at[:, columns(j)], total.at[j], e_in.at[j])

    def mem_out(j):
        return pltpu.make_async_copy(total.at[j], memory.at[:, columns(j)], out_sem.at[j])

    def far(j, side):
        return remote(
            far_code.at[j, side], relay.at[j, side], a_send.at[j, side], a_recv.at[j, side],
            right if side == 0 else left,
        )

    def near(j, side):
        return remote(
            near_code.at[j, side], piece.at[j, side], b_send.at[j, side], b_recv.at[j, side],
            right if side == 0 else left,
        )

    def q_out(step):
        return remote(q_taps, q_near.at[:, x], q_send.at[step - 1], q_recv.at[step - 1], sp_at(x + step, z))

    def q_in(step):
        source = lax.rem(x + RING - step, RING)
        return remote(q_taps, q_near.at[:, source], q_send.at[step - 1], q_recv.at[step - 1], right)

    def t_far(side):
        some = pl.ds(side * (rank // 2), rank // 2)
        return remote(t_term.at[far_z, some], t_relay.at[side], t_send.at[side], t_recv.at[side], towards[side])

    def t_out(side):
        return remote(
            t_term.at[near_z[side]], t_near.at[side], t_send.at[2 + side], t_recv.at[2 + side], towards[side]
        )

    def p_scatter(d):
        return remote(p_src.at[lax.rem(sp + d, count_sp)], p_near.at[d - 1], s1.at[d - 1], r1.at[d - 1], at_sp(d))

    def p_share(d):
        return remote(p_one, p_far.at[rep], s2.at[d - 1], r2.at[d - 1], at_rep(d))

    def p_share_in(d):
        source = lax.rem(rep + count_rep - d, count_rep)
        return remote(p_one, p_far.at[source], s2.at[d - 1], r2.at[d - 1], at_rep(d))

    def p_gather(d):
        return remote(p_all.at[sp], p_all.at[sp], s3.at[d - 1], r3.at[d - 1], at_sp(d))

    def p_gather_in(d):
        ref = p_all.at[lax.rem(sp + count_sp - d, count_sp)]
        return remote(ref, ref, s3.at[d - 1], r3.at[d - 1], at_sp(d))

    def x_out(step):
        return remote(x_term.at[step - 1], x_got.at[step - 1], x_send.at[step - 1], x_recv.at[step - 1], sp_at(x + step, z))

    def q_scatter(d):
        return remote(q_src.at[lax.rem(rep + d, count_rep)], q_got.at[d - 1], s4.at[d - 1], r4.at[d - 1], at_rep(d))

    def q_gather(d):
        return remote(q_next.at[rep], q_next.at[rep], s5.at[d - 1], r5.at[d - 1], at_rep(d))

    def q_gather_in(d):
        ref = q_next.at[lax.rem(rep + count_rep - d, count_rep)]
        return remote(ref, ref, s5.at[d - 1], r5.at[d - 1], at_rep(d))

    barrier = pltpu.get_barrier_semaphore()
    for d in range(1, count_sp):
        pl.semaphore_signal(barrier, inc=1, device_id=at_sp(d), device_id_type=MESH)
    for d in range(1, count_rep):
        pl.semaphore_signal(barrier, inc=1, device_id=at_rep(d), device_id_type=MESH)

    def column_in(i):
        return pltpu.make_async_copy(frames.at[:, columns(i)], local.at[i], l_in.at[i])

    pairs = frames.shape[1] // COLS
    owners = COLS // share
    own_grad(0).start()
    for i in range(pairs):
        column_in(i).start()
    pl.semaphore_wait(barrier, count_sp + count_rep - 2)
    own_grad(0).wait()
    direct(0, 0).start()
    direct(0, 1).start()

    per_x = RING // owners
    for first in range(per_x):
        for i in range(first, pairs, per_x):
            column_in(i).wait()
            turned = local[i].T
            for k in range(owners):
                owner = i * owners + k
                flipped[owner // RING, owner % RING] = turned[k * share : (k + 1) * share]
    for side in range(2):
        frames_far(side).start()
    for side in range(2):
        frames_near(side).start()
    own_frames = pltpu.make_async_copy(flipped.at[:, z], raw.at[z], f_own)
    own_frames.start()
    for j in range(CHUNKS):
        err_in(j).start()
    for j in range(1, CHUNKS):
        own_grad(j).start()

    thirds = [third.astype(jnp.float32) for third in split(q_own[...])]
    lanes = q_taps.shape[2]
    thirds.append(jnp.zeros((lanes - 3 * rank, q_own.shape[1]), jnp.float32))
    q_turned[...] = jnp.concatenate(thirds, axis=0).T
    for tap in range(TAPS):
        q_taps[tap] = q_turned[pl.ds(tap, share, stride=TAPS), :].astype(jnp.bfloat16)
    for step in (1, 3, 2):
        q_out(step).start()
    own_q = pltpu.make_async_copy(q_taps, q_near.at[:, x], q_copy)
    own_q.start()

    lane = lax.broadcasted_iota(jnp.int32, (RING * share, width), 1)

    def place(row, value):
        at = pl.ds(pl.multiple_of(row * width, width), width)
        wide = value.astype(jnp.float32)
        taps[0, :, at] = jnp.where(lane == 0, 0.0, pltpu.roll(wide, 1, 1)).astype(taps.dtype)
        taps[1, :, at] = value
        taps[2, :, at] = jnp.where(lane == width - 1, 0.0, pltpu.roll(wide, width - 1, 1)).astype(taps.dtype)

    def place_band(which):
        def place_row(row, carry):
            at = pl.ds(pl.multiple_of(row * width, width), width)
            place(which * (band // width) + row + 1, raw[which, :, :, at].reshape(RING * share, width))
            return carry

        lax.fori_loop(0, band // width, place_row, 0)

    def start_forward(j):
        for side in range(2):
            direct_in(j, side).wait_recv()
            forward(j, side).start()

    def start_direct(j):
        for side in range(2):
            direct(j, side).start()

    own_frames.wait()
    place_band(z)
    start_forward(0)
    for j in range(1, CHUNKS):
        own_grad(j).wait()

    for j in range(CHUNKS):
        err_in(j).wait()
        term = exact_dot(q_own[...], total[j], ((1,), (0,)))
        for h in range(2):
            p_src[2 * j + h] = term[h * (rank // 2) : (h + 1) * (rank // 2)]

    for side in range(2):
        frames_far(side).wait_recv()
        frames_on(side).start()
    for side in range(2):
        frames_near_in(side).wait_recv()
    start_direct(1)
    place_band(z_down)
    place_band(z_up)
    for side in range(2):
        frames_far_in(side).wait_recv()

    bottom = raw.at[RING - 1, :, :, band - width : band]
    above = remote(bottom, halo.at[0], h_send.at[0], h_recv.at[0], right)
    below = remote(raw.at[0, :, :, 0:width], halo.at[1], h_send.at[1], h_recv.at[1], left)
    above.start()
    below.start()
    place_band(lax.rem(z + 2, RING))
    rows = RING * band // width
    above.wait()
    below.wait()
    zero = jnp.zeros((RING * share, width), halo.dtype)
    place(0, jnp.where(x == 0, zero, halo[0].reshape(RING * share, width)))
    place(rows + 1, jnp.where(x == RING - 1, zero, halo[1].reshape(RING * share, width)))

    def t_band(which):
        acc = None
        for a in range(3):
            at = pl.ds(pl.multiple_of(which * band + a * width, width), band)
            stacked = taps[:, :, at].reshape(3 * RING * share, band)
            term = jnp.dot(q_flip[a], stacked, preferred_element_type=jnp.float32)
            acc = term if acc is None else acc + term
        t_term[which] = acc[:rank] + (acc[rank : 2 * rank] + acc[2 * rank : 3 * rank])

    def t_start():
        own_q.wait()
        for step in (1, 3, 2):
            q_in(step).wait_recv()
        for a in range(3):
            q_flip[a] = q_near[3 * a : 3 * a + 3].reshape(3 * RING * share, lanes).T

    def t_bands(first):
        def one(i, carry):
            t_band(first + i)
            return carry

        lax.fori_loop(0, RING // 2, one, 0)

    def t_finish():
        for side in range(2):
            t_far(side).start()

    def t_pass_on():
        for side in range(2):
            some = pl.ds(side * (rank // 2), rank // 2)
            t_far(side).wait_recv()
            t_term[near_z[side], some] = t_term[near_z[side], some] + t_relay[side]
            t_out(side).start()

    def p_terms():
        for side in range(2):
            t_out(side).wait_recv()
        full = t_term[z] + (t_near[0] + t_near[1])
        parts = jnp.concatenate(split(full), axis=0)

        def add(j, carry):
            acc = jnp.dot(parts, gbuf[j, slot(z, 0, band)], preferred_element_type=jnp.float32)
            term = acc[:rank] + (acc[rank : 2 * rank] + acc[2 * rank :])
            for h in range(2):
                p_src[2 * j + h] = p_src[2 * j + h] + term[h * (rank // 2) : (h + 1) * (rank // 2)]
            return carry

        lax.fori_loop(0, CHUNKS, add, 0)
        for d in range(1, count_sp):
            p_scatter(d).start()

    def p_sum_sp():
        acc = p_src[sp]
        for d in range(1, count_sp):
            p_scatter(d).wait_recv()
            acc = acc + p_near[d - 1]
        p_one[...] = acc
        p_far[rep] = acc
        for d in range(1, count_rep):
            p_share(d).start()

    def p_sum_rep():
        for d in range(1, count_rep):
            p_share_in(d).wait_recv()
        acc = p_far[0]
        for i in range(1, count_rep):
            acc = acc + p_far[i]
        p_all[sp] = acc
        for d in range(1, count_sp):
            p_gather(d).start()

    def p_chunk(j):
        return jnp.concatenate([p_all[2 * j], p_all[2 * j + 1]], axis=0)

    def orthogonal():
        for d in range(1, count_sp):
            p_gather_in(d).wait_recv()
        p_total = jnp.concatenate([p_chunk(j) for j in range(CHUNKS)], axis=1)
        gram = exact_dot(p_total, p_total, ((1,), (1,)))
        row_at = lax.broadcasted_iota(jnp.int32, (rank, rank), 0)
        col_at = lax.broadcasted_iota(jnp.int32, (rank, rank), 1)
        work[:, :rank] = gram
        work[:, rank : 2 * rank] = jnp.where(row_at == col_at, 1.0, 0.0)
        shape = (rank, 2 * rank)
        line = lax.broadcasted_iota(jnp.int32, shape, 0)
        spot = lax.broadcasted_iota(jnp.int32, shape, 1)

        def eliminate(k, carry):
            state = work[:, : 2 * rank]
            pivot = work[pl.ds(k, 1), : 2 * rank]
            column = jnp.sum(jnp.where(spot == k, state, 0.0), axis=1, keepdims=True)
            diagonal = jnp.sum(jnp.where(spot[:1] == k, pivot, 0.0), axis=1, keepdims=True)
            inverse = 1.0 / jnp.sqrt(diagonal)
            pivot = pivot * inverse
            work[:, : 2 * rank] = jnp.where(
                line > k, state - (column * inverse) * pivot, jnp.where(line == k, pivot, state)
            )
            return carry

        lax.fori_loop(0, rank, eliminate, 0)
        lower_inverse = jnp.where(col_at <= row_at, work[:, rank : 2 * rank], 0.0)
        whole = exact_dot(lower_inverse, p_total, ((1,), (0,)))
        p0, p1, p2 = split(whole)
        p_side[...] = jnp.concatenate([p0, p1, p2, p0, p1, p0], axis=0)
        q_sum[...] = jnp.zeros_like(q_sum)

    def by_p(rows_of, k):
        m0, m1, m2 = split(rows_of)
        m_side = jnp.concatenate([m0, m0, m0, m1, m1, m2], axis=1)
        across = jnp.concatenate([p_side[i * rank : (i + 1) * rank, columns(k)] for i in range(6)], axis=1)
        return jnp.dot(m_side, across.T, preferred_element_type=jnp.float32)

    def add_q(k):
        q_sum[:, :rank] = q_sum[:, :rank] + by_p(total[k], k)

    last = CHUNKS - 1

    def last_terms():
        for step in (1, 3, 2):
            owner = lax.rem(x + step, RING)
            terms = by_p(part[last, owner].reshape(q_sum.shape[0], COLS), last)
            x_term[step - 1] = terms.T
            x_out(step).start()

    def last_own():
        count = part.shape[4]
        for side in range(2):
            for tap in range(TAPS):
                at = pl.ds(side * count * TAPS + tap, count, stride=TAPS)
                total[last, at, :] = total[last, at, :] + part[last, x, side, tap]
        add_q(last)

    def last_sum():
        for step in (1, 3, 2):
            x_out(step).wait_recv()
        got = x_got[0] + x_got[1] + x_got[2]
        filled = jnp.concatenate([got, jnp.zeros((128 - rank, got.shape[1]), jnp.float32)], axis=0).T
        count = part.shape[4]
        for side in range(2):
            for tap in range(TAPS):
                at = pl.ds(side * count * TAPS + tap, count, stride=TAPS)
                line = (side * TAPS + tap) * count
                q_sum[at, :] = q_sum[at, :] + filled[line : line + count]

    def multiply(first, count):
        depth = gbuf.shape[1]
        per_side = part.shape[4]

        def one(a, carry):
            at = pl.ds(pl.multiple_of(a * width, width), depth)
            stacked = taps[:, :, at].reshape(3 * RING * share, depth)
            chosen = gbuf[first] if count == 1 else jnp.concatenate([gbuf[first], gbuf[first + 1]], axis=1)
            product = jnp.dot(stacked, chosen, preferred_element_type=jnp.float32)
            for c in range(count):
                for b in range(3):
                    for owner in range(RING):
                        for side in range(2):
                            line = b * RING * share + (owner * 2 + side) * per_side
                            part[first + c, owner, side, a * 3 + b] = product[
                                line : line + per_side, c * COLS : (c + 1) * COLS
                            ]
            @pl.when((a == 0) & (first == 0))
            def _():
                start_forward(1)
                start_direct(3)

            return carry

        lax.fori_loop(0, 3, one, 0)
        for c in range(count):
            for side in range(2):
                put(far_code.at[first + c, side], part[first + c, x_far, side].reshape(half_rows, COLS))
                far(first + c, side).start()

    half_rows = TAPS * part.shape[4]

    def put(ref, block):
        signed, scale = encode(block)
        ref[:half_rows] = signed
        ref[half_rows:] = scale

    def pass_on(k):
        for side, owner in ((0, x_right), (1, x_left)):
            put(near_code.at[k, side, 1 - side], part[k, owner, 1 - side].reshape(half_rows, COLS))
            far(k, side).wait_recv()
            both = part[k, owner, side].reshape(half_rows, COLS) + decode(relay[k, side])
            put(near_code.at[k, side, side], both)
            near(k, side).start()

    def add_near(k, own):
        count = part.shape[4]
        for side in range(2):
            got = decode(piece[k, 0, side]) + decode(piece[k, 1, side])
            for tap in range(TAPS):
                at = pl.ds(side * count * TAPS + tap, count, stride=TAPS)
                term = got[tap * count : (tap + 1) * count]
                if own:
                    term = term + part[k, x, side, tap]
                total[k, at, :] = total[k, at, :] + term

    def complete(k, with_q):
        near(k, 0).wait_recv()
        near(k, 1).wait_recv()
        add_near(k, True)
        mem_out(k).start()
        pl.when(with_q)(lambda: add_q(k))

    def complete_last():
        near(last, 0).wait_recv()
        near(last, 1).wait_recv()
        add_near(last, False)
        mem_out(last).start()

    def over(first, count, body):
        def one(i, carry):
            body(first + i)
            return carry

        lax.fori_loop(0, count, one, 0)

    def step(j, carry):
        pl.when(j == 0)(lambda: start_direct(2))

        @pl.when((j > 0) & (j + 3 < CHUNKS))
        def _():
            start_direct(j + 3)

        @pl.when((j > 0) & (j + 2 < CHUNKS))
        def _():
            start_forward(j + 2)

        @pl.when(j < CHUNKS)
        def _():
            forward_in(j, 0).wait_recv()
            forward_in(j, 1).wait_recv()

        alone = (j == 0) | (j == CHUNKS - 1)
        even = lax.rem(j, 2) == 0
        pl.when(alone)(lambda: multiply(j, 1))
        pl.when((j > 0) & (j < CHUNKS - 1) & even)(lambda: multiply(j - 1, 2))

        pl.when((j == 1) | (j == CHUNKS))(lambda: pass_on(j - 1))
        pl.when((j > 1) & (j < CHUNKS) & jnp.logical_not(even))(lambda: over(j - 2, 2, pass_on))

        @pl.when(j == T_AT)
        def _():
            t_start()
            t_bands(0)
            start_forward(2)
            t_bands(RING // 2)
            t_finish()

        pl.when(j == T_AT + 1)(t_pass_on)
        pl.when(j == last)(last_terms)

        for at, stage in zip(P_AT, (p_terms, p_sum_sp, p_sum_rep, orthogonal)):
            pl.when(j == at)(stage)
        ready = j >= P_AT[-1]

        pl.when(j == 2)(lambda: complete(0, ready))
        pl.when((j > 2) & (j <= CHUNKS) & even)(lambda: over(j - 3, 2, lambda k: complete(k, ready)))
        pl.when(j == P_AT[-1])(lambda: over(0, EARLY, add_q))

        return carry

    lax.fori_loop(0, CHUNKS + 1, step, 0)
    last_own()
    last_sum()

    lines = rank // count_rep
    q_lines = q_sum[...].T
    for i in range(count_rep):
        q_src[i] = q_lines[i * lines : (i + 1) * lines]
    for d in range(1, count_rep):
        q_scatter(d).start()
    acc = q_src[rep]
    for d in range(1, count_rep):
        q_scatter(d).wait_recv()
        acc = acc + q_got[d - 1]
    q_next[rep] = acc * (1.0 / count_rep)
    for d in range(1, count_rep):
        q_gather(d).start()
    complete_last()
    for d in range(1, count_rep):
        q_gather_in(d).wait_recv()

    def finish(j, carry):
        for side in range(2):
            direct(j, side).wait_send()
            forward(j, side).wait_send()
            far(j, side).wait_send()
            near(j, side).wait_send()
        mem_out(j).wait()
        return carry

    lax.fori_loop(0, CHUNKS, finish, 0)
    for side in range(2):
        frames_near(side).wait_send()
        frames_far(side).wait_send()
        frames_on(side).wait_send()
        t_far(side).wait_send()
        t_out(side).wait_send()
    for step_ in (1, 3, 2):
        q_out(step_).wait_send()
        x_out(step_).wait_send()
    for d in range(1, count_sp):
        p_scatter(d).wait_send()
        p_gather(d).wait_send()
    for d in range(1, count_rep):
        p_share(d).wait_send()
        q_scatter(d).wait_send()
        q_gather(d).wait_send()


def compressed_step(count_rep, frames, g, err, q_own):
    band, chans = g.shape
    width = band // 4
    rows = err.shape[0]
    rank = q_own.shape[0]
    count_sp = RING * RING
    share = chans // count_sp
    per_side = share // 2
    code_rows = TAPS * per_side + SCALE_ROWS
    dma = pltpu.SemaphoreType.DMA
    two = dma((CHUNKS, 2))
    f32, bf16 = jnp.float32, jnp.bfloat16
    any_spec, vmem_spec = pl.BlockSpec(memory_space=pl.ANY), pl.BlockSpec(memory_space=pltpu.VMEM)
    p_block = (rank // 2, COLS)
    q_block = (rank // count_rep, rows)
    return pl.pallas_call(
        functools.partial(step_kernel, count_rep),
        out_shape=(
            jax.ShapeDtypeStruct((rows, chans), f32),
            jax.ShapeDtypeStruct((count_rep, *q_block), f32),
            jax.ShapeDtypeStruct((6 * rank, chans), bf16),
        ),
        in_specs=[any_spec, any_spec, any_spec, vmem_spec],
        out_specs=(any_spec, vmem_spec, vmem_spec),
        scratch_shapes=[
            pltpu.VMEM((chans // COLS, band, COLS), bf16),
            pltpu.VMEM((2, RING // 2, share, band), bf16),
            pltpu.VMEM((2, rank // 2, band), f32),
            pltpu.VMEM((rows, 128), f32),
            pltpu.VMEM((TAPS, share, 128), bf16),
            pltpu.VMEM((RING, RING, share, band), bf16),
            pltpu.VMEM((RING, RING, share, band), bf16),
            pltpu.VMEM((2, RING, share, width), bf16),
            pltpu.VMEM((3, RING * share, RING * band + 2 * width), bf16),
            pltpu.VMEM((CHUNKS, RING * band, COLS), bf16),
            pltpu.VMEM((CHUNKS, RING, 2, TAPS, per_side, COLS), f32),
            pltpu.VMEM((CHUNKS, 2, code_rows, COLS), bf16),
            pltpu.VMEM((CHUNKS, 2, 2, code_rows, COLS), bf16),
            pltpu.VMEM((CHUNKS, 2, code_rows, COLS), bf16),
            pltpu.VMEM((CHUNKS, 2, 2, code_rows, COLS), bf16),
            pltpu.VMEM((CHUNKS, rows, COLS), f32),
            pltpu.VMEM((TAPS, RING, share, 128), bf16),
            pltpu.VMEM((3, 128, 3 * RING * share), bf16),
            pltpu.VMEM((RING, rank, band), f32),
            pltpu.VMEM((2, rank, band), f32),
            pltpu.VMEM((count_sp, *p_block), f32),
            pltpu.VMEM((count_sp - 1, *p_block), f32),
            pltpu.VMEM(p_block, f32),
            pltpu.VMEM((count_rep, *p_block), f32),
            pltpu.VMEM((count_sp, *p_block), f32),
            pltpu.VMEM((rank, 128), f32),
            pltpu.VMEM((count_rep, *q_block), f32),
            pltpu.VMEM((count_rep - 1, *q_block), f32),
            pltpu.VMEM((rows, 128), f32),
            pltpu.VMEM((RING - 1, rank, rows), f32),
            pltpu.VMEM((RING - 1, rank, rows), f32),
            dma((chans // COLS,)), dma((6,)), dma((6,)), dma, dma((2,)), dma((2,)), dma((CHUNKS,)), dma((CHUNKS,)),
            two, two, two, two, two, two, two, two, dma((CHUNKS,)),
            dma((3,)), dma((3,)), dma, dma((4,)), dma((4,)),
            dma((count_sp - 1,)), dma((count_sp - 1,)), dma((count_rep - 1,)), dma((count_rep - 1,)),
            dma((count_sp - 1,)), dma((count_sp - 1,)), dma((count_rep - 1,)), dma((count_rep - 1,)),
            dma((count_rep - 1,)), dma((count_rep - 1,)), dma((3,)), dma((3,)),
        ],
        compiler_params=pltpu.CompilerParams(
            collective_id=0, has_side_effects=True, vmem_limit_bytes=58 * 1024 * 1024
        ),
        cost_estimate=pl.CostEstimate(flops=2 * rows * 16 * chans * band, bytes_accessed=10**7, transcendentals=0),
        name="compressed_step",
    )(frames, g, err, q_own)


def feedback_kernel(memory, q_parts, p_side, error_next, q_next, q_side):
    count, lines, rows = q_parts.shape
    block = memory.shape[0]

    @pl.when(pl.program_id(0) == 0)
    def _():
        for i in range(count):
            q_next[i * lines : (i + 1) * lines] = q_parts[i]
        q0, q1, q2 = split(q_next[...])
        q_side[...] = jnp.concatenate([q0, q0, q0, q1, q1, q2], axis=0).T

    at = pl.ds(pl.multiple_of(pl.program_id(0) * block, block), block)
    error_next[...] = memory[...] - jnp.dot(q_side[at, :], p_side[...], preferred_element_type=jnp.float32)


def feedback(memory, q_parts, p_side):
    rows, chans = memory.shape
    count, lines, _ = q_parts.shape
    rank = count * lines
    block = (rows // 4, chans)
    return pl.pallas_call(
        feedback_kernel,
        grid=(rows // block[0],),
        out_shape=(jax.ShapeDtypeStruct(memory.shape, jnp.float32), jax.ShapeDtypeStruct((rank, rows), jnp.float32)),
        in_specs=[
            pl.BlockSpec(block, lambda i: (i, 0)),
            pl.BlockSpec(q_parts.shape, lambda i: (0, 0, 0)),
            pl.BlockSpec(p_side.shape, lambda i: (0, 0)),
        ],
        out_specs=(pl.BlockSpec(block, lambda i: (i, 0)), pl.BlockSpec((rank, rows), lambda i: (0, 0))),
        scratch_shapes=[pltpu.VMEM((rows, 6 * rank), jnp.bfloat16)],
        compiler_params=pltpu.CompilerParams(vmem_limit_bytes=60 * 1024 * 1024),
        name="feedback",
    )(memory, q_parts, p_side)


def per_device(count_rep, frames, out_grad, error_prev, q_prev):
    band_rows, width, chans = frames.shape[1:]
    band = band_rows * width
    memory, q_parts, p_side = compressed_step(
        count_rep,
        frames[0].reshape(band, chans),
        out_grad[0].reshape(band, chans),
        error_prev[0],
        q_prev,
    )
    error_next, q_next = feedback(memory, q_parts, p_side)
    return (error_next[None], q_next)


def solution(mesh):
    placed = (
        P("rep", "sp", None, None),
        P("rep", "sp", None, None),
        P("rep", "sp", None),
        P(None, "sp"),
    )
    return jax.shard_map(
        functools.partial(per_device, mesh.shape["rep"]),
        mesh=mesh,
        in_specs=placed,
        out_specs=(P("rep", "sp", None), P(None, "sp")),
        check_vma=False,
    )
```

```python
import functools

import jax
import jax.numpy as jnp
from jax import lax
from jax.experimental import pallas as pl
from jax.experimental.pallas import tpu as pltpu
from jax.sharding import PartitionSpec as P

MESH = pl.DeviceIdType.MESH
RING = 4
CHUNKS = 8
COLS = 128
TAPS = 9
T_AT = 0
P_AT = (2, 3, 4, 5)
EARLY = 3


def sp_at(x, z):
    return {"sp": lax.rem(x + RING, RING) * RING + lax.rem(z + RING, RING)}


def remote(src, dst, send, recv, device):
    return pltpu.make_async_remote_copy(
        src_ref=src, dst_ref=dst, send_sem=send, recv_sem=recv, device_id=device, device_id_type=MESH
    )


def split(value):
    high = value.astype(jnp.bfloat16)
    rest = value - high.astype(jnp.float32)
    middle = rest.astype(jnp.bfloat16)
    low = (rest - middle.astype(jnp.float32)).astype(jnp.bfloat16)
    return high, middle, low


def exact_dot(a, b, contract):
    return lax.dot_general(
        a, b, (contract, ((), ())), precision=lax.Precision.HIGHEST, preferred_element_type=jnp.float32
    )


SCALE_ROWS = 16
RANGE = 1024.0


def encode(block):
    largest = jnp.max(jnp.abs(block), axis=(0, 1), keepdims=True)
    scale = jnp.maximum(largest * 1.01, 1e-30).astype(jnp.bfloat16)
    size = jnp.abs(block) * (RANGE / scale.astype(jnp.float32))
    second = size * size
    fourth = second * second
    twelfth = fourth * fourth * fourth
    signed = jnp.where(block < 0, -twelfth, twelfth).astype(jnp.bfloat16)
    return signed, jnp.broadcast_to(scale, (SCALE_ROWS, block.shape[1]))


def decode(coded):
    count = coded.shape[0] - SCALE_ROWS
    signed = coded[:count].astype(jnp.float32)
    scale = coded[count : count + 1].astype(jnp.float32) * (1.0 / RANGE)
    size = jnp.abs(signed)
    value = jnp.exp(jnp.log(jnp.maximum(size, 1e-37)) * (1.0 / 12.0)) * scale
    value = jnp.where(size < 1e-37, 0.0, value)
    return jnp.where(signed < 0, -value, value)


def step_kernel(
    count_rep, frames, g, err, q_own, memory, q_next, p_side,
    local, f_relay, t_relay, q_turned, q_taps, flipped, raw, halo, taps, gbuf, part, far_code, near_code, relay, piece, total,
    q_near, q_flip, t_term, t_near, p_src, p_near, p_one, p_far, p_all, work, q_src, q_got, q_sum, x_term, x_got,
    l_in, f_send, f_recv, f_own, h_send, h_recv, e_in, g_own,
    d_send, d_recv, r_send, r_recv, a_send, a_recv, b_send, b_recv, out_sem,
    q_send, q_recv, q_copy, t_send, t_recv, s1, r1, s2, r2, s3, r3, s4, r4, s5, r5, x_send, x_recv,
):
    sp, rep = lax.axis_index("sp"), lax.axis_index("rep")
    x, z = sp // RING, lax.rem(sp, RING)
    up, down = sp_at(x, z + 1), sp_at(x, z - 1)
    right, left = sp_at(x + 1, z), sp_at(x - 1, z)
    z_up, z_down = lax.rem(z + 1, RING), lax.rem(z + 3, RING)
    x_right, x_left, x_far = lax.rem(x + 1, RING), lax.rem(x + 3, RING), lax.rem(x + 2, RING)
    band = g.shape[0]
    half = band // 2
    count_sp = RING * RING
    share = part.shape[4] * 2
    width = halo.shape[3]
    rank = q_own.shape[0]

    def at_sp(d):
        return {"sp": lax.rem(sp + d, count_sp)}

    def at_rep(d):
        return {"rep": lax.rem(rep + d, count_rep)}

    near_z, far_z = (z_up, z_down), lax.rem(z + 2, RING)
    towards = (up, down)
    some_x = RING // 2

    def frames_near(side):
        return remote(flipped.at[:, near_z[side]], raw.at[z], f_send.at[side], f_recv.at[side], towards[side])

    def frames_near_in(side):
        return remote(flipped.at[:, z], raw.at[near_z[1 - side]], f_send.at[side], f_recv.at[side], up)

    def frames_far(side):
        part_x = pl.ds(side * some_x, some_x)
        return remote(
            flipped.at[part_x, far_z], f_relay.at[side], f_send.at[2 + side], f_recv.at[2 + side], towards[side]
        )

    def frames_on(side):
        part_x = pl.ds(side * some_x, some_x)
        return remote(
            f_relay.at[side], raw.at[near_z[1 - side], part_x], f_send.at[4 + side], f_recv.at[4 + side], towards[side]
        )

    def frames_far_in(side):
        part_x = pl.ds(side * some_x, some_x)
        return remote(f_relay.at[side], raw.at[far_z, part_x], f_send.at[4 + side], f_recv.at[4 + side], up)

    def columns(j):
        return pl.ds(pl.multiple_of(j * COLS, COLS), COLS)

    def slot(which, first, count):
        return pl.ds(pl.multiple_of(which * band + first, half), count)

    def own_grad(j):
        return pltpu.make_async_copy(g.at[:, columns(j)], gbuf.at[j, slot(z, 0, band)], g_own.at[j])

    def direct(j, side):
        ref = gbuf.at[j, slot(z, 0, band)]
        return remote(ref, ref, d_send.at[j, side], d_recv.at[j, side], up if side == 0 else down)

    def direct_in(j, side):
        ref = gbuf.at[j, slot(z_down if side == 0 else z_up, 0, band)]
        return remote(ref, ref, d_send.at[j, side], d_recv.at[j, side], up)

    def forward(j, side):
        ref = gbuf.at[j, slot(z_down if side == 0 else z_up, side * half, half)]
        return remote(ref, ref, r_send.at[j, side], r_recv.at[j, side], up if side == 0 else down)

    def forward_in(j, side):
        ref = gbuf.at[j, slot(lax.rem(z + 2, RING), side * half, half)]
        return remote(ref, ref, r_send.at[j, side], r_recv.at[j, side], up)

    def err_in(j):
        return pltpu.make_async_copy(err.at[:, columns(j)], total.at[j], e_in.at[j])

    def mem_out(j):
        return pltpu.make_async_copy(total.at[j], memory.at[:, columns(j)], out_sem.at[j])

    def far(j, side):
        return remote(
            far_code.at[j, side], relay.at[j, side], a_send.at[j, side], a_recv.at[j, side],
            right if side == 0 else left,
        )

    def near(j, side):
        return remote(
            near_code.at[j, side], piece.at[j, side], b_send.at[j, side], b_recv.at[j, side],
            right if side == 0 else left,
        )

    def q_out(step):
        return remote(q_taps, q_near.at[:, x], q_send.at[step - 1], q_recv.at[step - 1], sp_at(x + step, z))

    def q_in(step):
        source = lax.rem(x + RING - step, RING)
        return remote(q_taps, q_near.at[:, source], q_send.at[step - 1], q_recv.at[step - 1], right)

    def t_far(side):
        some = pl.ds(side * (rank // 2), rank // 2)
        return remote(t_term.at[far_z, some], t_relay.at[side], t_send.at[side], t_recv.at[side], towards[side])

    def t_out(side):
        return remote(
            t_term.at[near_z[side]], t_near.at[side], t_send.at[2 + side], t_recv.at[2 + side], towards[side]
        )

    def p_scatter(d):
        return remote(p_src.at[lax.rem(sp + d, count_sp)], p_near.at[d - 1], s1.at[d - 1], r1.at[d - 1], at_sp(d))

    def p_share(d):
        return remote(p_one, p_far.at[rep], s2.at[d - 1], r2.at[d - 1], at_rep(d))

    def p_share_in(d):
        source = lax.rem(rep + count_rep - d, count_rep)
        return remote(p_one, p_far.at[source], s2.at[d - 1], r2.at[d - 1], at_rep(d))

    def p_gather(d):
        return remote(p_all.at[sp], p_all.at[sp], s3.at[d - 1], r3.at[d - 1], at_sp(d))

    def p_gather_in(d):
        ref = p_all.at[lax.rem(sp + count_sp - d, count_sp)]
        return remote(ref, ref, s3.at[d - 1], r3.at[d - 1], at_sp(d))

    def x_out(step):
        return remote(x_term.at[step - 1], x_got.at[step - 1], x_send.at[step - 1], x_recv.at[step - 1], sp_at(x + step, z))

    def q_scatter(d):
        return remote(q_src.at[lax.rem(rep + d, count_rep)], q_got.at[d - 1], s4.at[d - 1], r4.at[d - 1], at_rep(d))

    def q_gather(d):
        return remote(q_next.at[rep], q_next.at[rep], s5.at[d - 1], r5.at[d - 1], at_rep(d))

    def q_gather_in(d):
        ref = q_next.at[lax.rem(rep + count_rep - d, count_rep)]
        return remote(ref, ref, s5.at[d - 1], r5.at[d - 1], at_rep(d))

    barrier = pltpu.get_barrier_semaphore()
    for d in range(1, count_sp):
        pl.semaphore_signal(barrier, inc=1, device_id=at_sp(d), device_id_type=MESH)
    for d in range(1, count_rep):
        pl.semaphore_signal(barrier, inc=1, device_id=at_rep(d), device_id_type=MESH)

    def column_in(i):
        return pltpu.make_async_copy(frames.at[:, columns(i)], local.at[i], l_in.at[i])

    pairs = frames.shape[1] // COLS
    owners = COLS // share
    own_grad(0).start()
    for i in range(pairs):
        column_in(i).start()
    pl.semaphore_wait(barrier, count_sp + count_rep - 2)
    own_grad(0).wait()
    direct(0, 0).start()
    direct(0, 1).start()

    per_x = RING // owners
    for first in range(per_x):
        for i in range(first, pairs, per_x):
            column_in(i).wait()
            turned = local[i].T
            for k in range(owners):
                owner = i * owners + k
                flipped[owner // RING, owner % RING] = turned[k * share : (k + 1) * share]
    for side in range(2):
        frames_far(side).start()
    for side in range(2):
        frames_near(side).start()
    own_frames = pltpu.make_async_copy(flipped.at[:, z], raw.at[z], f_own)
    own_frames.start()
    for j in range(CHUNKS):
        err_in(j).start()
    for j in range(1, CHUNKS):
        own_grad(j).start()

    thirds = [third.astype(jnp.float32) for third in split(q_own[...])]
    lanes = q_taps.shape[2]
    thirds.append(jnp.zeros((lanes - 3 * rank, q_own.shape[1]), jnp.float32))
    q_turned[...] = jnp.concatenate(thirds, axis=0).T
    for tap in range(TAPS):
        q_taps[tap] = q_turned[pl.ds(tap, share, stride=TAPS), :].astype(jnp.bfloat16)
    for step in (1, 3, 2):
        q_out(step).start()
    own_q = pltpu.make_async_copy(q_taps, q_near.at[:, x], q_copy)
    own_q.start()

    lane = lax.broadcasted_iota(jnp.int32, (RING * share, width), 1)

    def place(row, value):
        at = pl.ds(pl.multiple_of(row * width, width), width)
        wide = value.astype(jnp.float32)
        taps[0, :, at] = jnp.where(lane == 0, 0.0, pltpu.roll(wide, 1, 1)).astype(taps.dtype)
        taps[1, :, at] = value
        taps[2, :, at] = jnp.where(lane == width - 1, 0.0, pltpu.roll(wide, width - 1, 1)).astype(taps.dtype)

    def place_band(which):
        def place_row(row, carry):
            at = pl.ds(pl.multiple_of(row * width, width), width)
            place(which * (band // width) + row + 1, raw[which, :, :, at].reshape(RING * share, width))
            return carry

        lax.fori_loop(0, band // width, place_row, 0)

    def start_forward(j):
        for side in range(2):
            direct_in(j, side).wait_recv()
            forward(j, side).start()

    def start_direct(j):
        for side in range(2):
            direct(j, side).start()

    own_frames.wait()
    place_band(z)
    start_forward(0)
    for j in range(1, CHUNKS):
        own_grad(j).wait()

    for j in range(CHUNKS):
        err_in(j).wait()
        term = exact_dot(q_own[...], total[j], ((1,), (0,)))
        for h in range(2):
            p_src[2 * j + h] = term[h * (rank // 2) : (h + 1) * (rank // 2)]

    for side in range(2):
        frames_far(side).wait_recv()
        frames_on(side).start()
    for side in range(2):
        frames_near_in(side).wait_recv()
    start_direct(1)
    place_band(z_down)
    place_band(z_up)
    for side in range(2):
        frames_far_in(side).wait_recv()

    bottom = raw.at[RING - 1, :, :, band - width : band]
    above = remote(bottom, halo.at[0], h_send.at[0], h_recv.at[0], right)
    below = remote(raw.at[0, :, :, 0:width], halo.at[1], h_send.at[1], h_recv.at[1], left)
    above.start()
    below.start()
    place_band(lax.rem(z + 2, RING))
    rows = RING * band // width
    above.wait()
    below.wait()
    zero = jnp.zeros((RING * share, width), halo.dtype)
    place(0, jnp.where(x == 0, zero, halo[0].reshape(RING * share, width)))
    place(rows + 1, jnp.where(x == RING - 1, zero, halo[1].reshape(RING * share, width)))

    def t_band(which):
        acc = None
        for a in range(3):
            at = pl.ds(pl.multiple_of(which * band + a * width, width), band)
            stacked = taps[:, :, at].reshape(3 * RING * share, band)
            term = jnp.dot(q_flip[a], stacked, preferred_element_type=jnp.float32)
            acc = term if acc is None else acc + term
        t_term[which] = acc[:rank] + (acc[rank : 2 * rank] + acc[2 * rank : 3 * rank])

    def t_start():
        own_q.wait()
        for step in (1, 3, 2):
            q_in(step).wait_recv()
        for a in range(3):
            q_flip[a] = q_near[3 * a : 3 * a + 3].reshape(3 * RING * share, lanes).T

    def t_bands(first):
        def one(i, carry):
            t_band(first + i)
            return carry

        lax.fori_loop(0, RING // 2, one, 0)

    def t_finish():
        for side in range(2):
            t_far(side).start()

    def t_pass_on():
        for side in range(2):
            some = pl.ds(side * (rank // 2), rank // 2)
            t_far(side).wait_recv()
            t_term[near_z[side], some] = t_term[near_z[side], some] + t_relay[side]
            t_out(side).start()

    def p_terms():
        for side in range(2):
            t_out(side).wait_recv()
        full = t_term[z] + (t_near[0] + t_near[1])
        parts = jnp.concatenate(split(full), axis=0)

        def add(j, carry):
            acc = jnp.dot(parts, gbuf[j, slot(z, 0, band)], preferred_element_type=jnp.float32)
            term = acc[:rank] + (acc[rank : 2 * rank] + acc[2 * rank :])
            for h in range(2):
                p_src[2 * j + h] = p_src[2 * j + h] + term[h * (rank // 2) : (h + 1) * (rank // 2)]
            return carry

        lax.fori_loop(0, CHUNKS, add, 0)
        for d in range(1, count_sp):
            p_scatter(d).start()

    def p_sum_sp():
        acc = p_src[sp]
        for d in range(1, count_sp):
            p_scatter(d).wait_recv()
            acc = acc + p_near[d - 1]
        p_one[...] = acc
        p_far[rep] = acc
        for d in range(1, count_rep):
            p_share(d).start()

    def p_sum_rep():
        for d in range(1, count_rep):
            p_share_in(d).wait_recv()
        acc = p_far[0]
        for i in range(1, count_rep):
            acc = acc + p_far[i]
        p_all[sp] = acc
        for d in range(1, count_sp):
            p_gather(d).start()

    def p_chunk(j):
        return jnp.concatenate([p_all[2 * j], p_all[2 * j + 1]], axis=0)

    def orthogonal():
        for d in range(1, count_sp):
            p_gather_in(d).wait_recv()
        p_total = jnp.concatenate([p_chunk(j) for j in range(CHUNKS)], axis=1)
        gram = exact_dot(p_total, p_total, ((1,), (1,)))
        row_at = lax.broadcasted_iota(jnp.int32, (rank, rank), 0)
        col_at = lax.broadcasted_iota(jnp.int32, (rank, rank), 1)
        work[:, :rank] = gram
        work[:, rank : 2 * rank] = jnp.where(row_at == col_at, 1.0, 0.0)
        shape = (rank, 2 * rank)
        line = lax.broadcasted_iota(jnp.int32, shape, 0)
        spot = lax.broadcasted_iota(jnp.int32, shape, 1)

        def eliminate(k, carry):
            state = work[:, : 2 * rank]
            pivot = work[pl.ds(k, 1), : 2 * rank]
            column = jnp.sum(jnp.where(spot == k, state, 0.0), axis=1, keepdims=True)
            diagonal = jnp.sum(jnp.where(spot[:1] == k, pivot, 0.0), axis=1, keepdims=True)
            inverse = 1.0 / jnp.sqrt(diagonal)
            pivot = pivot * inverse
            work[:, : 2 * rank] = jnp.where(
                line > k, state - (column * inverse) * pivot, jnp.where(line == k, pivot, state)
            )
            return carry

        lax.fori_loop(0, rank, eliminate, 0)
        lower_inverse = jnp.where(col_at <= row_at, work[:, rank : 2 * rank], 0.0)
        whole = exact_dot(lower_inverse, p_total, ((1,), (0,)))
        p0, p1, p2 = split(whole)
        p_side[...] = jnp.concatenate([p0, p1, p2, p0, p1, p0], axis=0)
        q_sum[...] = jnp.zeros_like(q_sum)

    def by_p(rows_of, k):
        m0, m1, m2 = split(rows_of)
        m_side = jnp.concatenate([m0, m0, m0, m1, m1, m2], axis=1)
        across = jnp.concatenate([p_side[i * rank : (i + 1) * rank, columns(k)] for i in range(6)], axis=1)
        return jnp.dot(m_side, across.T, preferred_element_type=jnp.float32)

    def add_q(k):
        q_sum[:, :rank] = q_sum[:, :rank] + by_p(total[k], k)

    last = CHUNKS - 1

    def last_terms():
        for step in (1, 3, 2):
            owner = lax.rem(x + step, RING)
            terms = by_p(part[last, owner].reshape(q_sum.shape[0], COLS), last)
            x_term[step - 1] = terms.T
            x_out(step).start()

    def last_own():
        count = part.shape[4]
        for side in range(2):
            for tap in range(TAPS):
                at = pl.ds(side * count * TAPS + tap, count, stride=TAPS)
                total[last, at, :] = total[last, at, :] + part[last, x, side, tap]
        add_q(last)

    def last_sum():
        for step in (1, 3, 2):
            x_out(step).wait_recv()
        got = x_got[0] + x_got[1] + x_got[2]
        filled = jnp.concatenate([got, jnp.zeros((128 - rank, got.shape[1]), jnp.float32)], axis=0).T
        count = part.shape[4]
        for side in range(2):
            for tap in range(TAPS):
                at = pl.ds(side * count * TAPS + tap, count, stride=TAPS)
                line = (side * TAPS + tap) * count
                q_sum[at, :] = q_sum[at, :] + filled[line : line + count]

    def multiply(first, count, after):
        depth = gbuf.shape[1]
        per_side = part.shape[4]

        def one(a, carry):
            at = pl.ds(pl.multiple_of(a * width, width), depth)
            stacked = taps[:, :, at].reshape(3 * RING * share, depth)
            chosen = gbuf[first] if count == 1 else jnp.concatenate([gbuf[first], gbuf[first + 1]], axis=1)
            product = jnp.dot(stacked, chosen, preferred_element_type=jnp.float32)
            for c in range(count):
                for b in range(3):
                    for owner in range(RING):
                        for side in range(2):
                            line = b * RING * share + (owner * 2 + side) * per_side
                            part[first + c, owner, side, a * 3 + b] = product[
                                line : line + per_side, c * COLS : (c + 1) * COLS
                            ]
            @pl.when((a == 0) & (after < CHUNKS))
            def _():
                start_forward(after)

            @pl.when((a == 0) & (after + 1 < CHUNKS))
            def _():
                start_direct(after + 1)

            return carry

        lax.fori_loop(0, 3, one, 0)
        for c in range(count):
            for side in range(2):
                put(far_code.at[first + c, side], part[first + c, x_far, side].reshape(half_rows, COLS))
                far(first + c, side).start()

    half_rows = TAPS * part.shape[4]

    def put(ref, block):
        signed, scale = encode(block)
        ref[:half_rows] = signed
        ref[half_rows:] = scale

    def pass_on(k):
        for side, owner in ((0, x_right), (1, x_left)):
            put(near_code.at[k, side, 1 - side], part[k, owner, 1 - side].reshape(half_rows, COLS))
            far(k, side).wait_recv()
            both = part[k, owner, side].reshape(half_rows, COLS) + decode(relay[k, side])
            put(near_code.at[k, side, side], both)
            near(k, side).start()

    def add_near(k, own):
        count = part.shape[4]
        for side in range(2):
            got = decode(piece[k, 0, side]) + decode(piece[k, 1, side])
            for tap in range(TAPS):
                at = pl.ds(side * count * TAPS + tap, count, stride=TAPS)
                term = got[tap * count : (tap + 1) * count]
                if own:
                    term = term + part[k, x, side, tap]
                total[k, at, :] = total[k, at, :] + term

    def complete(k, with_q):
        near(k, 0).wait_recv()
        near(k, 1).wait_recv()
        add_near(k, True)
        mem_out(k).start()
        pl.when(with_q)(lambda: add_q(k))

    def complete_last():
        near(last, 0).wait_recv()
        near(last, 1).wait_recv()
        add_near(last, False)
        mem_out(last).start()

    def over(first, count, body):
        def one(i, carry):
            body(first + i)
            return carry

        lax.fori_loop(0, count, one, 0)

    def step(j, carry):
        @pl.when(j < CHUNKS)
        def _():
            forward_in(j, 0).wait_recv()
            forward_in(j, 1).wait_recv()

        alone = (j == 0) | (j == CHUNKS - 1)
        even = lax.rem(j, 2) == 0
        pl.when(alone)(lambda: multiply(j, 1, j + 1))
        pl.when((j > 0) & (j < CHUNKS - 1) & even)(lambda: multiply(j - 1, 2, j + 1))

        @pl.when((j < CHUNKS - 1) & jnp.logical_not(even))
        def _():
            start_forward(j + 1)
            pl.when(j + 2 < CHUNKS)(lambda: start_direct(j + 2))


        pl.when((j == 1) | (j == CHUNKS))(lambda: pass_on(j - 1))
        pl.when((j > 1) & (j < CHUNKS) & jnp.logical_not(even))(lambda: over(j - 2, 2, pass_on))

        @pl.when(j == T_AT)
        def _():
            t_start()
            t_bands(0)
            t_bands(RING // 2)
            t_finish()

        pl.when(j == T_AT + 1)(t_pass_on)
        pl.when(j == last)(last_terms)

        for at, stage in zip(P_AT, (p_terms, p_sum_sp, p_sum_rep, orthogonal)):
            pl.when(j == at)(stage)
        ready = j >= P_AT[-1]

        pl.when(j == 2)(lambda: complete(0, ready))
        pl.when((j > 2) & (j <= CHUNKS) & even)(lambda: over(j - 3, 2, lambda k: complete(k, ready)))
        pl.when(j == P_AT[-1])(lambda: over(0, EARLY, add_q))

        return carry

    lax.fori_loop(0, CHUNKS + 1, step, 0)
    last_own()
    last_sum()

    lines = rank // count_rep
    q_lines = q_sum[...].T
    for i in range(count_rep):
        q_src[i] = q_lines[i * lines : (i + 1) * lines]
    for d in range(1, count_rep):
        q_scatter(d).start()
    acc = q_src[rep]
    for d in range(1, count_rep):
        q_scatter(d).wait_recv()
        acc = acc + q_got[d - 1]
    q_next[rep] = acc * (1.0 / count_rep)
    for d in range(1, count_rep):
        q_gather(d).start()
    complete_last()
    for d in range(1, count_rep):
        q_gather_in(d).wait_recv()

    def finish(j, carry):
        for side in range(2):
            direct(j, side).wait_send()
            forward(j, side).wait_send()
            far(j, side).wait_send()
            near(j, side).wait_send()
        mem_out(j).wait()
        return carry

    lax.fori_loop(0, CHUNKS, finish, 0)
    for side in range(2):
        frames_near(side).wait_send()
        frames_far(side).wait_send()
        frames_on(side).wait_send()
        t_far(side).wait_send()
        t_out(side).wait_send()
    for step_ in (1, 3, 2):
        q_out(step_).wait_send()
        x_out(step_).wait_send()
    for d in range(1, count_sp):
        p_scatter(d).wait_send()
        p_gather(d).wait_send()
    for d in range(1, count_rep):
        p_share(d).wait_send()
        q_scatter(d).wait_send()
        q_gather(d).wait_send()


def compressed_step(count_rep, frames, g, err, q_own):
    band, chans = g.shape
    width = band // 4
    rows = err.shape[0]
    rank = q_own.shape[0]
    count_sp = RING * RING
    share = chans // count_sp
    per_side = share // 2
    code_rows = TAPS * per_side + SCALE_ROWS
    dma = pltpu.SemaphoreType.DMA
    two = dma((CHUNKS, 2))
    f32, bf16 = jnp.float32, jnp.bfloat16
    any_spec, vmem_spec = pl.BlockSpec(memory_space=pl.ANY), pl.BlockSpec(memory_space=pltpu.VMEM)
    p_block = (rank // 2, COLS)
    q_block = (rank // count_rep, rows)
    return pl.pallas_call(
        functools.partial(step_kernel, count_rep),
        out_shape=(
            jax.ShapeDtypeStruct((rows, chans), f32),
            jax.ShapeDtypeStruct((count_rep, *q_block), f32),
            jax.ShapeDtypeStruct((6 * rank, chans), bf16),
        ),
        in_specs=[any_spec, any_spec, any_spec, vmem_spec],
        out_specs=(any_spec, vmem_spec, vmem_spec),
        scratch_shapes=[
            pltpu.VMEM((chans // COLS, band, COLS), bf16),
            pltpu.VMEM((2, RING // 2, share, band), bf16),
            pltpu.VMEM((2, rank // 2, band), f32),
            pltpu.VMEM((rows, 128), f32),
            pltpu.VMEM((TAPS, share, 128), bf16),
            pltpu.VMEM((RING, RING, share, band), bf16),
            pltpu.VMEM((RING, RING, share, band), bf16),
            pltpu.VMEM((2, RING, share, width), bf16),
            pltpu.VMEM((3, RING * share, RING * band + 2 * width), bf16),
            pltpu.VMEM((CHUNKS, RING * band, COLS), bf16),
            pltpu.VMEM((CHUNKS, RING, 2, TAPS, per_side, COLS), f32),
            pltpu.VMEM((CHUNKS, 2, code_rows, COLS), bf16),
            pltpu.VMEM((CHUNKS, 2, 2, code_rows, COLS), bf16),
            pltpu.VMEM((CHUNKS, 2, code_rows, COLS), bf16),
            pltpu.VMEM((CHUNKS, 2, 2, code_rows, COLS), bf16),
            pltpu.VMEM((CHUNKS, rows, COLS), f32),
            pltpu.VMEM((TAPS, RING, share, 128), bf16),
            pltpu.VMEM((3, 128, 3 * RING * share), bf16),
            pltpu.VMEM((RING, rank, band), f32),
            pltpu.VMEM((2, rank, band), f32),
            pltpu.VMEM((count_sp, *p_block), f32),
            pltpu.VMEM((count_sp - 1, *p_block), f32),
            pltpu.VMEM(p_block, f32),
            pltpu.VMEM((count_rep, *p_block), f32),
            pltpu.VMEM((count_sp, *p_block), f32),
            pltpu.VMEM((rank, 128), f32),
            pltpu.VMEM((count_rep, *q_block), f32),
            pltpu.VMEM((count_rep - 1, *q_block), f32),
            pltpu.VMEM((rows, 128), f32),
            pltpu.VMEM((RING - 1, rank, rows), f32),
            pltpu.VMEM((RING - 1, rank, rows), f32),
            dma((chans // COLS,)), dma((6,)), dma((6,)), dma, dma((2,)), dma((2,)), dma((CHUNKS,)), dma((CHUNKS,)),
            two, two, two, two, two, two, two, two, dma((CHUNKS,)),
            dma((3,)), dma((3,)), dma, dma((4,)), dma((4,)),
            dma((count_sp - 1,)), dma((count_sp - 1,)), dma((count_rep - 1,)), dma((count_rep - 1,)),
            dma((count_sp - 1,)), dma((count_sp - 1,)), dma((count_rep - 1,)), dma((count_rep - 1,)),
            dma((count_rep - 1,)), dma((count_rep - 1,)), dma((3,)), dma((3,)),
        ],
        compiler_params=pltpu.CompilerParams(
            collective_id=0, has_side_effects=True, vmem_limit_bytes=58 * 1024 * 1024
        ),
        cost_estimate=pl.CostEstimate(flops=2 * rows * 16 * chans * band, bytes_accessed=10**7, transcendentals=0),
        name="compressed_step",
    )(frames, g, err, q_own)


def feedback_kernel(memory, q_parts, p_side, error_next, q_next, q_side):
    count, lines, rows = q_parts.shape
    block = memory.shape[0]

    @pl.when(pl.program_id(0) == 0)
    def _():
        for i in range(count):
            q_next[i * lines : (i + 1) * lines] = q_parts[i]
        q0, q1, q2 = split(q_next[...])
        q_side[...] = jnp.concatenate([q0, q0, q0, q1, q1, q2], axis=0).T

    at = pl.ds(pl.multiple_of(pl.program_id(0) * block, block), block)
    error_next[...] = memory[...] - jnp.dot(q_side[at, :], p_side[...], preferred_element_type=jnp.float32)


def feedback(memory, q_parts, p_side):
    rows, chans = memory.shape
    count, lines, _ = q_parts.shape
    rank = count * lines
    block = (rows // 4, chans)
    return pl.pallas_call(
        feedback_kernel,
        grid=(rows // block[0],),
        out_shape=(jax.ShapeDtypeStruct(memory.shape, jnp.float32), jax.ShapeDtypeStruct((rank, rows), jnp.float32)),
        in_specs=[
            pl.BlockSpec(block, lambda i: (i, 0)),
            pl.BlockSpec(q_parts.shape, lambda i: (0, 0, 0)),
            pl.BlockSpec(p_side.shape, lambda i: (0, 0)),
        ],
        out_specs=(pl.BlockSpec(block, lambda i: (i, 0)), pl.BlockSpec((rank, rows), lambda i: (0, 0))),
        scratch_shapes=[pltpu.VMEM((rows, 6 * rank), jnp.bfloat16)],
        compiler_params=pltpu.CompilerParams(vmem_limit_bytes=60 * 1024 * 1024),
        name="feedback",
    )(memory, q_parts, p_side)


def per_device(count_rep, frames, out_grad, error_prev, q_prev):
    band_rows, width, chans = frames.shape[1:]
    band = band_rows * width
    memory, q_parts, p_side = compressed_step(
        count_rep,
        frames[0].reshape(band, chans),
        out_grad[0].reshape(band, chans),
        error_prev[0],
        q_prev,
    )
    error_next, q_next = feedback(memory, q_parts, p_side)
    return (error_next[None], q_next)


def solution(mesh):
    placed = (
        P("rep", "sp", None, None),
        P("rep", "sp", None, None),
        P("rep", "sp", None),
        P(None, "sp"),
    )
    return jax.shard_map(
        functools.partial(per_device, mesh.shape["rep"]),
        mesh=mesh,
        in_specs=placed,
        out_specs=(P("rep", "sp", None), P(None, "sp")),
        check_vma=False,
    )
```

```python
import functools

import jax
import jax.numpy as jnp
from jax import lax
from jax.experimental import pallas as pl
from jax.experimental.pallas import tpu as pltpu
from jax.sharding import PartitionSpec as P

MESH = pl.DeviceIdType.MESH
RING = 4
CHUNKS = 8
COLS = 128
TAPS = 9
T_AT = 0
P_AT = (2, 3, 4, 5)
EARLY = 3


def sp_at(x, z):
    return {"sp": lax.rem(x + RING, RING) * RING + lax.rem(z + RING, RING)}


def remote(src, dst, send, recv, device):
    return pltpu.make_async_remote_copy(
        src_ref=src, dst_ref=dst, send_sem=send, recv_sem=recv, device_id=device, device_id_type=MESH
    )


def split(value):
    high = value.astype(jnp.bfloat16)
    rest = value - high.astype(jnp.float32)
    middle = rest.astype(jnp.bfloat16)
    low = (rest - middle.astype(jnp.float32)).astype(jnp.bfloat16)
    return high, middle, low


def exact_dot(a, b, contract):
    return lax.dot_general(
        a, b, (contract, ((), ())), precision=lax.Precision.HIGHEST, preferred_element_type=jnp.float32
    )


SCALE_ROWS = 16
RANGE = 1024.0


def encode(block):
    largest = jnp.max(jnp.abs(block), axis=(0, 1), keepdims=True)
    scale = jnp.maximum(largest * 1.01, 1e-30).astype(jnp.bfloat16)
    size = jnp.abs(block) * (RANGE / scale.astype(jnp.float32))
    second = size * size
    fourth = second * second
    twelfth = fourth * fourth * fourth
    signed = jnp.where(block < 0, -twelfth, twelfth).astype(jnp.bfloat16)
    return signed, jnp.broadcast_to(scale, (SCALE_ROWS, block.shape[1]))


def decode(coded):
    count = coded.shape[0] - SCALE_ROWS
    signed = coded[:count].astype(jnp.float32)
    scale = coded[count : count + 1].astype(jnp.float32) * (1.0 / RANGE)
    size = jnp.abs(signed)
    value = jnp.exp(jnp.log(jnp.maximum(size, 1e-37)) * (1.0 / 12.0)) * scale
    value = jnp.where(size < 1e-37, 0.0, value)
    return jnp.where(signed < 0, -value, value)


def step_kernel(
    count_rep, frames, g, err, q_own, memory, q_next, p_side,
    local, f_relay, t_relay, q_turned, q_taps, flipped, raw, halo, taps, gbuf, part, far_code, near_code, relay, piece, total,
    q_near, q_flip, t_term, t_near, p_src, p_near, p_one, p_far, p_all, work, q_src, q_got, q_sum, x_term, x_got,
    l_in, f_send, f_recv, f_own, h_send, h_recv, e_in, g_own,
    d_send, d_recv, r_send, r_recv, a_send, a_recv, b_send, b_recv, out_sem,
    q_send, q_recv, q_copy, t_send, t_recv, s1, r1, s2, r2, s3, r3, s4, r4, s5, r5, x_send, x_recv,
):
    sp, rep = lax.axis_index("sp"), lax.axis_index("rep")
    x, z = sp // RING, lax.rem(sp, RING)
    up, down = sp_at(x, z + 1), sp_at(x, z - 1)
    right, left = sp_at(x + 1, z), sp_at(x - 1, z)
    z_up, z_down = lax.rem(z + 1, RING), lax.rem(z + 3, RING)
    x_right, x_left, x_far = lax.rem(x + 1, RING), lax.rem(x + 3, RING), lax.rem(x + 2, RING)
    band = g.shape[0]
    half = band // 2
    count_sp = RING * RING
    share = part.shape[4] * 2
    width = halo.shape[3]
    rank = q_own.shape[0]

    def at_sp(d):
        return {"sp": lax.rem(sp + d, count_sp)}

    def at_rep(d):
        return {"rep": lax.rem(rep + d, count_rep)}

    near_z, far_z = (z_up, z_down), lax.rem(z + 2, RING)
    towards = (up, down)
    some_x = RING // 2

    def frames_near(side):
        return remote(flipped.at[:, near_z[side]], raw.at[z], f_send.at[side], f_recv.at[side], towards[side])

    def frames_near_in(side):
        return remote(flipped.at[:, z], raw.at[near_z[1 - side]], f_send.at[side], f_recv.at[side], up)

    def frames_far(side):
        part_x = pl.ds(side * some_x, some_x)
        return remote(
            flipped.at[part_x, far_z], f_relay.at[side], f_send.at[2 + side], f_recv.at[2 + side], towards[side]
        )

    def frames_on(side):
        part_x = pl.ds(side * some_x, some_x)
        return remote(
            f_relay.at[side], raw.at[near_z[1 - side], part_x], f_send.at[4 + side], f_recv.at[4 + side], towards[side]
        )

    def frames_far_in(side):
        part_x = pl.ds(side * some_x, some_x)
        return remote(f_relay.at[side], raw.at[far_z, part_x], f_send.at[4 + side], f_recv.at[4 + side], up)

    def columns(j):
        return pl.ds(pl.multiple_of(j * COLS, COLS), COLS)

    def slot(which, first, count):
        return pl.ds(pl.multiple_of(which * band + first, half), count)

    def own_grad(j):
        return pltpu.make_async_copy(g.at[:, columns(j)], gbuf.at[j, slot(z, 0, band)], g_own.at[j])

    def direct(j, side):
        ref = gbuf.at[j, slot(z, 0, band)]
        return remote(ref, ref, d_send.at[j, side], d_recv.at[j, side], up if side == 0 else down)

    def direct_in(j, side):
        ref = gbuf.at[j, slot(z_down if side == 0 else z_up, 0, band)]
        return remote(ref, ref, d_send.at[j, side], d_recv.at[j, side], up)

    def forward(j, side):
        ref = gbuf.at[j, slot(z_down if side == 0 else z_up, side * half, half)]
        return remote(ref, ref, r_send.at[j, side], r_recv.at[j, side], up if side == 0 else down)

    def forward_in(j, side):
        ref = gbuf.at[j, slot(lax.rem(z + 2, RING), side * half, half)]
        return remote(ref, ref, r_send.at[j, side], r_recv.at[j, side], up)

    def err_in(j):
        return pltpu.make_async_copy(err.at[:, columns(j)], total.at[j], e_in.at[j])

    def mem_out(j):
        return pltpu.make_async_copy(total.at[j], memory.at[:, columns(j)], out_sem.at[j])

    def far(j, side):
        return remote(
            far_code.at[j, side], relay.at[j, side], a_send.at[j, side], a_recv.at[j, side],
            right if side == 0 else left,
        )

    def near(j, side):
        return remote(
            near_code.at[j, side], piece.at[j, side], b_send.at[j, side], b_recv.at[j, side],
            right if side == 0 else left,
        )

    def q_out(step):
        return remote(q_taps, q_near.at[:, x], q_send.at[step - 1], q_recv.at[step - 1], sp_at(x + step, z))

    def q_in(step):
        source = lax.rem(x + RING - step, RING)
        return remote(q_taps, q_near.at[:, source], q_send.at[step - 1], q_recv.at[step - 1], right)

    def t_far(side):
        some = pl.ds(side * (rank // 2), rank // 2)
        return remote(t_term.at[far_z, some], t_relay.at[side], t_send.at[side], t_recv.at[side], towards[side])

    def t_out(side):
        return remote(
            t_term.at[near_z[side]], t_near.at[side], t_send.at[2 + side], t_recv.at[2 + side], towards[side]
        )

    def p_scatter(d):
        return remote(p_src.at[lax.rem(sp + d, count_sp)], p_near.at[d - 1], s1.at[d - 1], r1.at[d - 1], at_sp(d))

    def p_share(d):
        return remote(p_one, p_far.at[rep], s2.at[d - 1], r2.at[d - 1], at_rep(d))

    def p_share_in(d):
        source = lax.rem(rep + count_rep - d, count_rep)
        return remote(p_one, p_far.at[source], s2.at[d - 1], r2.at[d - 1], at_rep(d))

    def p_gather(d):
        return remote(p_all.at[sp], p_all.at[sp], s3.at[d - 1], r3.at[d - 1], at_sp(d))

    def p_gather_in(d):
        ref = p_all.at[lax.rem(sp + count_sp - d, count_sp)]
        return remote(ref, ref, s3.at[d - 1], r3.at[d - 1], at_sp(d))

    def x_out(step):
        return remote(x_term.at[step - 1], x_got.at[step - 1], x_send.at[step - 1], x_recv.at[step - 1], sp_at(x + step, z))

    def q_scatter(d):
        return remote(q_src.at[lax.rem(rep + d, count_rep)], q_got.at[d - 1], s4.at[d - 1], r4.at[d - 1], at_rep(d))

    def q_gather(d):
        return remote(q_next.at[rep], q_next.at[rep], s5.at[d - 1], r5.at[d - 1], at_rep(d))

    def q_gather_in(d):
        ref = q_next.at[lax.rem(rep + count_rep - d, count_rep)]
        return remote(ref, ref, s5.at[d - 1], r5.at[d - 1], at_rep(d))

    barrier = pltpu.get_barrier_semaphore()
    for d in range(1, count_sp):
        pl.semaphore_signal(barrier, inc=1, device_id=at_sp(d), device_id_type=MESH)
    for d in range(1, count_rep):
        pl.semaphore_signal(barrier, inc=1, device_id=at_rep(d), device_id_type=MESH)

    def column_in(i):
        return pltpu.make_async_copy(frames.at[:, columns(i)], local.at[i], l_in.at[i])

    pairs = frames.shape[1] // COLS
    owners = COLS // share
    own_grad(0).start()
    for i in range(pairs):
        column_in(i).start()
    pl.semaphore_wait(barrier, count_sp + count_rep - 2)
    own_grad(0).wait()
    direct(0, 0).start()
    direct(0, 1).start()

    per_x = RING // owners
    for first in range(per_x):
        for i in range(first, pairs, per_x):
            column_in(i).wait()
            turned = local[i].T
            for k in range(owners):
                owner = i * owners + k
                flipped[owner // RING, owner % RING] = turned[k * share : (k + 1) * share]
    for side in range(2):
        frames_far(side).start()
    for side in range(2):
        frames_near(side).start()
    own_frames = pltpu.make_async_copy(flipped.at[:, z], raw.at[z], f_own)
    own_frames.start()
    for j in range(CHUNKS):
        err_in(j).start()
    for j in range(1, CHUNKS):
        own_grad(j).start()

    thirds = [third.astype(jnp.float32) for third in split(q_own[...])]
    lanes = q_taps.shape[2]
    thirds.append(jnp.zeros((lanes - 3 * rank, q_own.shape[1]), jnp.float32))
    q_turned[...] = jnp.concatenate(thirds, axis=0).T
    for tap in range(TAPS):
        q_taps[tap] = q_turned[pl.ds(tap, share, stride=TAPS), :].astype(jnp.bfloat16)
    for step in (1, 3, 2):
        q_out(step).start()
    own_q = pltpu.make_async_copy(q_taps, q_near.at[:, x], q_copy)
    own_q.start()

    lane = lax.broadcasted_iota(jnp.int32, (RING * share, width), 1)

    def place(row, value):
        at = pl.ds(pl.multiple_of(row * width, width), width)
        wide = value.astype(jnp.float32)
        taps[0, :, at] = jnp.where(lane == 0, 0.0, pltpu.roll(wide, 1, 1)).astype(taps.dtype)
        taps[1, :, at] = value
        taps[2, :, at] = jnp.where(lane == width - 1, 0.0, pltpu.roll(wide, width - 1, 1)).astype(taps.dtype)

    def place_band(which):
        def place_row(row, carry):
            at = pl.ds(pl.multiple_of(row * width, width), width)
            place(which * (band // width) + row + 1, raw[which, :, :, at].reshape(RING * share, width))
            return carry

        lax.fori_loop(0, band // width, place_row, 0)

    def start_forward(j):
        for side in range(2):
            direct_in(j, side).wait_recv()
            forward(j, side).start()

    def start_direct(j):
        for side in range(2):
            direct(j, side).start()

    own_frames.wait()
    place_band(z)
    start_forward(0)
    for j in range(1, CHUNKS):
        own_grad(j).wait()

    for side in range(2):
        frames_far(side).wait_recv()
        frames_on(side).start()

    for j in range(CHUNKS):
        err_in(j).wait()
    q0, q1, _ = split(q_own[...])
    both = jnp.concatenate([q0, q1], axis=0)

    def p_start(i, carry):
        j = 2 * i
        e0, e1, _ = split(jnp.concatenate([total[j], total[j + 1]], axis=1))
        main = jnp.dot(both, e0, preferred_element_type=jnp.float32)
        term = main[:rank] + (main[rank:] + jnp.dot(q0, e1, preferred_element_type=jnp.float32))
        for c in range(2):
            for h in range(2):
                p_src[2 * (j + c) + h] = term[h * (rank // 2) : (h + 1) * (rank // 2), c * COLS : (c + 1) * COLS]
        return carry

    lax.fori_loop(0, CHUNKS // 2, p_start, 0)

    for side in range(2):
        frames_near_in(side).wait_recv()
    start_direct(1)
    place_band(z_down)
    place_band(z_up)
    for side in range(2):
        frames_far_in(side).wait_recv()

    bottom = raw.at[RING - 1, :, :, band - width : band]
    above = remote(bottom, halo.at[0], h_send.at[0], h_recv.at[0], right)
    below = remote(raw.at[0, :, :, 0:width], halo.at[1], h_send.at[1], h_recv.at[1], left)
    above.start()
    below.start()
    place_band(lax.rem(z + 2, RING))
    rows = RING * band // width
    above.wait()
    below.wait()
    zero = jnp.zeros((RING * share, width), halo.dtype)
    place(0, jnp.where(x == 0, zero, halo[0].reshape(RING * share, width)))
    place(rows + 1, jnp.where(x == RING - 1, zero, halo[1].reshape(RING * share, width)))

    def t_band(which):
        acc = None
        for a in range(3):
            at = pl.ds(pl.multiple_of(which * band + a * width, width), band)
            stacked = taps[:, :, at].reshape(3 * RING * share, band)
            term = jnp.dot(q_flip[a], stacked, preferred_element_type=jnp.float32)
            acc = term if acc is None else acc + term
        t_term[which] = acc[:rank] + (acc[rank : 2 * rank] + acc[2 * rank : 3 * rank])

    def t_start():
        own_q.wait()
        for step in (1, 3, 2):
            q_in(step).wait_recv()
        for a in range(3):
            q_flip[a] = q_near[3 * a : 3 * a + 3].reshape(3 * RING * share, lanes).T

    def t_bands(first):
        def one(i, carry):
            t_band(first + i)
            return carry

        lax.fori_loop(0, RING // 2, one, 0)

    def t_finish():
        for side in range(2):
            t_far(side).start()

    def t_pass_on():
        for side in range(2):
            some = pl.ds(side * (rank // 2), rank // 2)
            t_far(side).wait_recv()
            t_term[near_z[side], some] = t_term[near_z[side], some] + t_relay[side]
            t_out(side).start()

    def p_terms():
        for side in range(2):
            t_out(side).wait_recv()
        full = t_term[z] + (t_near[0] + t_near[1])
        parts = jnp.concatenate(split(full), axis=0)

        def add(j, carry):
            acc = jnp.dot(parts, gbuf[j, slot(z, 0, band)], preferred_element_type=jnp.float32)
            term = acc[:rank] + (acc[rank : 2 * rank] + acc[2 * rank :])
            for h in range(2):
                p_src[2 * j + h] = p_src[2 * j + h] + term[h * (rank // 2) : (h + 1) * (rank // 2)]
            return carry

        lax.fori_loop(0, CHUNKS, add, 0)
        for d in range(1, count_sp):
            p_scatter(d).start()

    def p_sum_sp():
        acc = p_src[sp]
        for d in range(1, count_sp):
            p_scatter(d).wait_recv()
            acc = acc + p_near[d - 1]
        p_one[...] = acc
        p_far[rep] = acc
        for d in range(1, count_rep):
            p_share(d).start()

    def p_sum_rep():
        for d in range(1, count_rep):
            p_share_in(d).wait_recv()
        acc = p_far[0]
        for i in range(1, count_rep):
            acc = acc + p_far[i]
        p_all[sp] = acc
        for d in range(1, count_sp):
            p_gather(d).start()

    def p_chunk(j):
        return jnp.concatenate([p_all[2 * j], p_all[2 * j + 1]], axis=0)

    def orthogonal():
        for d in range(1, count_sp):
            p_gather_in(d).wait_recv()
        p_total = jnp.concatenate([p_chunk(j) for j in range(CHUNKS)], axis=1)
        gram = exact_dot(p_total, p_total, ((1,), (1,)))
        row_at = lax.broadcasted_iota(jnp.int32, (rank, rank), 0)
        col_at = lax.broadcasted_iota(jnp.int32, (rank, rank), 1)
        work[:, :rank] = gram
        work[:, rank : 2 * rank] = jnp.where(row_at == col_at, 1.0, 0.0)
        shape = (rank, 2 * rank)
        line = lax.broadcasted_iota(jnp.int32, shape, 0)
        spot = lax.broadcasted_iota(jnp.int32, shape, 1)

        def eliminate(k, carry):
            state = work[:, : 2 * rank]
            pivot = work[pl.ds(k, 1), : 2 * rank]
            column = jnp.sum(jnp.where(spot == k, state, 0.0), axis=1, keepdims=True)
            diagonal = jnp.sum(jnp.where(spot[:1] == k, pivot, 0.0), axis=1, keepdims=True)
            inverse = 1.0 / jnp.sqrt(diagonal)
            pivot = pivot * inverse
            work[:, : 2 * rank] = jnp.where(
                line > k, state - (column * inverse) * pivot, jnp.where(line == k, pivot, state)
            )
            return carry

        lax.fori_loop(0, rank, eliminate, 0)
        lower_inverse = jnp.where(col_at <= row_at, work[:, rank : 2 * rank], 0.0)
        whole = exact_dot(lower_inverse, p_total, ((1,), (0,)))
        p0, p1, p2 = split(whole)
        p_side[...] = jnp.concatenate([p0, p1, p2, p0, p1, p0], axis=0)
        q_sum[...] = jnp.zeros_like(q_sum)

    def by_p(rows_of, k):
        m0, m1, m2 = split(rows_of)
        m_side = jnp.concatenate([m0, m0, m0, m1, m1, m2], axis=1)
        across = jnp.concatenate([p_side[i * rank : (i + 1) * rank, columns(k)] for i in range(6)], axis=1)
        return jnp.dot(m_side, across.T, preferred_element_type=jnp.float32)

    def add_q(k):
        q_sum[:, :rank] = q_sum[:, :rank] + by_p(total[k], k)

    last = CHUNKS - 1

    def last_terms():
        for step in (1, 3, 2):
            owner = lax.rem(x + step, RING)
            terms = by_p(part[last, owner].reshape(q_sum.shape[0], COLS), last)
            x_term[step - 1] = terms.T
            x_out(step).start()

    def last_own():
        count = part.shape[4]
        for side in range(2):
            for tap in range(TAPS):
                at = pl.ds(side * count * TAPS + tap, count, stride=TAPS)
                total[last, at, :] = total[last, at, :] + part[last, x, side, tap]
        add_q(last)

    def last_sum():
        for step in (1, 3, 2):
            x_out(step).wait_recv()
        got = x_got[0] + x_got[1] + x_got[2]
        filled = jnp.concatenate([got, jnp.zeros((128 - rank, got.shape[1]), jnp.float32)], axis=0).T
        count = part.shape[4]
        for side in range(2):
            for tap in range(TAPS):
                at = pl.ds(side * count * TAPS + tap, count, stride=TAPS)
                line = (side * TAPS + tap) * count
                q_sum[at, :] = q_sum[at, :] + filled[line : line + count]

    def multiply(first, count, after):
        depth = gbuf.shape[1]
        per_side = part.shape[4]

        def one(a, carry):
            at = pl.ds(pl.multiple_of(a * width, width), depth)
            stacked = taps[:, :, at].reshape(3 * RING * share, depth)
            chosen = gbuf[first] if count == 1 else jnp.concatenate([gbuf[first], gbuf[first + 1]], axis=1)
            product = jnp.dot(stacked, chosen, preferred_element_type=jnp.float32)
            for c in range(count):
                for b in range(3):
                    for owner in range(RING):
                        for side in range(2):
                            line = b * RING * share + (owner * 2 + side) * per_side
                            part[first + c, owner, side, a * 3 + b] = product[
                                line : line + per_side, c * COLS : (c + 1) * COLS
                            ]
            @pl.when((a == 0) & (after < CHUNKS))
            def _():
                start_forward(after)

            @pl.when((a == 0) & (after + 1 < CHUNKS))
            def _():
                start_direct(after + 1)

            return carry

        lax.fori_loop(0, 3, one, 0)
        for c in range(count):
            for side in range(2):
                put(far_code.at[first + c, side], part[first + c, x_far, side].reshape(half_rows, COLS))
                far(first + c, side).start()

    half_rows = TAPS * part.shape[4]

    def put(ref, block):
        signed, scale = encode(block)
        ref[:half_rows] = signed
        ref[half_rows:] = scale

    def pass_on(k):
        for side, owner in ((0, x_right), (1, x_left)):
            put(near_code.at[k, side, 1 - side], part[k, owner, 1 - side].reshape(half_rows, COLS))
            far(k, side).wait_recv()
            both = part[k, owner, side].reshape(half_rows, COLS) + decode(relay[k, side])
            put(near_code.at[k, side, side], both)
            near(k, side).start()

    def add_near(k, own):
        count = part.shape[4]
        for side in range(2):
            got = decode(piece[k, 0, side]) + decode(piece[k, 1, side])
            for tap in range(TAPS):
                at = pl.ds(side * count * TAPS + tap, count, stride=TAPS)
                term = got[tap * count : (tap + 1) * count]
                if own:
                    term = term + part[k, x, side, tap]
                total[k, at, :] = total[k, at, :] + term

    def complete(k, with_q):
        near(k, 0).wait_recv()
        near(k, 1).wait_recv()
        add_near(k, True)
        mem_out(k).start()
        pl.when(with_q)(lambda: add_q(k))

    def complete_last():
        near(last, 0).wait_recv()
        near(last, 1).wait_recv()
        add_near(last, False)
        mem_out(last).start()

    def over(first, count, body):
        def one(i, carry):
            body(first + i)
            return carry

        lax.fori_loop(0, count, one, 0)

    def step(j, carry):
        @pl.when(j < CHUNKS)
        def _():
            forward_in(j, 0).wait_recv()
            forward_in(j, 1).wait_recv()

        alone = (j == 0) | (j == CHUNKS - 1)
        even = lax.rem(j, 2) == 0
        pl.when(alone)(lambda: multiply(j, 1, j + 1))
        pl.when((j > 0) & (j < CHUNKS - 1) & even)(lambda: multiply(j - 1, 2, j + 1))

        @pl.when((j < CHUNKS - 1) & jnp.logical_not(even))
        def _():
            start_forward(j + 1)
            pl.when(j + 2 < CHUNKS)(lambda: start_direct(j + 2))


        pl.when((j == 1) | (j == CHUNKS))(lambda: pass_on(j - 1))
        pl.when((j > 1) & (j < CHUNKS) & jnp.logical_not(even))(lambda: over(j - 2, 2, pass_on))

        @pl.when(j == T_AT)
        def _():
            t_start()
            t_bands(0)
            t_bands(RING // 2)
            t_finish()

        pl.when(j == T_AT + 1)(t_pass_on)
        pl.when(j == last)(last_terms)

        for at, stage in zip(P_AT, (p_terms, p_sum_sp, p_sum_rep, orthogonal)):
            pl.when(j == at)(stage)
        ready = j >= P_AT[-1]

        pl.when(j == 2)(lambda: complete(0, ready))
        pl.when((j > 2) & (j <= CHUNKS) & even)(lambda: over(j - 3, 2, lambda k: complete(k, ready)))
        pl.when(j == P_AT[-1])(lambda: over(0, EARLY, add_q))

        return carry

    lax.fori_loop(0, CHUNKS + 1, step, 0)
    last_own()
    last_sum()

    lines = rank // count_rep
    q_lines = q_sum[...].T
    for i in range(count_rep):
        q_src[i] = q_lines[i * lines : (i + 1) * lines]
    for d in range(1, count_rep):
        q_scatter(d).start()
    acc = q_src[rep]
    for d in range(1, count_rep):
        q_scatter(d).wait_recv()
        acc = acc + q_got[d - 1]
    q_next[rep] = acc * (1.0 / count_rep)
    for d in range(1, count_rep):
        q_gather(d).start()
    complete_last()
    for d in range(1, count_rep):
        q_gather_in(d).wait_recv()

    def finish(j, carry):
        for side in range(2):
            direct(j, side).wait_send()
            forward(j, side).wait_send()
            far(j, side).wait_send()
            near(j, side).wait_send()
        mem_out(j).wait()
        return carry

    lax.fori_loop(0, CHUNKS, finish, 0)
    for side in range(2):
        frames_near(side).wait_send()
        frames_far(side).wait_send()
        frames_on(side).wait_send()
        t_far(side).wait_send()
        t_out(side).wait_send()
    for step_ in (1, 3, 2):
        q_out(step_).wait_send()
        x_out(step_).wait_send()
    for d in range(1, count_sp):
        p_scatter(d).wait_send()
        p_gather(d).wait_send()
    for d in range(1, count_rep):
        p_share(d).wait_send()
        q_scatter(d).wait_send()
        q_gather(d).wait_send()


def compressed_step(count_rep, frames, g, err, q_own):
    band, chans = g.shape
    width = band // 4
    rows = err.shape[0]
    rank = q_own.shape[0]
    count_sp = RING * RING
    share = chans // count_sp
    per_side = share // 2
    code_rows = TAPS * per_side + SCALE_ROWS
    dma = pltpu.SemaphoreType.DMA
    two = dma((CHUNKS, 2))
    f32, bf16 = jnp.float32, jnp.bfloat16
    any_spec, vmem_spec = pl.BlockSpec(memory_space=pl.ANY), pl.BlockSpec(memory_space=pltpu.VMEM)
    p_block = (rank // 2, COLS)
    q_block = (rank // count_rep, rows)
    return pl.pallas_call(
        functools.partial(step_kernel, count_rep),
        out_shape=(
            jax.ShapeDtypeStruct((rows, chans), f32),
            jax.ShapeDtypeStruct((count_rep, *q_block), f32),
            jax.ShapeDtypeStruct((6 * rank, chans), bf16),
        ),
        in_specs=[any_spec, any_spec, any_spec, vmem_spec],
        out_specs=(any_spec, vmem_spec, vmem_spec),
        scratch_shapes=[
            pltpu.VMEM((chans // COLS, band, COLS), bf16),
            pltpu.VMEM((2, RING // 2, share, band), bf16),
            pltpu.VMEM((2, rank // 2, band), f32),
            pltpu.VMEM((rows, 128), f32),
            pltpu.VMEM((TAPS, share, 128), bf16),
            pltpu.VMEM((RING, RING, share, band), bf16),
            pltpu.VMEM((RING, RING, share, band), bf16),
            pltpu.VMEM((2, RING, share, width), bf16),
            pltpu.VMEM((3, RING * share, RING * band + 2 * width), bf16),
            pltpu.VMEM((CHUNKS, RING * band, COLS), bf16),
            pltpu.VMEM((CHUNKS, RING, 2, TAPS, per_side, COLS), f32),
            pltpu.VMEM((CHUNKS, 2, code_rows, COLS), bf16),
            pltpu.VMEM((CHUNKS, 2, 2, code_rows, COLS), bf16),
            pltpu.VMEM((CHUNKS, 2, code_rows, COLS), bf16),
            pltpu.VMEM((CHUNKS, 2, 2, code_rows, COLS), bf16),
            pltpu.VMEM((CHUNKS, rows, COLS), f32),
            pltpu.VMEM((TAPS, RING, share, 128), bf16),
            pltpu.VMEM((3, 128, 3 * RING * share), bf16),
            pltpu.VMEM((RING, rank, band), f32),
            pltpu.VMEM((2, rank, band), f32),
            pltpu.VMEM((count_sp, *p_block), f32),
            pltpu.VMEM((count_sp - 1, *p_block), f32),
            pltpu.VMEM(p_block, f32),
            pltpu.VMEM((count_rep, *p_block), f32),
            pltpu.VMEM((count_sp, *p_block), f32),
            pltpu.VMEM((rank, 128), f32),
            pltpu.VMEM((count_rep, *q_block), f32),
            pltpu.VMEM((count_rep - 1, *q_block), f32),
            pltpu.VMEM((rows, 128), f32),
            pltpu.VMEM((RING - 1, rank, rows), f32),
            pltpu.VMEM((RING - 1, rank, rows), f32),
            dma((chans // COLS,)), dma((6,)), dma((6,)), dma, dma((2,)), dma((2,)), dma((CHUNKS,)), dma((CHUNKS,)),
            two, two, two, two, two, two, two, two, dma((CHUNKS,)),
            dma((3,)), dma((3,)), dma, dma((4,)), dma((4,)),
            dma((count_sp - 1,)), dma((count_sp - 1,)), dma((count_rep - 1,)), dma((count_rep - 1,)),
            dma((count_sp - 1,)), dma((count_sp - 1,)), dma((count_rep - 1,)), dma((count_rep - 1,)),
            dma((count_rep - 1,)), dma((count_rep - 1,)), dma((3,)), dma((3,)),
        ],
        compiler_params=pltpu.CompilerParams(
            collective_id=0, has_side_effects=True, vmem_limit_bytes=58 * 1024 * 1024
        ),
        cost_estimate=pl.CostEstimate(flops=2 * rows * 16 * chans * band, bytes_accessed=10**7, transcendentals=0),
        name="compressed_step",
    )(frames, g, err, q_own)


def feedback_kernel(memory, q_parts, p_side, error_next, q_next, q_side):
    count, lines, rows = q_parts.shape
    block = memory.shape[0]

    @pl.when(pl.program_id(0) == 0)
    def _():
        for i in range(count):
            q_next[i * lines : (i + 1) * lines] = q_parts[i]
        q0, q1, q2 = split(q_next[...])
        q_side[...] = jnp.concatenate([q0, q0, q0, q1, q1, q2], axis=0).T

    at = pl.ds(pl.multiple_of(pl.program_id(0) * block, block), block)
    error_next[...] = memory[...] - jnp.dot(q_side[at, :], p_side[...], preferred_element_type=jnp.float32)


def feedback(memory, q_parts, p_side):
    rows, chans = memory.shape
    count, lines, _ = q_parts.shape
    rank = count * lines
    block = (rows // 4, chans)
    return pl.pallas_call(
        feedback_kernel,
        grid=(rows // block[0],),
        out_shape=(jax.ShapeDtypeStruct(memory.shape, jnp.float32), jax.ShapeDtypeStruct((rank, rows), jnp.float32)),
        in_specs=[
            pl.BlockSpec(block, lambda i: (i, 0)),
            pl.BlockSpec(q_parts.shape, lambda i: (0, 0, 0)),
            pl.BlockSpec(p_side.shape, lambda i: (0, 0)),
        ],
        out_specs=(pl.BlockSpec(block, lambda i: (i, 0)), pl.BlockSpec((rank, rows), lambda i: (0, 0))),
        scratch_shapes=[pltpu.VMEM((rows, 6 * rank), jnp.bfloat16)],
        compiler_params=pltpu.CompilerParams(vmem_limit_bytes=60 * 1024 * 1024),
        name="feedback",
    )(memory, q_parts, p_side)


def per_device(count_rep, frames, out_grad, error_prev, q_prev):
    band_rows, width, chans = frames.shape[1:]
    band = band_rows * width
    memory, q_parts, p_side = compressed_step(
        count_rep,
        frames[0].reshape(band, chans),
        out_grad[0].reshape(band, chans),
        error_prev[0],
        q_prev,
    )
    error_next, q_next = feedback(memory, q_parts, p_side)
    return (error_next[None], q_next)


def solution(mesh):
    placed = (
        P("rep", "sp", None, None),
        P("rep", "sp", None, None),
        P("rep", "sp", None),
        P(None, "sp"),
    )
    return jax.shard_map(
        functools.partial(per_device, mesh.shape["rep"]),
        mesh=mesh,
        in_specs=placed,
        out_specs=(P("rep", "sp", None), P(None, "sp")),
        check_vma=False,
    )
```
